32 devices in a mesh: wide: 8 (over z, x), narrow: 4 (over y, core).
Axes of the slice: x: 2, y: 2, z: 4, core: 2. Of those that a mesh axis runs over, the one named last changes fastest.
Arguments:
- cells_in: bfloat16 [2, 8, 1024, 1120], P(None, 'wide', 'narrow'), may hold values from -6 to 6
- lengths: int32 [2, 8], P(None, 'wide'), may hold values from 128 to 1024, as said below
- w_qkv: bfloat16 [60, 62720], P('narrow', 'wide'), may hold values from -0.25 to 0.25
- w_out: bfloat16 [20, 62720], P('narrow', 'wide'), may hold values from -0.75 to 0.75
- w_up: bfloat16 [560, 8960], P('narrow', 'wide'), may hold values from -0.1875 to 0.1875
- w_down: bfloat16 [560, 8960], P('narrow', 'wide'), may hold values from -0.09375 to 0.09375
- ln1_gain: float32 [1120], replicated, may hold values from 0.1 to 1.9
- ln1_shift: float32 [1120], replicated, may hold values from -1.5 to 1.5
- bias_qv: float32 [2240], replicated, may hold values from -1.5 to 1.5
- bias_out: float32 [1120], replicated, may hold values from -1.5 to 1.5
- ln2_gain: float32 [1120], replicated, may hold values from 0.1 to 1.9
- ln2_shift: float32 [1120], replicated, may hold values from -1.5 to 1.5
- bias_up: float32 [4480], replicated, may hold values from -2.5 to 2.5
- bias_down: float32 [1120], replicated, may hold values from -1.5 to 1.5
- cotangent: bfloat16 [2, 8, 1024, 1120], P(None, 'wide', 'narrow'), may hold values from -8 to 8
Outputs:
- cells_out: bfloat16 [2, 8, 1024, 1120], P(None, 'wide', 'narrow')
- grad_in: bfloat16 [2, 8, 1024, 1120], P(None, 'wide', 'narrow')
- grad_qkv: float32 [60, 62720], P('narrow', 'wide')
- grad_out: float32 [20, 62720], P('narrow', 'wide')
- grad_up: float32 [560, 8960], P('narrow', 'wide')
- grad_down: float32 [560, 8960], P('narrow', 'wide')
- grad_ln1_gain: float32 [1120], replicated
- grad_ln1_shift: float32 [1120], replicated
- grad_bias_qv: float32 [2240], replicated
- grad_bias_out: float32 [1120], replicated
- grad_ln2_gain: float32 [1120], replicated
- grad_ln2_shift: float32 [1120], replicated
- grad_bias_up: float32 [4480], replicated
- grad_bias_down: float32 [1120], replicated
The draws below stay inside these ranges and needn't reach their ends.
Inputs may be any that keep to these rules, and one draw needn't show every extreme that they name: For every cell column c, one of the 2 micro-batches has lengths[b, c] = 1024.
All inputs are finite; a program needn't handle non-finite values.
Results may differ from the reference program's by a relative error of at most 0.013.
Values may be sent and summed in bfloat16 or wider, within the bound.
A program may use at most 320 MiB of HBM per device.

```python
import jax
import jax.numpy as jnp
from jax import lax

D = 1120
HEADS = 20
HEAD_DIM = 56
FF = 4480
LEN = 1024
MB = 2
CELLS = 8


def draw_lengths(key, part):
    base_lengths = jax.random.randint(jax.random.fold_in(key, 11), (MB, CELLS), LEN // 8, LEN + 1)
    full_batch = jax.random.randint(jax.random.fold_in(key, 12), (CELLS,), 0, MB)
    batch_rows = jnp.arange(MB, dtype=jnp.int32)[:, None]
    return jnp.where(batch_rows == full_batch[None, :], LEN, base_lengths).astype(jnp.int32)


def draw_cotangent(key, part):
    cell_place = jnp.arange(CELLS, dtype=jnp.float32)[None, :, None, None] / (CELLS - 1)
    token_place = jnp.arange(LEN, dtype=jnp.float32)[None, None, :, None] / (LEN - 1)
    row_scale = 0.6 * 3.0 ** (0.5 * cell_place + 0.5 * token_place)
    values = jax.random.normal(jax.random.fold_in(key, 23), (MB, CELLS, LEN, D), jnp.float32)
    values = jnp.clip(values, -4.0, 4.0)
    return (values * row_scale).astype(jnp.bfloat16)


def block_levels(rng, shape, shards, low, largest):
    def one(axis_at, blocks):
        heights = jax.random.uniform(jax.random.fold_in(jax.random.fold_in(rng, 6), axis_at), (blocks,), jnp.float32, low / len(shards), largest / len(shards))
        return jnp.repeat(jnp.exp(heights), shape[axis_at] // blocks).reshape((-1,) + (1,) * (len(shape) - axis_at - 1))

    loudness = one(*shards[0])
    for cut in shards[1:]:
        loudness = loudness * one(*cut)
    return loudness


def scatter_about(own_key, dims, scale, limit, pieces=(), kind=jnp.bfloat16):
    drawn = scale * jax.random.normal(own_key, dims, jnp.float32)
    if pieces:
        drawn = drawn * block_levels(own_key, dims, pieces, -0.22, 0.18)
    return jnp.clip(drawn, -limit, limit).astype(kind)


def setup_inputs(seed: int = 0) -> dict:
    seeds = jax.random.split(jax.random.key(seed), 16)
    return {
        "cells_in": scatter_about(seeds[0], (MB, CELLS, LEN, D), 1.0, 6.0, ((1, 8), (2, 4))),
        "lengths": draw_lengths(jax.random.fold_in(seeds[15], 71), 0),
        "w_qkv": scatter_about(seeds[2], (HEADS * 3, HEAD_DIM * D), (D // 2) ** -0.5, 0.25, ((0, 4), (1, 8))),
        "w_out": scatter_about(seeds[3], (HEADS, HEAD_DIM * D), (D // 16) ** -0.5, 0.75, ((0, 4), (1, 8))),
        "w_up": scatter_about(seeds[4], (FF // 8, 8 * D), D ** -0.5, 0.1875, ((0, 4), (1, 8))),
        "w_down": scatter_about(seeds[5], (FF // 8, 8 * D), FF ** -0.5, 0.09375, ((0, 4), (1, 8))),
        "ln1_gain": jnp.clip(1.0 + 0.18 * jax.random.normal(seeds[6], (D,), jnp.float32), 0.1, 1.9),
        "ln1_shift": scatter_about(seeds[7], (D,), 0.3, 1.5, (), jnp.float32),
        "bias_qv": scatter_about(seeds[8], (2 * D,), 0.3, 1.5, (), jnp.float32),
        "bias_out": scatter_about(seeds[9], (D,), 0.3, 1.5, (), jnp.float32),
        "ln2_gain": jnp.clip(1.0 + 0.18 * jax.random.normal(seeds[10], (D,), jnp.float32), 0.1, 1.9),
        "ln2_shift": scatter_about(seeds[11], (D,), 0.3, 1.5, (), jnp.float32),
        "bias_up": scatter_about(seeds[12], (FF,), 0.5, 2.5, (), jnp.float32),
        "bias_down": scatter_about(seeds[13], (D,), 0.3, 1.5, (), jnp.float32),
        "cotangent": draw_cotangent(jax.random.fold_in(seeds[15], 71), 0),
    }


@jax.custom_vjp
def low(v):
    return lax.optimization_barrier(v.astype(jnp.bfloat16)).astype(jnp.float32)

@jax.custom_vjp
def low_back(v):
    return v

def low_keep(v):
    return (low(v), None)

def low_pass(kept, grad):
    return (grad,)

def back_keep(v):
    return (v, None)

def back_low(kept, grad):
    return (low(grad),)
low.defvjp(low_keep, low_pass)
low_back.defvjp(back_keep, back_low)
norm_eps = 1e-05

def layer_norm(values, scale_vec, shift_vec):
    center = values - lax.optimization_barrier(jnp.mean(values, axis=-1, keepdims=True))
    spread = lax.optimization_barrier(jnp.mean(center * center, axis=-1, keepdims=True))
    return center * lax.rsqrt(spread + norm_eps) * scale_vec + shift_vec

def cell_forward(params, cell_rows, cell_len):
    w_qkv, w_out, w_up, w_down, ln1_gain, ln1_shift, bias_qv, bias_out, ln2_gain, ln2_shift, bias_up, bias_down = params
    highest = lax.Precision.HIGHEST
    qkv_mat = jnp.transpose(w_qkv.reshape(HEADS, 3, HEAD_DIM, D), (3, 1, 0, 2)).reshape(D, 3 * D)
    out_mat = w_out.reshape(D, D)
    up_mat = jnp.transpose(w_up.reshape(FF, D))
    down_mat = w_down.reshape(FF, D)
    normed = low(layer_norm(cell_rows, ln1_gain, ln1_shift))
    qkv_bias = jnp.concatenate([bias_qv[:D], jnp.zeros((D,), jnp.float32), bias_qv[D:]])
    qkv = low_back(low(jnp.dot(normed, qkv_mat, precision=highest) + qkv_bias))
    queries = qkv[:, :D].reshape(LEN, HEADS, HEAD_DIM)
    key_rows = qkv[:, D:2 * D].reshape(LEN, HEADS, HEAD_DIM)
    value_rows = qkv[:, 2 * D:].reshape(LEN, HEADS, HEAD_DIM)
    scores = jnp.einsum('qhe,khe->hqk', queries, key_rows, precision=highest) * HEAD_DIM ** (-0.5)
    scores = low_back(scores)
    positions = jnp.arange(LEN, dtype=jnp.int32)
    allowed = (positions[None, :] <= positions[:, None]) & (positions[None, :] < cell_len)
    scores = jnp.where(allowed[None], scores, -1e+30)
    probs = low(jax.nn.softmax(scores, axis=-1))
    mixed = jnp.einsum('hqk,khe->qhe', probs, value_rows, precision=highest).reshape(LEN, D)
    mixed = low_back(low(mixed))
    attended = low_back(jnp.dot(mixed, out_mat, precision=highest) + bias_out)
    middle = cell_rows + attended
    normed2 = low(layer_norm(middle, ln2_gain, ln2_shift))
    upper = low_back(jnp.dot(normed2, up_mat, precision=highest) + bias_up)
    hidden = low(jax.nn.gelu(upper, approximate=True))
    return middle + jnp.dot(hidden, down_mat, precision=highest) + bias_down

def reference(cells_in, lengths, w_qkv, w_out, w_up, w_down, ln1_gain, ln1_shift, bias_qv, bias_out, ln2_gain, ln2_shift, bias_up, bias_down, cotangent):
    params = (w_qkv.astype(jnp.float32), w_out.astype(jnp.float32), w_up.astype(jnp.float32), w_down.astype(jnp.float32), ln1_gain.astype(jnp.float32), ln1_shift.astype(jnp.float32), bias_qv.astype(jnp.float32), bias_out.astype(jnp.float32), ln2_gain.astype(jnp.float32), ln2_shift.astype(jnp.float32), bias_up.astype(jnp.float32), bias_down.astype(jnp.float32))
    flat_cells = cells_in.astype(jnp.float32).reshape(MB * CELLS, LEN, D)
    flat_lengths = lengths.reshape(MB * CELLS).astype(jnp.int32)

    def forward(params_in, cells_all):

        def one_cell(item):
            return cell_forward(params_in, item[0], item[1])
        return lax.map(jax.checkpoint(one_cell), (cells_all, flat_lengths))
    outputs, pullback = jax.vjp(forward, params, flat_cells)
    grad_params, grad_cells = pullback(cotangent.astype(jnp.float32).reshape(MB * CELLS, LEN, D))
    shape_all = (MB, CELLS, LEN, D)
    return (outputs.reshape(shape_all).astype(jnp.bfloat16), grad_cells.reshape(shape_all).astype(jnp.bfloat16), grad_params[0], grad_params[1], grad_params[2], grad_params[3], grad_params[4], grad_params[5], grad_params[6], grad_params[7], grad_params[8], grad_params[9], grad_params[10], grad_params[11])
```

```python
import functools

import jax
import jax.numpy as jnp
from jax import lax
from jax.experimental import pallas as pl
from jax.experimental.pallas import tpu as pltpu
from jax.sharding import PartitionSpec as P

HEAD_DIM = 56
PAD_DIM = 64
OUTER = 8
NORM_EPS = 1e-05
MESH = pl.DeviceIdType.MESH
BF16 = jnp.bfloat16
F32 = jnp.float32
PIECE = 48
SCALE = HEAD_DIM ** (-0.5)


def place(inner):
    w = lax.axis_index("wide")
    n = lax.axis_index("narrow")
    outer = w // inner
    return outer // 2, outer % 2, n // 2, n % 2, w % inner


def device(inner, z, x, y, c, wi):
    return ((2 * z + x) * inner + wi, 2 * y + c)


def slab(y, x, z):
    return y * 8 + x * 4 + z


def remote(src, dst, send, recv, dev):
    return pltpu.make_async_remote_copy(
        src_ref=src, dst_ref=dst, send_sem=send, recv_sem=recv, device_id=dev, device_id_type=MESH
    )


def greet(devices):
    barrier = pltpu.get_barrier_semaphore()
    for dev in devices:
        pl.semaphore_signal(barrier, inc=1, device_id=dev, device_id_type=MESH)
    pl.semaphore_wait(barrier, len(devices))


def neighbours(inner):
    z, x, y, c, wi = place(inner)
    along = [device(inner, (z + d) % 4, x, y, c, wi) for d in (1, 2, 3)]
    return (
        along,
        device(inner, z, 1 - x, y, c, wi),
        device(inner, z, x, 1 - y, c, wi),
        device(inner, z, x, y, 1 - c, wi),
    )


def gather_kernel(inner, blocks, pieces, *refs):
    w_refs, x_ref, g_ref = refs[:blocks], refs[blocks], refs[blocks + 1]
    outs = refs[blocks + 2 : 2 * blocks + 2]
    xo, go = refs[2 * blocks + 2], refs[2 * blocks + 3]
    zs, zr, xs, xr, ys, yr, fxs, fxr, fys, fyr, ss, sr, ls = refs[2 * blocks + 4 :]
    z, x, y, c, wi = place(inner)
    along, xdev, ydev, cdev = neighbours(inner)
    greet([*along, xdev, ydev, cdev])

    total = blocks * pieces

    def view(k, s):
        b, p = k // pieces, k % pieces
        return outs[b].at[s, pl.ds(p * PIECE, PIECE)]

    def own(k):
        b, p = k // pieces, k % pieces
        return w_refs[b].at[pl.ds(p * PIECE, PIECE)]

    locals_ = [
        pltpu.make_async_copy(w_refs[b], outs[b].at[slab(y, x, z)], ls.at[b]) for b in range(blocks)
    ]

    def zcopy(k, d):
        return remote(own(k), view(k, slab(y, x, z)), zs.at[k, d - 1], zr.at[k, d - 1], along[d - 1])

    def zwait(k, d):
        v = view(k, slab(y, x, (z + 4 - d) % 4))
        return remote(v, v, zs.at[k, d - 1], zr.at[k, d - 1], along[d - 1])

    def xcopy(k, d):
        s = slab(y, x, (z + 4 - d) % 4)
        src = own(k) if d == 0 else view(k, s)
        return remote(src, view(k, s), xs.at[k, d], xr.at[k, d], xdev)

    def xwait(k, d):
        v = view(k, slab(y, 1 - x, (z + 4 - d) % 4))
        return remote(v, v, xs.at[k, d], xr.at[k, d], xdev)

    def ycopy(k, d):
        s = slab(y, x, (z + 4 - d) % 4)
        src = own(k) if d == 0 else view(k, s)
        return remote(src, view(k, s), ys.at[k, d], yr.at[k, d], ydev)

    def ywait(k, d):
        v = view(k, slab(1 - y, x, (z + 4 - d) % 4))
        return remote(v, v, ys.at[k, d], yr.at[k, d], ydev)

    def fycopy(k, d):
        v = view(k, slab(y, 1 - x, (z + 4 - d) % 4))
        return remote(v, v, fys.at[k, d], fyr.at[k, d], ydev)

    def fywait(k, d):
        v = view(k, slab(1 - y, 1 - x, (z + 4 - d) % 4))
        return remote(v, v, fys.at[k, d], fyr.at[k, d], ydev)

    def fxcopy(k, d):
        v = view(k, slab(1 - y, x, (z + 4 - d) % 4))
        return remote(v, v, fxs.at[k, d - 2], fxr.at[k, d - 2], xdev)

    def fxwait(k, d):
        v = view(k, slab(1 - y, 1 - x, (z + 4 - d) % 4))
        return remote(v, v, fxs.at[k, d - 2], fxr.at[k, d - 2], xdev)

    def a1(k):
        for d in (1, 2, 3):
            zcopy(k, d).start()
        xcopy(k, 0).start()
        ycopy(k, 0).start()

    def a2(k):
        for d in (1, 2, 3):
            zwait(k, d).wait_recv()
            xcopy(k, d).start()
            ycopy(k, d).start()

    def a3(k):
        for d in (0, 1):
            xwait(k, d).wait_recv()
            fycopy(k, d).start()
            ywait(k, d + 2).wait_recv()
            fxcopy(k, d + 2).start()

    def a4(k):
        for d in (0, 1):
            xwait(k, d + 2).wait_recv()
            ywait(k, d).wait_recv()
            fywait(k, d).wait_recv()
            fxwait(k, d + 2).wait_recv()

    n_own = 2 * y + c
    n_sib = 2 * y + 1 - c
    n_y = 2 * (1 - y) + c
    n_ys = 2 * (1 - y) + 1 - c

    def swap(i, src, dst):
        mine = pltpu.make_async_copy(src.at[y], dst.at[n_own], ls.at[blocks + i])
        side = remote(src.at[y], dst.at[n_own], ss.at[i, 0], sr.at[i, 0], cdev)
        over = remote(src.at[1 - y], dst.at[n_own], ss.at[i, 1], sr.at[i, 1], ydev)
        over_in = remote(dst.at[n_y], dst.at[n_y], ss.at[i, 1], sr.at[i, 1], ydev)
        fwd = remote(dst.at[n_y], dst.at[n_y], ss.at[i, 2], sr.at[i, 2], cdev)
        return mine, side, over, over_in, fwd

    def swap_start(parts):
        parts[0].start()
        parts[1].start()
        parts[2].start()

    def swap_mid(parts):
        parts[3].wait_recv()
        parts[4].start()

    def swap_end(i, dst, parts):
        parts[0].wait()
        side_in = remote(dst.at[n_sib], dst.at[n_sib], ss.at[i, 0], sr.at[i, 0], cdev)
        fwd_in = remote(dst.at[n_ys], dst.at[n_ys], ss.at[i, 2], sr.at[i, 2], cdev)
        side_in.wait_recv()
        fwd_in.wait_recv()
        parts[1].wait_send()
        parts[2].wait_send()
        parts[4].wait_send()

    xp = swap(0, x_ref, xo)
    gp = swap(1, g_ref, go)
    swap_start(xp)
    a1(0)
    for b in range(blocks):
        locals_[b].start()
    for k in range(total + 2):
        if k + 1 < total:
            a1(k + 1)
        if k < total:
            a2(k)
        if 0 <= k - 1 < total:
            a3(k - 1)
        if 0 <= k - 2 < total:
            a4(k - 2)
        if k == 0:
            swap_mid(xp)
        if k == 3:
            swap_start(gp)
        if k == 6:
            swap_mid(gp)
    swap_end(0, xo, xp)
    swap_end(1, go, gp)
    for b in range(blocks):
        locals_[b].wait()
    for k in range(total):
        for d in (1, 2, 3):
            zcopy(k, d).wait_send()
        for d in range(4):
            xcopy(k, d).wait_send()
            ycopy(k, d).wait_send()
        for d in (0, 1):
            fycopy(k, d).wait_send()
            fxcopy(k, d + 2).wait_send()


def gather_all(inner, weights, cells, cot):
    blocks = len(weights)
    rows, width = weights[0].shape
    pieces = rows // PIECE
    total = blocks * pieces
    dma = pltpu.SemaphoreType.DMA
    any_ = pl.BlockSpec(memory_space=pl.ANY)
    local_rows = cells.shape[1]
    return pl.pallas_call(
        functools.partial(gather_kernel, inner, blocks, pieces),
        out_shape=[jax.ShapeDtypeStruct((16, rows, width), BF16)] * blocks
        + [jax.ShapeDtypeStruct((4, local_rows, width), BF16)] * 2,
        in_specs=[any_] * (blocks + 2),
        out_specs=[any_] * (blocks + 2),
        scratch_shapes=[
            dma((total, 3)), dma((total, 3)),
            dma((total, 4)), dma((total, 4)),
            dma((total, 4)), dma((total, 4)),
            dma((total, 2)), dma((total, 2)),
            dma((total, 2)), dma((total, 2)),
            dma((2, 3)), dma((2, 3)),
            dma((blocks + 2,)),
        ],
        compiler_params=pltpu.CompilerParams(collective_id=0, has_side_effects=True),
        name="gather_weights",
    )(*weights, cells, cot)


def reduce_kernel(inner, blocks, pieces, *refs):
    parts, small = refs[:blocks], refs[blocks]
    out, small_out = refs[blocks + 1], refs[blocks + 2]
    r1, rx, ry, rz, sx, sy, st, own32 = refs[blocks + 3 : blocks + 11]
    acc, got = refs[blocks + 11 : blocks + 13]
    s1, q1, s2, q2, s3, q3, sz, qz, sa, qa = refs[blocks + 13 :]
    z, x, y, c, wi = place(inner)
    along, xdev, ydev, cdev = neighbours(inner)
    greet([*along, xdev, ydev, cdev])
    total = blocks * pieces

    def rows(k):
        return parts[k // pieces], pl.ds((k % pieces) * PIECE, PIECE)

    def cut(k, s, count):
        ref, r = rows(k)
        return ref.at[pl.ds(s, count), r]

    def load(k, s, count):
        ref, r = rows(k)
        return ref[pl.ds(s, count), r].astype(F32)

    def first(k):
        return (
            remote(cut(k, slab(1 - y, 1 - x, 0), 2), r1.at[k, pl.ds(0, 2)], s1.at[k, 0], q1.at[k, 0], ydev),
            remote(cut(k, slab(1 - y, 1 - x, 2), 2), r1.at[k, pl.ds(2, 2)], s1.at[k, 1], q1.at[k, 1], xdev),
        )

    def second(k):
        return (
            remote(cut(k, slab(y, 1 - x, 2), 2), rx.at[k, pl.ds(2, 2)], s2.at[k, 0], q2.at[k, 0], xdev),
            remote(cut(k, slab(1 - y, x, 0), 2), ry.at[k, pl.ds(0, 2)], s2.at[k, 1], q2.at[k, 1], ydev),
        )

    def third(k):
        return (
            remote(sx.at[k], rx.at[k, pl.ds(0, 2)], s3.at[k, 0], q3.at[k, 0], xdev),
            remote(sy.at[k], ry.at[k, pl.ds(2, 2)], s3.at[k, 1], q3.at[k, 1], ydev),
        )

    def last(k, d):
        return remote(st.at[k, d - 1], rz.at[k, d - 1], sz.at[k, d - 1], qz.at[k, d - 1], along[d - 1])

    def stage1(k):
        for cp in (*first(k), *second(k)):
            cp.start()

    def stage2(k):
        f = first(k)
        t = third(k)
        f[0].wait_recv()
        sx[k] = (load(k, slab(y, 1 - x, 0), 2) + r1[k, 0:2].astype(F32)).astype(BF16)
        t[0].start()
        f[1].wait_recv()
        sy[k] = (load(k, slab(1 - y, x, 2), 2) + r1[k, 2:4].astype(F32)).astype(BF16)
        t[1].start()

    def stage3(k):
        for cp in (*second(k), *third(k)):
            cp.wait_recv()
        for d in (1, 2, 3):
            j = (z + d) % 4
            st[k, d - 1] = (
                load(k, slab(y, x, j), 1)[0] + rx[k, j].astype(F32) + ry[k, j].astype(F32)
            ).astype(BF16)
            last(k, d).start()
        own32[k] = load(k, slab(y, x, z), 1)[0] + rx[k, z].astype(F32) + ry[k, z].astype(F32)

    def stage4(k):
        for d in (1, 2, 3):
            last(k, d).wait_recv()
        out[k] = (
            own32[k] + rz[k, 0].astype(F32) + rz[k, 1].astype(F32) + rz[k, 2].astype(F32)
        )

    peers = [
        cdev, xdev, ydev,
        device(inner, z + 1 - 2 * (z % 2), x, y, c, wi),
        device(inner, (z + 2) % 4, x, y, c, wi),
    ]

    def small_copy(i):
        return remote(acc.at[i], got.at[i], sa.at[i], qa.at[i], peers[i])

    acc[0] = small[...]
    for k in range(total + 2):
        if k < total:
            stage1(k)
        if k < 5:
            small_copy(k).start()
        if k < total:
            stage2(k)
        if 0 <= k - 1 < total:
            stage3(k - 1)
        if 0 <= k - 2 < total:
            stage4(k - 2)
        if k < 5:
            small_copy(k).wait()
            acc[k + 1] = acc[k] + got[k]
    small_out[...] = acc[5]
    for k in range(total):
        for cp in (*first(k), *second(k), *third(k), last(k, 1), last(k, 2), last(k, 3)):
            cp.wait_send()


def reduce_all(inner, parts, small):
    blocks = len(parts)
    rows, width = parts[0].shape[1:]
    pieces = rows // PIECE
    total = blocks * pieces
    dma = pltpu.SemaphoreType.DMA
    vm = pl.BlockSpec(memory_space=pltpu.VMEM)
    out, small_sum = pl.pallas_call(
        functools.partial(reduce_kernel, inner, blocks, pieces),
        out_shape=[
            jax.ShapeDtypeStruct((total, PIECE, width), F32),
            jax.ShapeDtypeStruct(small.shape, F32),
        ],
        in_specs=[vm] * (blocks + 1),
        out_specs=[vm, vm],
        scratch_shapes=[
            pltpu.VMEM((total, 4, PIECE, width), BF16),
            pltpu.VMEM((total, 4, PIECE, width), BF16),
            pltpu.VMEM((total, 4, PIECE, width), BF16),
            pltpu.VMEM((total, 3, PIECE, width), BF16),
            pltpu.VMEM((total, 2, PIECE, width), BF16),
            pltpu.VMEM((total, 2, PIECE, width), BF16),
            pltpu.VMEM((total, 3, PIECE, width), BF16),
            pltpu.VMEM((total, PIECE, width), F32),
            pltpu.VMEM((6, *small.shape), F32),
            pltpu.VMEM((5, *small.shape), F32),
            dma((total, 2)), dma((total, 2)),
            dma((total, 2)), dma((total, 2)),
            dma((total, 2)), dma((total, 2)),
            dma((total, 3)), dma((total, 3)),
            dma((5,)), dma((5,)),
        ],
        compiler_params=pltpu.CompilerParams(
            collective_id=1, has_side_effects=True, vmem_limit_bytes=62 * 2**20
        ),
        name="reduce_grads",
    )(*parts, small)
    return out.reshape(blocks, rows, width), small_sum


def dot(a, b, dims):
    return lax.dot_general(a, b, (dims, ((), ())), preferred_element_type=F32)


def dot_nn(a, b):
    return dot(a, b, ((1,), (0,)))


def dot_nt(a, b):
    return dot(a, b, ((1,), (1,)))


def dot_tn(a, b):
    return dot(a, b, ((0,), (0,)))


def norm_parts(v):
    center = v - jnp.mean(v, axis=-1, keepdims=True)
    rstd = lax.rsqrt(jnp.mean(center * center, axis=-1, keepdims=True) + NORM_EPS)
    return center * rstd, rstd


def norm_back(e, gain, xhat, rstd):
    eg = e * gain
    return rstd * (
        eg - jnp.mean(eg, axis=-1, keepdims=True) - xhat * jnp.mean(eg * xhat, axis=-1, keepdims=True)
    )


def attend(q, k, v, cell_len):
    heads, total = q.shape[0], q.shape[1]
    block = min(512, total)
    outs, sums = [], []
    for start in range(0, total, block):
        end = start + block
        allowed = visible(start, block, end, cell_len)
        s = jnp.einsum("hqe,hke->hqk", q[:, start:end], k[:, :end], preferred_element_type=F32) * SCALE
        s = jnp.where(allowed[None], s, -1e30)
        m = jnp.max(s, axis=-1, keepdims=True)
        e = jnp.exp(s - m)
        t = jnp.sum(e, axis=-1, keepdims=True)
        p = (e / t).astype(BF16)
        outs.append(jnp.einsum("hqk,hke->hqe", p, v[:, :end], preferred_element_type=F32).astype(BF16))
        sums.append(m + jnp.log(t))
    return jnp.concatenate(outs, axis=1), sums


def visible(start, rows, count, cell_len):
    qp = start + jnp.arange(rows, dtype=jnp.int32)[:, None]
    kp = jnp.arange(count, dtype=jnp.int32)[None, :]
    return (kp <= qp) & (kp < cell_len)


def attend_back(q, k, v, g, cell_len, sums):
    total = q.shape[1]
    block = min(512, total)
    gq = []
    gk = jnp.zeros(k.shape, F32)
    gv = jnp.zeros(v.shape, F32)
    for i, start in enumerate(range(0, total, block)):
        end = start + block
        allowed = visible(start, block, end, cell_len)
        qb, gb = q[:, start:end], g[:, start:end]
        s = jnp.einsum("hqe,hke->hqk", qb, k[:, :end], preferred_element_type=F32) * SCALE
        s = jnp.where(allowed[None], s, -1e30)
        p = jnp.exp(s - sums[i])
        pl_ = p.astype(BF16)
        gv = gv.at[:, :end].add(jnp.einsum("hqk,hqe->hke", pl_, gb, preferred_element_type=F32))
        gp = jnp.einsum("hqe,hke->hqk", gb, v[:, :end], preferred_element_type=F32)
        inner = jnp.sum(p * gp, axis=-1, keepdims=True)
        gs = (p * (gp - inner)).astype(BF16)
        gq.append(jnp.einsum("hqk,hke->hqe", gs, k[:, :end], preferred_element_type=F32) * SCALE)
        gk = gk.at[:, :end].add(jnp.einsum("hqk,hqe->hke", gs, qb, preferred_element_type=F32) * SCALE)
    return jnp.concatenate(gq, axis=1), gk, gv


def order_matrix():
    heads = 5
    dst = jnp.arange(4 * heads * PAD_DIM, dtype=jnp.int32)[:, None]
    src = jnp.arange(OUTER * 144, dtype=jnp.int32)[None, :]
    xz, i = src // 144, src % 144
    w = 2 * (xz % 4) + xz // 4
    e = i % 7
    group = i // 7
    part = jnp.where(group < 15, group % 3, 3)
    head = jnp.where(group < 15, group // 3, group - 15)
    want = part * heads * PAD_DIM + head * PAD_DIM + w * 7 + e
    return ((dst == want) & (i < 140)).astype(BF16)


def gelu(u):
    t = jnp.tanh(0.7978845608 * (u + 0.044715 * u * u * u))
    h = 0.5 * u * (1.0 + t)
    d = 0.5 * (1.0 + t) + 0.5 * u * (1.0 - t * t) * 0.7978845608 * (1.0 + 3 * 0.044715 * u * u)
    return h, d


def pad_rows(a, rows):
    return jnp.pad(a, ((0, rows - a.shape[0]), (0, 0)))


def on_device(
    cells_in, lengths, w_qkv, w_out, w_up, w_down, ln1_gain, ln1_shift, bias_qv, bias_out,
    ln2_gain, ln2_shift, bias_up, bias_down, cotangent,
):
    wide = lax.axis_size("wide")
    inner = wide // OUTER
    shards = [w_qkv, w_out, w_up, w_down]
    if inner > 1:
        groups = [[o * inner + i for i in range(inner)] for o in range(OUTER)]
        shards = [
            lax.all_gather(s, "wide", axis=1, tiled=True, axis_index_groups=groups) for s in shards
        ]
    width = cells_in.shape[3]
    local_rows = cells_in.shape[2]
    heads = width // HEAD_DIM // 2
    n = lax.axis_index("narrow")
    y, c = n // 2, n % 2
    w_a = jnp.concatenate([shards[0].reshape(-1, width), shards[1].reshape(-1, width)], axis=0)
    rows = -(-w_a.shape[0] // PIECE) * PIECE
    w_a = pad_rows(w_a, rows)
    w_u = pad_rows(shards[2].reshape(-1, width), rows)
    w_d = pad_rows(shards[3].reshape(-1, width), rows)
    used = shards[2].size // width

    g_a, g_u, g_d, cells, cot = gather_all(inner, (w_a, w_u, w_d), cells_in[:, 0], cotangent[:, 0])
    order = order_matrix()
    mats = [dot_nn(order, g_a.reshape(2, OUTER * rows, width)[i]).astype(BF16) for i in range(2)]
    half = heads // 2 * PAD_DIM
    w_parts = [jnp.concatenate([m[p * half : (p + 1) * half] for m in mats], axis=0) for p in range(4)]
    wq, wk, wv, wo = w_parts
    wu = g_u.reshape(16 * rows, width)
    wd = g_d.reshape(16 * rows, width)

    def pick_heads(b):
        b = b.reshape(2, 2, heads // 2, HEAD_DIM)
        b = lax.dynamic_index_in_dim(b, c, axis=1, keepdims=False)
        return jnp.pad(b, ((0, 0), (0, 0), (0, PAD_DIM - HEAD_DIM))).reshape(-1)

    bq = pick_heads(bias_qv[:width])
    bv = pick_heads(bias_qv[width:])

    b_u = bias_up.reshape(2, 2, used, 4, 2)
    b_u = lax.dynamic_index_in_dim(b_u, c, axis=1, keepdims=False).transpose(0, 3, 2, 1)
    b_u = jnp.pad(b_u, ((0, 0), (0, 0), (0, 0), (0, rows - used))).reshape(-1)

    total = 4 * local_rows
    x32 = cells.reshape(total, width).astype(F32)
    cell_len = lax.dynamic_index_in_dim(lengths[:, 0], y, keepdims=False)
    xhat1, rstd1 = norm_parts(x32)
    normed = (xhat1 * ln1_gain + ln1_shift).astype(BF16)
    q = (dot_nt(normed, wq) + bq).astype(BF16)
    k = dot_nt(normed, wk).astype(BF16)
    v = (dot_nt(normed, wv) + bv).astype(BF16)

    def split(a):
        return a.reshape(total, heads, PAD_DIM).transpose(1, 0, 2)

    def join(a):
        return a.transpose(1, 0, 2).reshape(total, heads * PAD_DIM)

    qh, kh, vh = split(q), split(k), split(v)
    mixed_h, sums = attend(qh, kh, vh, cell_len)
    mixed = join(mixed_h)

    sibling = [(0, 1), (1, 0), (2, 3), (3, 2)]

    def own_rows(a):
        a = a.reshape(2, 2, local_rows, a.shape[-1])
        return lax.dynamic_index_in_dim(a, c, axis=1, keepdims=False).reshape(2 * local_rows, -1)

    def other_rows(a):
        a = a.reshape(2, 2, local_rows, a.shape[-1])
        return lax.dynamic_index_in_dim(a, 1 - c, axis=1, keepdims=False).reshape(2 * local_rows, -1)

    def pair_sum(a):
        got = lax.ppermute(other_rows(a).astype(BF16), "narrow", sibling)
        return own_rows(a) + got.astype(F32)

    def pair_gather(a):
        got = lax.ppermute(a, "narrow", sibling)
        a = a.reshape(2, local_rows, -1)
        got = got.reshape(2, local_rows, -1)
        first = jnp.where(c == 0, a, got)
        second = jnp.where(c == 0, got, a)
        return jnp.stack([first, second], axis=1).reshape(total, -1)

    middle = own_rows(x32) + pair_sum(dot_nn(mixed, wo)) + bias_out
    xhat2, rstd2 = norm_parts(middle)
    normed2 = pair_gather((xhat2 * ln2_gain + ln2_shift).astype(BF16))
    upper = dot_nt(normed2, wu) + b_u
    hidden, slope = gelu(upper)
    hidden = hidden.astype(BF16)
    g_all = cot.reshape(total, width)
    out = (middle + pair_sum(dot_nn(hidden, wd)) + bias_down).astype(BF16)
    grad_upper = (dot_nt(g_all, wd) * slope).astype(BF16)
    p_d = dot_tn(hidden, g_all).astype(BF16).reshape(16, rows, width)
    p_u = dot_tn(grad_upper, normed2).astype(BF16).reshape(16, rows, width)
    gn2 = pair_sum(dot_nn(grad_upper, wu))
    g_own = own_rows(g_all).astype(F32)
    grad_middle = g_own + norm_back(gn2, ln2_gain, xhat2, rstd2)
    grad_att_own = grad_middle.astype(BF16)
    grad_att = pair_gather(grad_att_own)
    grad_mixed = dot_nt(grad_att, wo).astype(BF16)
    gq, gk, gv = attend_back(qh, kh, vh, split(grad_mixed), cell_len, sums)
    gq, gk, gv = (join(a.astype(BF16)) for a in (gq, gk, gv))
    grads_a = [dot_tn(a, normed).astype(BF16) for a in (gq, gk, gv)] + [
        dot_tn(mixed, grad_att).astype(BF16)
    ]
    p_a = []
    for i in range(2):
        stacked = jnp.concatenate([a[i * half : (i + 1) * half] for a in grads_a], axis=0)
        p_a.append(dot_tn(order, stacked).astype(BF16).reshape(OUTER, rows, width))
    p_a = jnp.concatenate(p_a, axis=0)
    gn1 = pair_sum(dot_nn(gq, wq) + dot_nn(gk, wk) + dot_nn(gv, wv))
    xo, ro = own_rows(xhat1), own_rows(rstd1)
    grad_in = (grad_middle + norm_back(gn1, ln1_gain, xo, ro)).astype(BF16)

    def col_sum(a):
        return jnp.sum(a.astype(F32), axis=0)

    def put_heads(s):
        s = s.reshape(2, 1, heads // 2, PAD_DIM)[..., :HEAD_DIM]
        zero = jnp.zeros_like(s)
        return jnp.where(c == 0, jnp.concatenate([s, zero], 1), jnp.concatenate([zero, s], 1)).reshape(-1)

    def put_hidden(s):
        s = s.reshape(2, 2, 4, rows)[..., :used].transpose(0, 3, 2, 1).reshape(2, 1, -1)
        zero = jnp.zeros_like(s)
        return jnp.where(c == 0, jnp.concatenate([s, zero], 1), jnp.concatenate([zero, s], 1)).reshape(-1)

    small = jnp.concatenate(
        [
            col_sum(gn1 * xo), col_sum(gn1),
            put_heads(col_sum(gq)), put_heads(col_sum(gv)),
            col_sum(grad_att_own), col_sum(gn2 * xhat2), col_sum(gn2),
            put_hidden(col_sum(grad_upper)), col_sum(g_own),
        ]
    ).reshape(-1, width)
    small = pad_rows(small, 16)
    reduced, small = reduce_all(inner, (p_d, p_u, p_a), small)

    def swap_back(a):
        a = a.reshape(2, local_rows, width)
        mine = lax.dynamic_index_in_dim(a, y, axis=0, keepdims=False)
        theirs = lax.dynamic_index_in_dim(a, 1 - y, axis=0, keepdims=False)
        got = lax.ppermute(theirs, "narrow", [(0, 2), (1, 3), (2, 0), (3, 1)])
        first = jnp.where(y == 0, mine, got)
        second = jnp.where(y == 0, got, mine)
        return jnp.stack([first, second], axis=0)[:, None]

    out, grad_in = swap_back(out), swap_back(grad_in)
    qkv_rows = shards[0].size // width
    grads = [
        reduced[2][:qkv_rows].reshape(shards[0].shape),
        reduced[2][qkv_rows : qkv_rows + shards[1].size // width].reshape(shards[1].shape),
        reduced[1][:used],
        reduced[0][:used],
    ]
    grads = [g.reshape(s.shape) for g, s in zip(grads, shards)]
    if inner > 1:
        grads = [
            lax.psum_scatter(g, "wide", scatter_dimension=1, axis_index_groups=groups, tiled=True)
            for g in grads
        ]
    hid = bias_up.shape[0] // width
    flat = [
        small[0], small[1], small[2:4].reshape(-1), small[4], small[5], small[6],
        small[7 : 7 + hid].reshape(-1), small[7 + hid],
    ]
    return (out, grad_in, *grads, *flat)


def solution(mesh):
    cell = P(None, "wide", "narrow", None)
    shard = P("narrow", "wide")
    return jax.shard_map(
        on_device,
        mesh=mesh,
        in_specs=(cell, P(None, "wide"), *[shard] * 4, *[P()] * 8, cell),
        out_specs=(cell, cell, *[shard] * 4, *[P()] * 8),
        check_vma=False,
    )
```

```python
import functools

import jax
import jax.numpy as jnp
import numpy as np
from jax import lax
from jax.experimental import pallas as pl
from jax.experimental.pallas import tpu as pltpu
from jax.sharding import PartitionSpec as P

HEAD_DIM = 56
PAD_DIM = 64
OUTER = 8
PIECE = 48
NORM_EPS = 1e-05
SCALE = HEAD_DIM ** (-0.5)
SCALE2 = SCALE * 1.4426950408889634
MESH = pl.DeviceIdType.MESH
BF16 = jnp.bfloat16
F32 = jnp.float32
BLOCK = 256
VMEM_LIMIT = 62 * 2**20


def place(inner):
    w = lax.axis_index("wide")
    n = lax.axis_index("narrow")
    outer = w // inner
    return outer // 2, outer % 2, n // 2, n % 2, w % inner


def device(inner, z, x, y, c, wi):
    return ((2 * z + x) * inner + wi, 2 * y + c)


def slab(y, x, z):
    return y * 8 + x * 4 + z


def remote(src, dst, send, recv, dev):
    return pltpu.make_async_remote_copy(
        src_ref=src, dst_ref=dst, send_sem=send, recv_sem=recv, device_id=dev, device_id_type=MESH
    )


def greet(devices):
    barrier = pltpu.get_barrier_semaphore()
    for dev in devices:
        pl.semaphore_signal(barrier, inc=1, device_id=dev, device_id_type=MESH)
    pl.semaphore_wait(barrier, len(devices))


class Links:
    def __init__(self, inner):
        z, x, y, c, wi = place(inner)
        self.z, self.x, self.y, self.c = z, x, y, c
        self.along = [device(inner, (z + d) % 4, x, y, c, wi) for d in (1, 2, 3)]
        self.xdev = device(inner, z, 1 - x, y, c, wi)
        self.ydev = device(inner, z, x, 1 - y, c, wi)
        self.cdev = device(inner, z, x, y, 1 - c, wi)
        self.pair = device(inner, z + 1 - 2 * (z % 2), x, y, c, wi)
        self.everyone = [*self.along, self.xdev, self.ydev, self.cdev]

    def back(self, d):
        return (self.z + 4 - d) % 4


dma = pltpu.SemaphoreType.DMA


def cut(ref, s, k):
    return ref.at[s, pl.ds(k * PIECE, PIECE)]


class LineGather:
    @staticmethod
    def sems(pieces):
        return [dma((pieces, 3)), dma((pieces, 3))]

    def __init__(self, links, own, out, at, sems):
        self.n, self.own, self.out, self.at = links, own, out, at
        self.zs, self.zr = sems

    def copy(self, k, d):
        src = self.own.at[pl.ds(k * PIECE, PIECE)]
        dst = cut(self.out, self.at(self.n.z), k)
        return remote(src, dst, self.zs.at[k, d - 1], self.zr.at[k, d - 1], self.n.along[d - 1])

    def came(self, k, d):
        v = cut(self.out, self.at(self.n.back(d)), k)
        return remote(v, v, self.zs.at[k, d - 1], self.zr.at[k, d - 1], self.n.along[d - 1])

    def start(self, k):
        for d in (1, 2, 3):
            self.copy(k, d).start()

    def wait(self, k):
        for d in (1, 2, 3):
            self.came(k, d).wait_recv()

    def sent(self, k):
        for d in (1, 2, 3):
            self.copy(k, d).wait_send()


class PlaneGather:
    @staticmethod
    def sems(pieces):
        return [dma((pieces, 4)) for _ in range(4)] + [dma((pieces, 2)) for _ in range(4)]

    def __init__(self, links, src, out, sems):
        self.n, self.src, self.out = links, src, out
        self.xs, self.xr, self.ys, self.yr, self.fxs, self.fxr, self.fys, self.fyr = sems

    def copy(self, k, d, over_x):
        n = self.n
        dst = cut(self.out, slab(n.y, n.x, n.back(d)), k)
        if over_x:
            return remote(self.src(k, d), dst, self.xs.at[k, d], self.xr.at[k, d], n.xdev)
        return remote(self.src(k, d), dst, self.ys.at[k, d], self.yr.at[k, d], n.ydev)

    def came(self, k, d, over_x):
        n = self.n
        if over_x:
            v = cut(self.out, slab(n.y, 1 - n.x, n.back(d)), k)
            return remote(v, v, self.xs.at[k, d], self.xr.at[k, d], n.xdev)
        v = cut(self.out, slab(1 - n.y, n.x, n.back(d)), k)
        return remote(v, v, self.ys.at[k, d], self.yr.at[k, d], n.ydev)

    def onward(self, k, d):
        n = self.n
        if d < 2:
            v = cut(self.out, slab(n.y, 1 - n.x, n.back(d)), k)
            return remote(v, v, self.fys.at[k, d], self.fyr.at[k, d], n.ydev)
        v = cut(self.out, slab(1 - n.y, n.x, n.back(d)), k)
        return remote(v, v, self.fxs.at[k, d - 2], self.fxr.at[k, d - 2], n.xdev)

    def crossed(self, k, d):
        n = self.n
        v = cut(self.out, slab(1 - n.y, 1 - n.x, n.back(d)), k)
        if d < 2:
            return remote(v, v, self.fys.at[k, d], self.fyr.at[k, d], n.ydev)
        return remote(v, v, self.fxs.at[k, d - 2], self.fxr.at[k, d - 2], n.xdev)

    def start(self, k, d):
        self.copy(k, d, True).start()
        self.copy(k, d, False).start()

    def forward(self, k):
        for d in (0, 1):
            self.came(k, d, True).wait_recv()
            self.onward(k, d).start()
            self.came(k, d + 2, False).wait_recv()
            self.onward(k, d + 2).start()

    def wait(self, k):
        for d in (0, 1):
            self.came(k, d + 2, True).wait_recv()
            self.came(k, d, False).wait_recv()
            self.crossed(k, d).wait_recv()
            self.crossed(k, d + 2).wait_recv()

    def sent(self, k):
        for d in range(4):
            self.copy(k, d, True).wait_send()
            self.copy(k, d, False).wait_send()
            self.onward(k, d).wait_send()


class PlaneReduce:
    @staticmethod
    def scratch(pieces, width):
        return [
            pltpu.VMEM((pieces, 4, PIECE, width), BF16),
            pltpu.VMEM((pieces, 4, PIECE, width), BF16),
            pltpu.VMEM((pieces, 4, PIECE, width), BF16),
            pltpu.VMEM((pieces, 4, PIECE, width), BF16),
        ] + [dma((pieces, 2)) for _ in range(6)]

    def __init__(self, links, part, out, scratch):
        self.n, self.part, self.out = links, part, out
        self.r1, self.rx, self.ry, self.mine = scratch[:4]
        self.s1, self.q1, self.s2, self.q2, self.s3, self.q3 = scratch[4:]

    def cut(self, k, s):
        return self.part.at[pl.ds(s, 2), pl.ds(k * PIECE, PIECE)]

    def load(self, k, s, count):
        return self.part[pl.ds(s, count), pl.ds(k * PIECE, PIECE)].astype(F32)

    def first(self, k):
        n, r = self.n, self.r1
        a = slab(1 - n.y, 1 - n.x, 0)
        return (
            remote(self.cut(k, a), r.at[k, pl.ds(0, 2)], self.s1.at[k, 0], self.q1.at[k, 0], n.ydev),
            remote(self.cut(k, a + 2), r.at[k, pl.ds(2, 2)], self.s1.at[k, 1], self.q1.at[k, 1], n.xdev),
        )

    def second(self, k):
        n = self.n
        ax, ay = slab(n.y, 1 - n.x, 2), slab(1 - n.y, n.x, 0)
        return (
            remote(self.cut(k, ax), self.rx.at[k, pl.ds(2, 2)], self.s2.at[k, 0], self.q2.at[k, 0], n.xdev),
            remote(self.cut(k, ay), self.ry.at[k, pl.ds(0, 2)], self.s2.at[k, 1], self.q2.at[k, 1], n.ydev),
        )

    def third(self, k):
        n, m = self.n, self.mine
        return (
            remote(m.at[k, pl.ds(0, 2)], self.rx.at[k, pl.ds(0, 2)], self.s3.at[k, 0], self.q3.at[k, 0], n.xdev),
            remote(m.at[k, pl.ds(2, 2)], self.ry.at[k, pl.ds(2, 2)], self.s3.at[k, 1], self.q3.at[k, 1], n.ydev),
        )

    def start(self, k):
        for cp in (*self.first(k), *self.second(k)):
            cp.start()

    def forward(self, k):
        n, f, t = self.n, self.first(k), self.third(k)
        f[0].wait_recv()
        self.mine[k, 0:2] = (self.load(k, slab(n.y, 1 - n.x, 0), 2) + self.r1[k, 0:2].astype(F32)).astype(BF16)
        t[0].start()
        f[1].wait_recv()
        self.mine[k, 2:4] = (self.load(k, slab(1 - n.y, n.x, 2), 2) + self.r1[k, 2:4].astype(F32)).astype(BF16)
        t[1].start()

    def finish(self, k):
        n = self.n
        for cp in (*self.second(k), *self.third(k)):
            cp.wait_recv()
        for j in (0, 2):
            self.out[pl.ds(j, 2), pl.ds(k * PIECE, PIECE)] = (
                self.load(k, slab(n.y, n.x, j), 2)
                + self.rx[k, j : j + 2].astype(F32)
                + self.ry[k, j : j + 2].astype(F32)
            ).astype(BF16)

    def sent(self, k):
        for cp in (*self.first(k), *self.second(k), *self.third(k)):
            cp.wait_send()


class LineReduce:
    @staticmethod
    def scratch(pieces, width):
        return [pltpu.VMEM((pieces, 3, PIECE, width), BF16), dma((pieces, 3)), dma((pieces, 3))]

    def __init__(self, links, line, out, used, scratch):
        self.n, self.line, self.out, self.used = links, line, out, used
        self.rz, self.sz, self.qz = scratch

    def copy(self, k, d):
        n = self.n
        src = cut(self.line, (n.z + d) % 4, k)
        return remote(src, self.rz.at[k, d - 1], self.sz.at[k, d - 1], self.qz.at[k, d - 1], n.along[d - 1])

    def start(self, k):
        for d in (1, 2, 3):
            self.copy(k, d).start()

    def finish(self, k):
        for d in (1, 2, 3):
            self.copy(k, d).wait_recv()
        total = self.line[self.n.z, pl.ds(k * PIECE, PIECE)].astype(F32)
        for d in range(3):
            total += self.rz[k, d].astype(F32)
        rows = min(PIECE, self.used - k * PIECE)
        self.out[pl.ds(k * PIECE, rows)] = total[:rows]

    def sent(self, k):
        for d in (1, 2, 3):
            self.copy(k, d).wait_send()


class Steps:
    def __init__(self, steps):
        self.steps = list(steps)

    def __call__(self, count=1):
        for _ in range(count):
            if self.steps:
                self.steps.pop(0)()

    def rest(self):
        self(len(self.steps))


def dot(a, b, dims):
    return lax.dot_general(a, b, (dims, ((), ())), preferred_element_type=F32)


def dot_nn(a, b):
    return dot(a, b, ((1,), (0,)))


def dot_nt(a, b):
    return dot(a, b, ((1,), (1,)))


def dot_tn(a, b):
    return dot(a, b, ((0,), (0,)))


def rows_at(i, size):
    return pl.ds(pl.multiple_of(i * size, size), size)


def loop(count, body):
    def step(i, carry):
        body(i)
        return carry

    lax.fori_loop(0, count, step, 0)


def norm_parts(v):
    center = v - jnp.mean(v, axis=-1, keepdims=True)
    rstd = lax.rsqrt(jnp.mean(center * center, axis=-1, keepdims=True) + NORM_EPS)
    return center * rstd, rstd


def norm_back(e, gain, xhat, rstd):
    eg = e * gain
    return rstd * (
        eg - jnp.mean(eg, axis=-1, keepdims=True) - xhat * jnp.mean(eg * xhat, axis=-1, keepdims=True)
    )


def gelu(u):
    t = jnp.tanh(0.7978845608 * (u + 0.044715 * u * u * u))
    h = 0.5 * u * (1.0 + t)
    d = 0.5 * (1.0 + t) + 0.5 * u * (1.0 - t * t) * 0.7978845608 * (1.0 + 3 * 0.044715 * u * u)
    return h, d


STRIP = 32


def k1_kernel(inner, pieces, *refs):
    it = iter(refs)
    take = lambda n: [next(it) for _ in range(n)]
    wa, wu, x_ref, g_ref, gain, shift = take(6)
    out_a, line_u, cells, normed, cot = take(5)
    za = take(2)
    pa = take(8)
    zu = take(2)
    ss, sr, ls = take(3)
    n = Links(inner)
    y, c = n.y, n.c
    greet(n.everyone)
    lga = LineGather(n, wa, out_a, lambda z: slab(y, n.x, z), za)
    lgu = LineGather(n, wu, line_u, lambda z: z, zu)

    def source(k, d):
        return wa.at[pl.ds(k * PIECE, PIECE)] if d == 0 else cut(out_a, slab(y, n.x, n.back(d)), k)

    pga = PlaneGather(n, source, out_a, pa)
    mine_a = pltpu.make_async_copy(wa, out_a.at[slab(y, n.x, n.z)], ls.at[0])
    mine_u = pltpu.make_async_copy(wu, line_u.at[n.z], ls.at[1])

    n_own, n_sib = 2 * y + c, 2 * y + 1 - c
    n_y, n_ys = 2 * (1 - y) + c, 2 * (1 - y) + 1 - c

    def swap(i, src, dst):
        return (
            pltpu.make_async_copy(src.at[y], dst.at[n_own], ls.at[2 + i]),
            remote(src.at[y], dst.at[n_own], ss.at[i, 0], sr.at[i, 0], n.cdev),
            remote(src.at[1 - y], dst.at[n_own], ss.at[i, 1], sr.at[i, 1], n.ydev),
            remote(dst.at[n_y], dst.at[n_y], ss.at[i, 1], sr.at[i, 1], n.ydev),
            remote(dst.at[n_y], dst.at[n_y], ss.at[i, 2], sr.at[i, 2], n.cdev),
            remote(dst.at[n_sib], dst.at[n_sib], ss.at[i, 0], sr.at[i, 0], n.cdev),
            remote(dst.at[n_ys], dst.at[n_ys], ss.at[i, 2], sr.at[i, 2], n.cdev),
        )

    xp, gp = swap(0, x_ref, cells), swap(1, g_ref, cot)

    def begin(p):
        for cp in p[:3]:
            cp.start()

    def middle(p):
        p[3].wait_recv()
        p[4].start()

    def end(p):
        p[0].wait()
        p[5].wait_recv()
        p[6].wait_recv()

    def done(p):
        for cp in (p[1], p[2], p[4]):
            cp.wait_send()

    for k in range(pieces):
        lga.start(k)
    for k in range(pieces):
        pga.start(k, 0)
    begin(xp)
    mine_a.start()
    mine_u.start()
    for k in range(pieces):
        for d in (1, 2, 3):
            lga.came(k, d).wait_recv()
            pga.start(k, d)
        if k == 0:
            for kk in range(pieces):
                lgu.start(kk)
            middle(xp)
        if k > 0:
            pga.forward(k - 1)
    begin(gp)
    end(xp)

    def norm(i):
        for b in range(4):
            r = rows_at(i, STRIP)
            xhat, _ = norm_parts(cells[b, r].astype(F32))
            normed[b, r] = (xhat * gain[...] + shift[...]).astype(BF16)

    loop(cells.shape[1] // STRIP, norm)
    pga.forward(pieces - 1)
    middle(gp)
    for k in range(pieces):
        pga.wait(k)
        lgu.wait(k)
    end(gp)
    mine_a.wait()
    mine_u.wait()
    for k in range(pieces):
        lga.sent(k)
        lgu.sent(k)
        pga.sent(k)
    done(xp)
    done(gp)


def k2_kernel(inner, pieces, *refs):
    it = iter(refs)
    take = lambda n: [next(it) for _ in range(n)]
    g_a, order, normed, cells, bias_qkv, bias_out, gain, shift, cell_len, line_u, wd = take(11)
    out_u, line_d, qkv, mixed, lse, middle, normed2, wa = take(8)
    bias, own, send, got = take(4)
    pu = take(8)
    zd = take(2)
    es, er, ls = take(3)
    n = Links(inner)
    y, c = n.y, n.c
    greet(n.everyone)
    lgd = LineGather(n, wd, line_d, lambda z: z, zd)
    pgu = PlaneGather(n, lambda k, d: cut(line_u, n.back(d), k), out_u, pu)
    locals_ = [
        pltpu.make_async_copy(line_u, out_u.at[pl.ds(slab(y, n.x, 0), 4)], ls.at[0]),
        pltpu.make_async_copy(wd, line_d.at[n.z], ls.at[1]),
    ]
    for k in range(pieces):
        for d in range(4):
            pgu.start(k, d)
    for k in range(pieces):
        lgd.start(k)
    for cp in locals_:
        cp.start()
    steps = Steps([functools.partial(pgu.forward, k) for k in range(pieces)])

    heads = order.shape[0] // (4 * PAD_DIM)
    part = 2 * heads * PAD_DIM
    for yy in range(2):
        for p in range(4):
            m = dot_nn(order[p * heads * PAD_DIM : (p + 1) * heads * PAD_DIM], g_a[yy]).astype(BF16)
            for h in range(heads):
                wa[pl.ds(p * part + h * 2 * PAD_DIM + yy * PAD_DIM, PAD_DIM)] = m[h * PAD_DIM : (h + 1) * PAD_DIM]

    blocks = qkv.shape[0] // BLOCK
    total = blocks * BLOCK

    def project(t):
        r = rows_at(t, BLOCK)
        a = normed[r]
        for p in range(3):
            w = wa[p * part : (p + 1) * part]
            cols = slice(p * part, (p + 1) * part)
            qkv[r, cols] = (dot_nt(a, w) + bias_qkv[:, cols]).astype(BF16)

    loop(blocks, project)
    steps()
    key = lax.broadcasted_iota(jnp.int32, (BLOCK, total), 1)
    row = lax.broadcasted_iota(jnp.int32, (BLOCK, total), 0)
    for i in range(blocks):
        ok = (key <= row + i * BLOCK) & (key < cell_len[0])
        bias[i] = jnp.where(ok, 0.0, -1e30)
    lane = lax.broadcasted_iota(jnp.int32, (BLOCK, 2 * PAD_DIM), 1)
    low = lane < PAD_DIM
    lse[...] = jnp.zeros_like(lse)

    for i in range(blocks):
        r = slice(i * BLOCK, (i + 1) * BLOCK)
        end = (i + 1) * BLOCK

        def attend(j, r=r, end=end, i=i):
            def cols(p):
                return pl.ds(pl.multiple_of(p * part + j * 2 * PAD_DIM, 2 * PAD_DIM), 2 * PAD_DIM)

            q, k, v = qkv[r, cols(0)], qkv[:end, cols(1)], qkv[:end, cols(2)]
            outs = []
            for half in range(2):
                qm = jnp.where(low if half == 0 else ~low, q, jnp.zeros_like(q))
                s = dot_nt(qm, k) * SCALE2 + bias[i, :, :end]
                m = jnp.max(s, axis=-1, keepdims=True)
                e = jnp.exp2(s - m)
                t = jnp.sum(e, axis=-1, keepdims=True)
                p = (e * (1.0 / t)).astype(BF16)
                outs.append(dot_nn(p, v))
                lse[r] = jnp.where(lane == 2 * j + half, m + jnp.log2(t), lse[r])
            mixed[r, cols(0)] = jnp.where(low, outs[0], outs[1]).astype(BF16)

        loop(heads, attend)
        steps()

    wo = wa.at[pl.ds(3 * part, part)]

    def swap(i, h):
        return remote(send.at[h], got.at[h], es.at[i, h], er.at[i, h], n.cdev)

    def n2(h):
        v = normed2.at[pl.ds(pl.multiple_of((2 * h + c) * BLOCK, BLOCK), BLOCK)]
        return remote(v, v, es.at[1, h], er.at[1, h], n.cdev)

    def n2_in(h):
        v = normed2.at[pl.ds(pl.multiple_of((2 * h + 1 - c) * BLOCK, BLOCK), BLOCK)]
        return remote(v, v, es.at[1, h], er.at[1, h], n.cdev)

    for h in range(2):
        send[h] = dot_nn(mixed[rows_at(2 * h + 1 - c, BLOCK)], wo[...]).astype(BF16)
        swap(0, h).start()
    for h in range(2):
        own[h] = dot_nn(mixed[rows_at(2 * h + c, BLOCK)], wo[...])
    for h in range(2):
        swap(0, h).wait_recv()

        def finish(i, h=h):
            r = rows_at(i, STRIP)
            x = cells[2 * h + c, r].astype(F32)
            mid = x + own[h, r] + got[h, r].astype(F32) + bias_out[...]
            middle[h, r] = mid
            xhat, _ = norm_parts(mid)
            start = pl.multiple_of((2 * h + c) * BLOCK + i * STRIP, STRIP)
            normed2[pl.ds(start, STRIP)] = (xhat * gain[...] + shift[...]).astype(BF16)

        loop(BLOCK // STRIP, finish)
        n2(h).start()
    steps.rest()
    for h in range(2):
        n2_in(h).wait_recv()
    for k in range(pieces):
        pgu.wait(k)
        lgd.wait(k)
    for cp in locals_:
        cp.wait()
    for h in range(2):
        swap(0, h).wait_send()
        n2(h).wait_send()
    for k in range(pieces):
        pgu.sent(k)
        lgd.sent(k)


CHUNK = 768
WIDE = 256


def k3_kernel(inner, pieces, *refs):
    it = iter(refs)
    take = lambda n: [next(it) for _ in range(n)]
    normed2, wu, bias_up, cot, line_d = take(5)
    out_d, hidden, slope, part_d = take(4)
    pd = take(8)
    (ls,) = take(1)
    n = Links(inner)
    greet([n.xdev, n.ydev])
    pgd = PlaneGather(n, lambda k, d: cut(line_d, n.back(d), k), out_d, pd)
    mine = pltpu.make_async_copy(line_d, out_d.at[pl.ds(slab(n.y, n.x, 0), 4)], ls.at[0])
    for k in range(pieces):
        for d in range(4):
            pgd.start(k, d)
    mine.start()
    steps = Steps([functools.partial(pgd.forward, k) for k in range(pieces)])
    units = hidden.shape[1]

    def up(t):
        r = rows_at(t, BLOCK)
        a = normed2[r]
        for q in range(units // CHUNK):
            cols = slice(q * CHUNK, (q + 1) * CHUNK)
            h, d = gelu(dot_nt(a, wu[cols]) + bias_up[:, cols])
            hidden[r, cols] = h.astype(BF16)
            slope[r, cols] = d.astype(BF16)

    loop(hidden.shape[0] // BLOCK, up)
    steps()

    def grad(q):
        part_d[rows_at(q, WIDE)] = dot_tn(hidden[:, rows_at(q, WIDE)], cot[...]).astype(BF16)

    loop(units // WIDE, grad)
    steps.rest()
    for k in range(pieces):
        pgd.wait(k)
    mine.wait()
    for k in range(pieces):
        pgd.sent(k)


def k4_kernel(inner, pieces, *refs):
    it = iter(refs)
    take = lambda n: [next(it) for _ in range(n)]
    hidden, slope, wd, wu, cot, normed2, middle, mixed, wo, bias_down, gain, part_d = take(12)
    cells_out, line_d, part_u, part_o, grad_mid, grad_mixed, sums, sum_up = take(8)
    grad_up, grad_att, own, send, got, outb = take(6)
    rd = take(10)
    es, er, ys, yr, ls = take(5)
    n = Links(inner)
    y, c = n.y, n.c
    greet([n.xdev, n.ydev, n.cdev])
    red = PlaneReduce(n, part_d, line_d, rd)
    for k in range(pieces):
        red.start(k)
    steps = Steps(
        [functools.partial(red.forward, k) for k in range(pieces)]
        + [functools.partial(red.finish, k) for k in range(pieces)]
    )
    units = hidden.shape[1]
    load = pltpu.make_async_copy(hidden, grad_up, ls.at[1])
    load.start()
    load.wait()

    def swap(i, h):
        return remote(send.at[i, h], got.at[i, h], es.at[i, h], er.at[i, h], n.cdev)

    for h in range(2):
        send[0, h] = dot_nn(grad_up[rows_at(2 * h + 1 - c, BLOCK)], wd[...]).astype(BF16)
        swap(0, h).start()
    for h in range(2):
        own[h] = dot_nn(grad_up[rows_at(2 * h + c, BLOCK)], wd[...])
    steps()
    for h in range(2):
        swap(0, h).wait_recv()

        def finish(i, h=h):
            r = rows_at(i, STRIP)
            outb[h, r] = (middle[h, r] + own[h, r] + got[0, h, r].astype(F32) + bias_down[...]).astype(BF16)

        loop(BLOCK // STRIP, finish)
    keep = pltpu.make_async_copy(outb.at[y], cells_out.at[y], ls.at[0])
    over = remote(outb.at[1 - y], cells_out.at[y], ys.at[0], yr.at[0], n.ydev)
    over_in = remote(outb.at[1 - y], cells_out.at[1 - y], ys.at[0], yr.at[0], n.ydev)
    keep.start()
    over.start()

    sum_up[...] = jnp.zeros_like(sum_up)

    def back(t):
        r = rows_at(t, BLOCK)
        a = cot[r]
        for q in range(units // CHUNK):
            cols = slice(q * CHUNK, (q + 1) * CHUNK)
            g = (dot_nt(a, wd[cols]) * slope[r, cols].astype(F32)).astype(BF16)
            grad_up[r, cols] = g
            sum_up[:, cols] += jnp.sum(g.astype(F32), axis=0, keepdims=True)

    loop(hidden.shape[0] // BLOCK, back)
    steps()
    for h in range(2):
        send[1, h] = dot_nn(grad_up[rows_at(2 * h + 1 - c, BLOCK)], wu[...]).astype(BF16)
        swap(1, h).start()
    for h in range(2):
        own[h] = dot_nn(grad_up[rows_at(2 * h + c, BLOCK)], wu[...])
    steps()
    sums[...] = jnp.zeros_like(sums)

    def att(h):
        v = grad_att.at[pl.ds(pl.multiple_of((2 * h + c) * BLOCK, BLOCK), BLOCK)]
        return remote(v, v, es.at[2, h], er.at[2, h], n.cdev)

    def att_in(h):
        v = grad_att.at[pl.ds(pl.multiple_of((2 * h + 1 - c) * BLOCK, BLOCK), BLOCK)]
        return remote(v, v, es.at[2, h], er.at[2, h], n.cdev)

    for h in range(2):
        swap(1, h).wait_recv()

        def finish2(i, h=h):
            r = rows_at(i, STRIP)
            at = pl.ds(pl.multiple_of((2 * h + c) * BLOCK + i * STRIP, STRIP), STRIP)
            e = own[h, r] + got[1, h, r].astype(F32)
            xhat, rstd = norm_parts(middle[h, r])
            top = cot[at].astype(F32)
            g = top + norm_back(e, gain[...], xhat, rstd)
            grad_mid[h, r] = g
            low = g.astype(BF16)
            grad_att[at] = low
            sums[0:1] += jnp.sum(e * xhat, axis=0, keepdims=True)
            sums[1:2] += jnp.sum(e, axis=0, keepdims=True)
            sums[2:3] += jnp.sum(low.astype(F32), axis=0, keepdims=True)
            sums[3:4] += jnp.sum(top, axis=0, keepdims=True)

        loop(BLOCK // STRIP, finish2)
        att(h).start()
    steps()

    def grad(q):
        part_u[rows_at(q, WIDE)] = dot_tn(grad_up[:, rows_at(q, WIDE)], normed2[...]).astype(BF16)

    loop(units // WIDE, grad)
    steps()
    for h in range(2):
        att_in(h).wait_recv()

    def to_heads(t):
        r = rows_at(t, BLOCK)
        grad_mixed[r] = dot_nt(grad_att[r], wo[...]).astype(BF16)

    loop(hidden.shape[0] // BLOCK, to_heads)
    part_o[...] = dot_tn(mixed[...], grad_att[...]).astype(BF16)
    steps.rest()
    keep.wait()
    over_in.wait_recv()
    over.wait_send()
    for h in range(2):
        swap(0, h).wait_send()
        swap(1, h).wait_send()
        att(h).wait_send()
    for k in range(pieces):
        red.sent(k)


def k5_kernel(inner, pieces, used, *refs):
    it = iter(refs)
    take = lambda n: [next(it) for _ in range(n)]
    qkv, lse, grad_mixed, normed, part_o, order_t, cell_len, part_u, line_d = take(9)
    grads, part_a, line_u, grad_d, sums = take(5)
    bias, gk, gv, stack, lse_t = take(5)
    ru = take(10)
    rz = take(3)
    n = Links(inner)
    greet([*n.along, n.xdev, n.ydev])
    red = PlaneReduce(n, part_u, line_u, ru)
    line = LineReduce(n, line_d, grad_d, used, rz)
    for k in range(pieces):
        red.start(k)
        line.start(k)
    steps = Steps(
        [functools.partial(red.forward, k) for k in range(pieces)]
        + [functools.partial(line.finish, k) for k in range(pieces)]
        + [functools.partial(red.finish, k) for k in range(pieces)]
    )
    total = qkv.shape[0]
    part = qkv.shape[1] // 3
    blocks = total // BLOCK
    heads = part // (2 * PAD_DIM)
    key = lax.broadcasted_iota(jnp.int32, (total, BLOCK), 0)
    row = lax.broadcasted_iota(jnp.int32, (total, BLOCK), 1)
    for i in range(blocks):
        ok = (key <= row + i * BLOCK) & (key < cell_len[0])
        bias[i] = jnp.where(ok, 0.0, -1e30)
    lse_t[...] = jnp.transpose(lse[...])
    low = lax.broadcasted_iota(jnp.int32, (BLOCK, 2 * PAD_DIM), 1) < PAD_DIM
    gk[...] = jnp.zeros_like(gk)
    gv[...] = jnp.zeros_like(gv)

    for i in range(blocks):
        r = slice(i * BLOCK, (i + 1) * BLOCK)
        end = (i + 1) * BLOCK
        wide_low = lax.broadcasted_iota(jnp.int32, (end, 2 * PAD_DIM), 1) < PAD_DIM

        def attend(j, r=r, end=end, i=i, wide_low=wide_low):
            def cols(p):
                return pl.ds(pl.multiple_of(p * part + j * 2 * PAD_DIM, 2 * PAD_DIM), 2 * PAD_DIM)

            q, k, v = qkv[r, cols(0)], qkv[:end, cols(1)], qkv[:end, cols(2)]
            g = grad_mixed[r, cols(0)]
            zero = jnp.zeros_like(q)
            gqs, gks, gvs = [], [], []
            for half in range(2):
                here = low if half == 0 else ~low
                s = dot_nt(k, jnp.where(here, q, zero)) * SCALE2 + bias[i, :end]
                p = jnp.exp2(s - lse_t[pl.ds(2 * j + half, 1), r])
                gp = dot_nt(v, jnp.where(here, g, zero))
                inner_sum = jnp.sum(p * gp, axis=0, keepdims=True)
                ds = (p * (gp - inner_sum)).astype(BF16)
                gvs.append(dot_nn(p.astype(BF16), g))
                gks.append(dot_nn(ds, q))
                gqs.append(dot_tn(ds, k))
            gk[:end, cols(0)] += jnp.where(wide_low, gks[0], gks[1])
            gv[:end, cols(0)] += jnp.where(wide_low, gvs[0], gvs[1])
            grads[r, cols(0)] = (jnp.where(low, gqs[0], gqs[1]) * SCALE).astype(BF16)

        loop(heads, attend)
        steps()

    def settle(t):
        r = rows_at(t, BLOCK)
        grads[r, part : 2 * part] = (gk[r] * SCALE).astype(BF16)
        grads[r, 2 * part :] = gv[r].astype(BF16)

    loop(blocks, settle)
    steps()
    sums[...] = jnp.sum(grads[...].astype(F32), axis=0, keepdims=True)
    for p in range(4):
        for h in range(heads):
            if p < 3:
                at = p * part + h * 2 * PAD_DIM
                m = dot_tn(grads[:, at : at + 2 * PAD_DIM], normed[...]).astype(BF16)
            else:
                m = part_o[h * 2 * PAD_DIM : (h + 1) * 2 * PAD_DIM]
            for yy in range(2):
                stack[yy, pl.ds(p * heads * PAD_DIM + h * PAD_DIM, PAD_DIM)] = m[yy * PAD_DIM : (yy + 1) * PAD_DIM]
    steps()
    size = order_t.shape[0]
    for yy in range(2):

        def reorder(i, yy=yy):
            part_a[yy, rows_at(i, size // 3)] = dot_nn(order_t[rows_at(i, size // 3)], stack[yy]).astype(BF16)

        loop(3, reorder)
    steps.rest()
    for k in range(pieces):
        red.sent(k)
        line.sent(k)


def k6_kernel(inner, pieces, used, *refs):
    it = iter(refs)
    take = lambda n: [next(it) for _ in range(n)]
    grads, wa, cells, grad_mid, gain, small, part_a, line_u = take(8)
    grad_in, grad_a, grad_u, small_out = take(4)
    own, send, got, outb, line_a, acc, inbox = take(7)
    ra = take(10)
    rzu = take(3)
    rza = take(3)
    es, er, ys, yr, ls, sa, qa = take(7)
    n = Links(inner)
    y, c = n.y, n.c
    greet(n.everyone)
    red = PlaneReduce(n, part_a, line_a, ra)
    linu = LineReduce(n, line_u, grad_u, used, rzu)
    lina = LineReduce(n, line_a, grad_a, used, rza)
    for k in range(pieces):
        red.start(k)
        linu.start(k)

    def swap(h):
        return remote(send.at[h], got.at[h], es.at[h], er.at[h], n.cdev)

    w = wa.at[pl.ds(0, grads.shape[1])]
    for h in range(2):
        send[h] = dot_nn(grads[rows_at(2 * h + 1 - c, BLOCK)], w[...]).astype(BF16)
        swap(h).start()
    for h in range(2):
        own[h] = dot_nn(grads[rows_at(2 * h + c, BLOCK)], w[...])
    red.forward(0)
    acc[0] = small[...]
    for h in range(2):
        swap(h).wait_recv()

        def finish(i, h=h):
            r = rows_at(i, STRIP)
            e = own[h, r] + got[h, r].astype(F32)
            xhat, rstd = norm_parts(cells[2 * h + c, r].astype(F32))
            outb[h, r] = (grad_mid[h, r] + norm_back(e, gain[...], xhat, rstd)).astype(BF16)
            acc[0, 0:1] += jnp.sum(e * xhat, axis=0, keepdims=True)
            acc[0, 1:2] += jnp.sum(e, axis=0, keepdims=True)

        loop(BLOCK // STRIP, finish)
    keep = pltpu.make_async_copy(outb.at[y], grad_in.at[y], ls.at[0])
    over = remote(outb.at[1 - y], grad_in.at[y], ys.at[0], yr.at[0], n.ydev)
    over_in = remote(outb.at[1 - y], grad_in.at[1 - y], ys.at[0], yr.at[0], n.ydev)
    keep.start()
    over.start()
    peers = [n.cdev, n.xdev, n.ydev, n.pair, n.along[1]]

    def small_copy(i):
        return remote(acc.at[i], inbox.at[i], sa.at[i], qa.at[i], peers[i])

    def small_step(i):
        if i > 0:
            small_copy(i - 1).wait_recv()
            acc[i] = acc[i - 1] + inbox[i - 1]
        if i < 5:
            small_copy(i).start()

    small_step(0)
    red.forward(1)
    small_step(1)
    red.finish(0)
    lina.start(0)
    small_step(2)
    red.forward(2)
    small_step(3)
    for k in range(pieces):
        linu.finish(k)
    small_step(4)
    red.finish(1)
    lina.start(1)
    small_step(5)
    small_out[...] = acc[5]
    lina.finish(0)
    red.finish(2)
    lina.start(2)
    lina.finish(1)
    lina.finish(2)
    keep.wait()
    over_in.wait_recv()
    over.wait_send()
    for h in range(2):
        swap(h).wait_send()
    for i in range(5):
        small_copy(i).wait_send()
    for k in range(pieces):
        red.sent(k)
        linu.sent(k)
        lina.sent(k)


ANY = pl.BlockSpec(memory_space=pl.ANY)
VM = pl.BlockSpec(memory_space=pltpu.VMEM)
SM = pl.BlockSpec(memory_space=pltpu.SMEM)


def call(kernel, ident, name, outs, ins, scratch):
    return pl.pallas_call(
        kernel,
        out_shape=[jax.ShapeDtypeStruct(s, d) for s, d, _ in outs],
        in_specs=[s for _, s in ins],
        out_specs=[s for _, _, s in outs],
        scratch_shapes=scratch,
        compiler_params=pltpu.CompilerParams(
            collective_id=ident, has_side_effects=True, vmem_limit_bytes=VMEM_LIMIT
        ),
        name=name,
    )(*[a for a, _ in ins])


def order_matrix(rows, heads):
    m = np.zeros((4 * heads * PAD_DIM, OUTER * rows), np.float32)
    each = HEAD_DIM // OUTER
    for x in range(2):
        for z in range(4):
            w = 2 * z + x
            for g in range(4 * heads):
                part, head = (g % 3, g // 3) if g < 3 * heads else (3, g - 3 * heads)
                for e in range(each):
                    m[part * heads * PAD_DIM + head * PAD_DIM + w * each + e, (x * 4 + z) * rows + g * each + e] = 1
    return m


def pad_rows(a, rows):
    return jnp.pad(a, ((0, rows - a.shape[0]), (0, 0)))


def on_device(
    cells_in, lengths, w_qkv, w_out, w_up, w_down, ln1_gain, ln1_shift, bias_qv, bias_out,
    ln2_gain, ln2_shift, bias_up, bias_down, cotangent,
):
    wide = lax.axis_size("wide")
    inner = wide // OUTER
    shards = [w_qkv, w_out, w_up, w_down]
    if inner > 1:
        groups = [[o * inner + i for i in range(inner)] for o in range(OUTER)]
        shards = [
            lax.all_gather(s, "wide", axis=1, tiled=True, axis_index_groups=groups) for s in shards
        ]
    width = cells_in.shape[3]
    local_rows = cells_in.shape[2]
    total = 4 * local_rows
    heads = width // HEAD_DIM // 4
    part = 2 * heads * PAD_DIM
    n = lax.axis_index("narrow")
    y, c = n // 2, n % 2
    w_a = jnp.concatenate([shards[0].reshape(-1, width), shards[1].reshape(-1, width)], axis=0)
    used = w_a.shape[0]
    rows = -(-used // PIECE) * PIECE
    pieces = rows // PIECE
    w_a = pad_rows(w_a, rows)
    w_u = pad_rows(shards[2].reshape(-1, width), rows)
    w_d = pad_rows(shards[3].reshape(-1, width), rows)
    units = 16 * rows
    order_np = order_matrix(rows, heads)
    order = jnp.asarray(order_np, BF16)
    order_t = jnp.asarray(np.ascontiguousarray(order_np.T), BF16)

    def line(v):
        return v.reshape(1, -1)

    def pick_heads(b):
        b = b.reshape(2, 2, heads, HEAD_DIM)
        b = lax.dynamic_index_in_dim(b, c, axis=1, keepdims=False)
        b = jnp.pad(b, ((0, 0), (0, 0), (0, PAD_DIM - HEAD_DIM)))
        return b.transpose(1, 0, 2).reshape(-1)

    zero = jnp.zeros((part,), F32)
    bias_qkv = line(jnp.concatenate([pick_heads(bias_qv[:width]), zero, pick_heads(bias_qv[width:])]))
    b_u = bias_up.reshape(2, 2, used, 4, 2)
    b_u = lax.dynamic_index_in_dim(b_u, c, axis=1, keepdims=False).transpose(0, 3, 2, 1)
    b_u = line(jnp.pad(b_u, ((0, 0), (0, 0), (0, 0), (0, rows - used))))
    cell_len = lax.dynamic_slice_in_dim(lengths[:, 0], y, 1)

    slabs = (16, rows, width)
    lines = (4, rows, width)
    g_a, line_u, cells, normed, cot = call(
        functools.partial(k1_kernel, inner, pieces), 0, "gather_first",
        [(slabs, BF16, ANY), (lines, BF16, ANY), ((4, local_rows, width), BF16, VM),
         ((4, local_rows, width), BF16, VM), ((4, local_rows, width), BF16, ANY)],
        [(w_a, ANY), (w_u, ANY), (cells_in[:, 0], ANY), (cotangent[:, 0], ANY),
         (line(ln1_gain), VM), (line(ln1_shift), VM)],
        [*LineGather.sems(pieces), *PlaneGather.sems(pieces), *LineGather.sems(pieces),
         dma((2, 3)), dma((2, 3)), dma((4,))],
    )
    normed = normed.reshape(total, width)
    cot = cot.reshape(total, width)
    half = (2, BLOCK, width)
    g_u, line_d, qkv, mixed, lse, middle, normed2, wa = call(
        functools.partial(k2_kernel, inner, pieces), 1, "attend",
        [(slabs, BF16, ANY), (lines, BF16, ANY), ((total, 3 * part), BF16, VM), ((total, part), BF16, VM),
         ((total, 2 * PAD_DIM), F32, VM), (half, F32, VM), ((total, width), BF16, VM), ((4 * part, width), BF16, VM)],
        [(g_a.reshape(2, OUTER * rows, width), VM), (order, VM), (normed, VM), (cells, VM), (bias_qkv, VM),
         (line(bias_out), VM), (line(ln2_gain), VM), (line(ln2_shift), VM), (cell_len, SM), (line_u, ANY), (w_d, ANY)],
        [pltpu.VMEM((total // BLOCK, BLOCK, total), F32), pltpu.VMEM(half, F32), pltpu.VMEM(half, BF16),
         pltpu.VMEM(half, BF16), *PlaneGather.sems(pieces), *LineGather.sems(pieces),
         dma((2, 2)), dma((2, 2)), dma((2,))],
    )
    wu = g_u.reshape(units, width)
    g_d, hidden, slope, part_d = call(
        functools.partial(k3_kernel, inner, pieces), 2, "hidden_units",
        [(slabs, BF16, ANY), ((total, units), BF16, VM), ((total, units), BF16, VM), ((units, width), BF16, VM)],
        [(normed2, VM), (wu, VM), (b_u, VM), (cot, VM), (line_d, ANY)],
        [*PlaneGather.sems(pieces), dma((1,))],
    )
    wd = g_d.reshape(units, width)
    two = (2, 2, BLOCK, width)
    cells_out, line_gd, part_u, part_o, grad_mid, grad_mixed, sums4, sum_up = call(
        functools.partial(k4_kernel, inner, pieces), 3, "hidden_units_back",
        [((2, local_rows, width), BF16, ANY), (lines, BF16, VM), ((units, width), BF16, VM), ((part, width), BF16, VM),
         (half, F32, VM), ((total, part), BF16, VM), ((8, width), F32, VM), ((1, units), F32, VM)],
        [(hidden, ANY), (slope, VM), (wd, VM), (wu, VM), (cot, VM), (normed2, VM), (middle, VM), (mixed, VM),
         (wa[3 * part :], VM), (line(bias_down), VM), (line(ln2_gain), VM), (part_d.reshape(slabs), VM)],
        [pltpu.VMEM((total, units), BF16), pltpu.VMEM((total, width), BF16), pltpu.VMEM(half, F32),
         pltpu.VMEM(two, BF16), pltpu.VMEM(two, BF16), pltpu.VMEM(half, BF16),
         *PlaneReduce.scratch(pieces, width), dma((3, 2)), dma((3, 2)), dma((1,)), dma((1,)), dma((2,))],
    )
    grads, part_a, line_gu, grad_d, sum_qkv = call(
        functools.partial(k5_kernel, inner, pieces, used), 4, "attend_back",
        [((total, 3 * part), BF16, VM), ((2, OUTER * rows, width), BF16, VM), (lines, BF16, VM),
         ((used, width), F32, VM), ((1, 3 * part), F32, VM)],
        [(qkv, VM), (lse, VM), (grad_mixed, VM), (normed, VM), (part_o, VM), (order_t, VM), (cell_len, SM),
         (part_u.reshape(slabs), VM), (line_gd, VM)],
        [pltpu.VMEM((total // BLOCK, total, BLOCK), F32), pltpu.VMEM((total, part), F32), pltpu.VMEM((total, part), F32),
         pltpu.VMEM((2, 4 * heads * PAD_DIM, width), BF16), pltpu.VMEM((2 * PAD_DIM, total), F32),
         *PlaneReduce.scratch(pieces, width), *LineReduce.scratch(pieces, width)],
    )

    def put_heads(s):
        s = s.reshape(heads, 2, PAD_DIM)[..., :HEAD_DIM].transpose(1, 0, 2)[:, None]
        zero = jnp.zeros_like(s)
        return jnp.where(c == 0, jnp.concatenate([s, zero], 1), jnp.concatenate([zero, s], 1)).reshape(-1)

    def put_hidden(s):
        s = s.reshape(2, 2, 4, rows)[..., :used].transpose(0, 3, 2, 1).reshape(2, 1, -1)
        zero = jnp.zeros_like(s)
        return jnp.where(c == 0, jnp.concatenate([s, zero], 1), jnp.concatenate([zero, s], 1)).reshape(-1)

    none = jnp.zeros((width,), F32)
    small = jnp.concatenate(
        [none, none, put_heads(sum_qkv[0, :part]), put_heads(sum_qkv[0, 2 * part :]), sums4[2], sums4[0], sums4[1],
         put_hidden(sum_up[0]), sums4[3]]
    ).reshape(-1, width)
    small = pad_rows(small, 16)
    grad_in, grad_a, grad_u, small = call(
        functools.partial(k6_kernel, inner, pieces, used), 5, "first_norm_back",
        [((2, local_rows, width), BF16, ANY), ((used, width), F32, VM), ((used, width), F32, VM), (small.shape, F32, VM)],
        [(grads, VM), (wa, VM), (cells, VM), (grad_mid, VM), (line(ln1_gain), VM), (small, VM),
         (part_a.reshape(slabs), VM), (line_gu, VM)],
        [pltpu.VMEM(half, F32), pltpu.VMEM(half, BF16), pltpu.VMEM(half, BF16), pltpu.VMEM(half, BF16),
         pltpu.VMEM(lines, BF16), pltpu.VMEM((6, *small.shape), F32), pltpu.VMEM((5, *small.shape), F32),
         *PlaneReduce.scratch(pieces, width), *LineReduce.scratch(pieces, width), *LineReduce.scratch(pieces, width),
         dma((2,)), dma((2,)), dma((1,)), dma((1,)), dma((1,)), dma((5,)), dma((5,))],
    )
    qkv_rows = shards[0].size // width
    grads = [grad_a[:qkv_rows], grad_a[qkv_rows:], grad_u, grad_d]
    grads = [g.reshape(s.shape) for g, s in zip(grads, shards)]
    if inner > 1:
        grads = [
            lax.psum_scatter(g, "wide", scatter_dimension=1, axis_index_groups=groups, tiled=True)
            for g in grads
        ]
    hid = bias_up.shape[0] // width
    flat = [
        small[0], small[1], small[2:4].reshape(-1), small[4], small[5], small[6],
        small[7 : 7 + hid].reshape(-1), small[7 + hid],
    ]
    return (cells_out[:, None], grad_in[:, None], *grads, *flat)


def solution(mesh):
    cell = P(None, "wide", "narrow", None)
    shard = P("narrow", "wide")
    return jax.shard_map(
        on_device,
        mesh=mesh,
        in_specs=(cell, P(None, "wide"), *[shard] * 4, *[P()] * 8, cell),
        out_specs=(cell, cell, *[shard] * 4, *[P()] * 8),
        check_vma=False,
    )
```

```python
import functools

import jax
import jax.numpy as jnp
import numpy as np
from jax import lax
from jax.experimental import pallas as pl
from jax.experimental.pallas import tpu as pltpu
from jax.sharding import PartitionSpec as P

HEAD_DIM = 56
PAD_DIM = 64
OUTER = 8
NORM_EPS = 1e-05
SCALE = HEAD_DIM ** (-0.5)
SCALE2 = SCALE * 1.4426950408889634
MESH = pl.DeviceIdType.MESH
BF16 = jnp.bfloat16
F32 = jnp.float32
BLOCK = 256
STRIP = 32
VMEM_LIMIT = 63 * 2**20 + 2**19


class Links:
    def __init__(self, inner):
        w = lax.axis_index("wide")
        n = lax.axis_index("narrow")
        outer, wi = w // inner, w % inner
        z, x, y, c = outer // 2, outer % 2, n // 2, n % 2
        self.z, self.x, self.y, self.c, self.n = z, x, y, c, n

        def device(z, x, y, c):
            return ((2 * z + x) * inner + wi, 2 * y + c)

        self.along = [device((z + d) % 4, x, y, c) for d in (1, 2, 3)]
        self.xdev = device(z, 1 - x, y, c)
        self.ydev = device(z, x, 1 - y, c)
        self.cdev = device(z, x, y, 1 - c)
        self.pair = device(z + 1 - 2 * (z % 2), x, y, c)
        self.everyone = [*self.along, self.xdev, self.ydev, self.cdev]
        self.own, self.sib = n, 2 * y + 1 - c
        self.far, self.far_sib = 2 * (1 - y) + c, 2 * (1 - y) + 1 - c

    def back(self, d):
        return (self.z + 4 - d) % 4

    def ahead(self, d):
        return (self.z + d) % 4


def remote(src, dst, send, recv, dev):
    return pltpu.make_async_remote_copy(
        src_ref=src, dst_ref=dst, send_sem=send, recv_sem=recv, device_id=dev, device_id_type=MESH
    )


def greet(devices):
    barrier = pltpu.get_barrier_semaphore()
    for dev in devices:
        pl.semaphore_signal(barrier, inc=1, device_id=dev, device_id_type=MESH)
    pl.semaphore_wait(barrier, len(devices))


dma = pltpu.SemaphoreType.DMA


class SlabGather:
    SEMS = [dma((3,)), dma((3,)), dma((4,)), dma((4,)), dma((1,))]

    def __init__(self, n, own, out, sems):
        self.n, self.own, self.out = n, own, out
        self.zs, self.zr, self.xs, self.xr, self.ls = sems
        self.keep = pltpu.make_async_copy(own, out.at[n.x * 4 + n.z], self.ls.at[0])

    def zcopy(self, d):
        n = self.n
        return remote(self.own, self.out.at[n.x * 4 + n.z], self.zs.at[d - 1], self.zr.at[d - 1], n.along[d - 1])

    def zcame(self, d):
        v = self.out.at[self.n.x * 4 + self.n.back(d)]
        return remote(v, v, self.zs.at[d - 1], self.zr.at[d - 1], self.n.along[d - 1])

    def xcopy(self, d):
        n = self.n
        v = self.out.at[n.x * 4 + n.back(d)]
        return remote(self.own if d == 0 else v, v, self.xs.at[d], self.xr.at[d], n.xdev)

    def xcame(self, d):
        n = self.n
        v = self.out.at[(1 - n.x) * 4 + n.back(d)]
        return remote(v, v, self.xs.at[d], self.xr.at[d], n.xdev)

    def start(self):
        for d in (1, 2, 3):
            self.zcopy(d).start()
        self.xcopy(0).start()
        self.keep.start()

    def cross(self, d):
        self.zcame(d).wait_recv()
        self.xcopy(d).start()

    def wait(self):
        self.keep.wait()
        for d in range(4):
            self.xcame(d).wait_recv()

    def sent(self):
        for d in (1, 2, 3):
            self.zcopy(d).wait_send()
        for d in range(4):
            self.xcopy(d).wait_send()


class CrossReduce:
    @staticmethod
    def scratch(rows, width):
        return [pltpu.VMEM((4, rows, width), BF16), dma((4,)), dma((4,))]

    def __init__(self, n, part, line, scratch):
        self.n, self.part, self.line = n, part, line
        self.rx, self.s, self.q = scratch
        self.rows = line.shape[1]

    def slab(self, x, d):
        rows = self.rows
        return pl.ds(pl.multiple_of((x * 4 + self.n.ahead(d)) * rows, 16), rows)

    def copy(self, d):
        src = self.part.at[self.slab(1 - self.n.x, d)]
        return remote(src, self.rx.at[d], self.s.at[d], self.q.at[d], self.n.xdev)

    def start(self, slots=(1, 2, 3, 0)):
        for d in slots:
            self.copy(d).start()

    def finish(self, d, part=None, x=None):
        part = self.part if part is None else part
        x = self.n.x if x is None else x
        self.copy(d).wait_recv()
        total = part[self.slab(x, d)].astype(F32) + self.rx[d].astype(F32)
        self.line[d] = total.astype(BF16)

    def sent(self):
        for d in range(4):
            self.copy(d).wait_send()


class LineReduce:
    @staticmethod
    def scratch(rows, width):
        return [pltpu.VMEM((3, rows, width), BF16), dma((3,)), dma((3,))]

    def __init__(self, n, line, out, scratch):
        self.n, self.line, self.out = n, line, out
        self.rz, self.s, self.q = scratch

    def copy(self, d):
        return remote(self.line.at[d], self.rz.at[d - 1], self.s.at[d - 1], self.q.at[d - 1], self.n.along[d - 1])

    def start(self, d):
        self.copy(d).start()

    def finish(self, line=None):
        for d in (1, 2, 3):
            self.copy(d).wait_recv()
        total = (self.line[0] if line is None else line).astype(F32)
        for d in range(3):
            total += self.rz[d].astype(F32)
        self.out[...] = total[: self.out.shape[0]]

    def sent(self):
        for d in (1, 2, 3):
            self.copy(d).wait_send()


class BlockGather:
    SEMS = [dma((2, 3)), dma((2, 3))]

    def __init__(self, n, src, dst, sems):
        self.n, self.src, self.dst = n, src, dst
        self.s, self.q = sems

    def rows(self, b, m):
        return self.dst.at[pl.ds(pl.multiple_of((4 * b + m) * BLOCK, BLOCK), BLOCK)]

    def copy(self, b, i):
        n = self.n
        if i == 2:
            v = self.rows(b, n.far)
            return remote(v, v, self.s.at[b, 2], self.q.at[b, 2], n.cdev)
        return remote(self.src(b), self.rows(b, n.own), self.s.at[b, i], self.q.at[b, i], (n.ydev, n.cdev)[i])

    def came(self, b, i):
        n = self.n
        v = self.rows(b, (n.far, n.sib, n.far_sib)[i])
        return remote(v, v, self.s.at[b, i], self.q.at[b, i], (n.ydev, n.cdev, n.cdev)[i])

    def start(self, b):
        self.copy(b, 0).start()
        self.copy(b, 1).start()

    def near(self, b):
        self.came(b, 1).wait_recv()

    def onward(self, b):
        self.came(b, 0).wait_recv()
        self.copy(b, 2).start()

    def wait(self, b):
        self.came(b, 2).wait_recv()

    def sent(self):
        for b in range(2):
            for i in range(3):
                self.copy(b, i).wait_send()


class BlockReduce:
    @staticmethod
    def scratch(width):
        return [pltpu.VMEM((2, 3, BLOCK, width), BF16), pltpu.VMEM((2, 3, BLOCK, width), BF16), dma((2, 3)), dma((2, 3))]

    NEAR, CROSS, OVER = 0, 1, 2

    def __init__(self, n, scratch):
        self.n = n
        self.out, self.got, self.s, self.q = scratch

    def copy(self, b, i):
        n = self.n
        dev = n.ydev if i == self.OVER else n.cdev
        return remote(self.out.at[b, i], self.got.at[b, i], self.s.at[b, i], self.q.at[b, i], dev)

    def put(self, b, i, value):
        self.out[b, i] = value.astype(BF16)
        if i != self.OVER:
            self.copy(b, i).start()

    def hold(self, b):
        self.copy(b, self.CROSS).wait_recv()

        def add(i):
            r = rows_at(i, 2 * STRIP)
            total = self.out[b, self.OVER, r].astype(F32) + self.got[b, self.CROSS, r].astype(F32)
            self.out[b, self.OVER, r] = total.astype(BF16)

        loop(BLOCK // (2 * STRIP), add)

    def over(self, b):
        self.copy(b, self.OVER).start()

    def near(self, b):
        self.copy(b, self.NEAR).wait_recv()

    def wait(self, b):
        self.copy(b, self.OVER).wait_recv()

    def extra(self, b, r):
        return self.got[b, self.NEAR, r].astype(F32) + self.got[b, self.OVER, r].astype(F32)

    def sent(self, over=True):
        for b in range(2):
            for i in range(3 if over else 2):
                self.copy(b, i).wait_send()


class Load:
    def __init__(self, src, buf, sem):
        self.src, self.buf = src, buf
        self.copy = pltpu.make_async_copy(src, buf, sem)
        self.waiting = False

    def start(self):
        self.copy.start()
        self.waiting = True

    def get(self):
        if self.waiting:
            self.copy.wait()
            self.waiting = False
        return self.buf


class Store:
    def __init__(self, dst, buf, sems):
        self.dst, self.buf, self.sems, self.copies = dst, buf, sems, []

    def put(self, start=None, size=None):
        src, dst = self.buf, self.dst
        if size is not None:
            src, dst = src.at[pl.ds(start, size)], dst.at[pl.ds(start, size)]
        copy = pltpu.make_async_copy(src, dst, self.sems.at[len(self.copies)])
        copy.start()
        self.copies.append(copy)

    def wait(self):
        for copy in self.copies:
            copy.wait()


class Steps:
    def __init__(self, steps):
        self.steps = list(steps)

    def __call__(self, count=1):
        for _ in range(count):
            if self.steps:
                self.steps.pop(0)()

    def rest(self):
        self(len(self.steps))


def dot(a, b, dims):
    return lax.dot_general(a, b, (dims, ((), ())), preferred_element_type=F32)


def dot_nn(a, b):
    return dot(a, b, ((1,), (0,)))


def dot_nt(a, b):
    return dot(a, b, ((1,), (1,)))


def dot_tn(a, b):
    return dot(a, b, ((0,), (0,)))


def rows_at(i, size):
    return pl.ds(pl.multiple_of(i * size, size), size)


def loop(count, body):
    def step(i, carry):
        body(i)
        return carry

    lax.fori_loop(0, count, step, 0)


def norm_parts(v):
    center = v - jnp.mean(v, axis=-1, keepdims=True)
    rstd = lax.rsqrt(jnp.mean(center * center, axis=-1, keepdims=True) + NORM_EPS)
    return center * rstd, rstd


def norm_back(e, gain, xhat, rstd):
    eg = e * gain
    return rstd * (
        eg - jnp.mean(eg, axis=-1, keepdims=True) - xhat * jnp.mean(eg * xhat, axis=-1, keepdims=True)
    )


def gelu(u):
    t = jnp.tanh(0.7978845608 * (u + 0.044715 * u * u * u))
    h = 0.5 * u * (1.0 + t)
    d = 0.5 * (1.0 + t) + 0.5 * u * (1.0 - t * t) * 0.7978845608 * (1.0 + 3 * 0.044715 * u * u)
    return h, d


PARTS = 4
CHUNK = 384
WIDE = 128


def head_cols(part, p, h):
    return pl.ds(pl.multiple_of(p * part + h // 2 * 2 * PAD_DIM, 2 * PAD_DIM), 2 * PAD_DIM)


def causal(swap):
    a = lax.broadcasted_iota(jnp.int32, (BLOCK, BLOCK), 0)
    b = lax.broadcasted_iota(jnp.int32, (BLOCK, BLOCK), 1)
    return jnp.where((a <= b) if swap else (b <= a), 0.0, -1e30)


def forward_kernel(inner, heads, *refs):
    it = iter(refs)
    take = lambda n: [next(it) for _ in range(n)]
    wq, wo, wu, wd, x_ref, g_ref, rows_in, bias_qkv, order_q, order_o, lens = take(11)
    out_u, out_d, cot, normed_st, qkv_st, mixed_st, lse_t, wa_st, middle, n2 = take(10)
    gq, go, own, mask, lenrow, lse = take(6)
    q_sems, o_sems, u_sems, d_sems = take(5), take(5), take(5), take(5)
    n1_sems, g_sems, red_s, ls = take(2), take(2), take(4), take(1)[0]
    n = Links(inner)
    normed, qkv, mixed, wa = (st.buf for st in (normed_st, qkv_st, mixed_st, wa_st))
    width = normed.shape[1]
    part = mixed.shape[1]
    greet(n.everyone)
    sq, so = SlabGather(n, wq, gq, q_sems), SlabGather(n, wo, go, o_sems)
    su, sd = SlabGather(n, wu, out_u, u_sems), SlabGather(n, wd, out_d, d_sems)
    sq.start()
    order_q.start()
    order_o.start()
    gain, shift = rows_in[0:1], rows_in[1:2]

    def own_rows(b):
        return pl.ds(pl.multiple_of((4 * b + n.own) * BLOCK, BLOCK), BLOCK)

    ng = BlockGather(n, lambda b: normed.at[own_rows(b)], normed, n1_sems)
    gg = BlockGather(n, lambda b: g_ref.at[b], cot, g_sems)
    for b in range(2):

        def norm(i, b=b):
            xhat, _ = norm_parts(x_ref[b, rows_at(i, 2 * STRIP)].astype(F32))
            at = pl.multiple_of((4 * b + n.own) * BLOCK + i * 2 * STRIP, 2 * STRIP)
            normed[pl.ds(at, 2 * STRIP)] = (xhat * gain + shift).astype(BF16)

        loop(BLOCK // (2 * STRIP), norm)
        ng.start(b)
    for d in (1, 2, 3):
        sq.cross(d)
    so.start()
    su.start()
    sd.start()
    keep_g = [pltpu.make_async_copy(g_ref.at[b], cot.at[own_rows(b)], ls.at[b]) for b in range(2)]
    for b in range(2):
        gg.start(b)
        keep_g[b].start()
    mask[...] = causal(False)
    key = lax.broadcasted_iota(jnp.int32, (8, 4 * BLOCK), 1)
    for b in range(2):
        lenrow[b] = jnp.where(key < lens[b], 0.0, -1e30)
    lse[...] = jnp.zeros_like(lse)
    mixed[...] = jnp.zeros_like(mixed)
    ng.onward(0)
    order_v = order_q.get()
    sq.wait()
    group = wa.shape[0] // 4
    slabs = jnp.concatenate([gq[s] for s in range(8)], axis=0)
    for p in range(3):
        wa[p * group : (p + 1) * group] = dot_nn(order_v[p * group : (p + 1) * group], slabs).astype(BF16)

    steps = Steps(
        [functools.partial(so.cross, d) for d in (1, 2, 3)]
        + [functools.partial(su.cross, d) for d in (1, 2, 3)]
        + [functools.partial(sd.cross, d) for d in (1, 2, 3)]
    )
    lane = lax.broadcasted_iota(jnp.int32, (BLOCK, 2 * PAD_DIM), 1)

    def project(b):
        def one(t):
            r = rows_at(4 * b + t, BLOCK)
            a = normed[r]
            for p in range(3):
                cols = slice(p * part, (p + 1) * part)
                qkv[r, cols] = (dot_nt(a, wa[cols]) + bias_qkv[:, cols]).astype(BF16)

        loop(4, one)

    def attend(b, blocks):
        base = 4 * b * BLOCK

        def head(h):
            half = h % 2
            here = lane // PAD_DIM == half
            for i in blocks:
                r = slice(base + i * BLOCK, base + (i + 1) * BLOCK)
                keys = slice(base, base + (i + 1) * BLOCK)
                end = (i + 1) * BLOCK
                q = qkv[r, head_cols(part, 0, h)]
                k, v = qkv[keys, head_cols(part, 1, h)], qkv[keys, head_cols(part, 2, h)]
                s = dot_nt(jnp.where(here, q, jnp.zeros_like(q)), k) * SCALE2 + lenrow[b, 0:1, :end]
                diag = s[:, i * BLOCK :] + mask[...]
                s = jnp.concatenate([s[:, : i * BLOCK], diag], axis=1) if i else diag
                m = jnp.max(s, axis=-1, keepdims=True)
                e = jnp.exp2(s - m)
                t = jnp.sum(e, axis=-1, keepdims=True)
                p = (e * (1.0 / t)).astype(BF16)
                o = dot_nn(p, v).astype(BF16)
                cols = head_cols(part, 0, h)
                mixed[r, cols] = jnp.where(here, o, mixed[r, cols])
                lse[r] = jnp.where(lane == h, m + jnp.log2(t), lse[r])

        loop(heads, head)

    red = BlockReduce(n, red_s)

    def out_project(b):
        w = wa.at[pl.ds(3 * group, group)]

        def rows(m):
            return mixed[pl.ds(pl.multiple_of((4 * b + m) * BLOCK, BLOCK), BLOCK)]

        red.put(b, red.CROSS, dot_nn(rows(n.far_sib), w[...]))
        red.put(b, red.OVER, dot_nn(rows(n.far), w[...]))
        red.hold(b)
        red.over(b)
        red.put(b, red.NEAR, dot_nn(rows(n.sib), w[...]))
        own[b] = dot_nn(rows(n.own), w[...])

    def second_norm(b):
        red.near(b)
        red.wait(b)
        bias_out, gain2, shift2 = rows_in[2:3], rows_in[3:4], rows_in[4:5]

        def finish(i):
            r = rows_at(i, STRIP)
            mid = x_ref[b, r].astype(F32) + own[b, r] + red.extra(b, r) + bias_out
            middle[b, r] = mid
            xhat, _ = norm_parts(mid)
            n2[b, r] = (xhat * gain2 + shift2).astype(BF16)

        loop(BLOCK // STRIP, finish)

    ng.near(0)
    ng.wait(0)
    project(0)
    steps(3)
    attend(0, (0, 3))
    ng.onward(1)
    attend(0, (1, 2))
    so.wait()
    ordo = order_o.get()
    slabs_o = jnp.concatenate([go[s] for s in range(8)], axis=0)
    wa[3 * group :] = dot_nn(ordo[...], slabs_o).astype(BF16)
    wa_st.put()
    out_project(0)
    ng.near(1)
    ng.wait(1)
    normed_st.put()
    project(1)
    qkv_st.put()
    gg.onward(0)
    steps(3)
    attend(1, (0, 3))
    gg.onward(1)
    attend(1, (1, 2))
    mixed_st.put()
    lse_t[...] = jnp.transpose(lse[...])[0:8]
    out_project(1)
    steps.rest()
    second_norm(0)
    second_norm(1)
    su.wait()
    sd.wait()
    for b in range(2):
        gg.near(b)
        gg.wait(b)
        keep_g[b].wait()
    for g in (sq, so, su, sd, ng, gg, red):
        g.sent()
    for st in (normed_st, qkv_st, mixed_st, wa_st):
        st.wait()


def hidden_kernel(inner, *refs):
    it = iter(refs)
    take = lambda n: [next(it) for _ in range(n)]
    n2_own, wu, wd, bias_up, cot, middle, rows_in = take(7)
    part_st, lined_st, gm_st, att, far_out, part_out, sums, sum_up = take(8)
    n2, hidden, grad_up, own, part_d = take(5)
    n2_sems, red_s, out_s, rd, ls = take(2), take(4), take(4), take(3), take(1)[0]
    n = Links(inner)
    greet([n.xdev, n.ydev, n.cdev])
    total, width = n2.shape
    units = hidden.shape[1]
    gather = BlockGather(n, lambda b: n2_own.at[b], n2, n2_sems)
    for b in range(2):
        gather.start(b)
    for ld in (wu, wd, cot, middle):
        ld.start()

    def block(b, m):
        return pl.ds(pl.multiple_of((4 * b + m) * BLOCK, BLOCK), BLOCK)

    for b in range(2):
        cp = pltpu.make_async_copy(n2_own.at[b], n2.at[block(b, n.own)], ls.at[b])
        cp.start()
        cp.wait()
    red, out = BlockReduce(n, red_s), BlockReduce(n, out_s)
    sum_up[...] = jnp.zeros_like(sum_up)
    sums[...] = jnp.zeros_like(sums)
    wu_v, wd_v, cot_v = wu.get(), wd.get(), cot.get()

    def units_of(r):
        def one(q):
            cols = rows_at(q, CHUNK)
            h, d = gelu(dot_nt(n2[r], wu_v[cols]) + bias_up[:, cols])
            hidden[r, cols] = h.astype(BF16)
            g = (dot_nt(cot_v[r], wd_v[cols]) * d).astype(BF16)
            grad_up[r, cols] = g
            sum_up[:, cols] += jnp.sum(g.astype(F32), axis=0, keepdims=True)

        loop(units // CHUNK, one)
        return dot_nn(hidden[r], wd_v[...]), dot_nn(grad_up[r], wu_v[...])

    bias_down, gain = rows_in[5:6], rows_in[3:4]
    middle_v = middle.get()

    def mine(b):
        o, g = units_of(block(b, n.own))
        own[b] = g
        part_out[b] = middle_v[b] + o + bias_down

    loop(2, mine)
    for b in range(2):
        gather.near(b)
        o, g = units_of(block(b, n.sib))
        red.put(b, red.NEAR, g)
        out.put(b, out.NEAR, o)
    for b in range(2):
        gather.onward(b)
        o, g = units_of(block(b, n.far))
        red.put(b, red.OVER, g)
        out.put(b, out.OVER, o)
        gather.wait(b)
        o, g = units_of(block(b, n.far_sib))
        red.put(b, red.CROSS, g)
        out.put(b, out.CROSS, o)
        red.hold(b)
        red.over(b)
        out.hold(b)
        far_out[b] = out.out[b, out.OVER]
    down = CrossReduce(n, part_d, lined_st.buf, rd)

    def grad_down(q):
        cols = rows_at(q, WIDE)
        part_d[cols] = dot_tn(hidden[:, cols], cot_v[...]).astype(BF16)

    loop(units // WIDE, grad_down)
    down.start()
    grad_mid = gm_st.buf
    part_u = part_st.buf

    def grad_units(first, count):
        def one(q):
            cols = rows_at(first + q, WIDE)
            part_u[cols] = dot_tn(grad_up[:, cols], n2[...]).astype(BF16)

        loop(count, one)

    def norm_back_of(b):
        red.near(b)
        red.wait(b)
        out.near(b)

        def finish(i):
            r = rows_at(i, STRIP)
            at = pl.ds(pl.multiple_of((4 * b + n.own) * BLOCK + i * STRIP, STRIP), STRIP)
            e = own[b, r] + red.extra(b, r)
            xhat, rstd = norm_parts(middle_v[b, r])
            top = cot_v[at].astype(F32)
            g = top + norm_back(e, gain, xhat, rstd)
            grad_mid[b, r] = g
            low = g.astype(BF16)
            att[b, r] = low
            part_out[b, r] += out.got[b, out.NEAR, r].astype(F32)
            sums[0:1] += jnp.sum(e * xhat, axis=0, keepdims=True)
            sums[1:2] += jnp.sum(e, axis=0, keepdims=True)
            sums[2:3] += jnp.sum(low.astype(F32), axis=0, keepdims=True)
            sums[3:4] += jnp.sum(top, axis=0, keepdims=True)

        loop(BLOCK // STRIP, finish)

    count = units // WIDE
    norm_back_of(0)
    grad_units(0, count)
    part_st.put()
    norm_back_of(1)
    gm_st.put()
    for d in (1, 2, 3, 0):
        down.finish(d)
    lined_st.put()
    gather.sent()
    red.sent()
    out.sent(False)
    down.sent()
    for st in (part_st, lined_st, gm_st):
        st.wait()


def backward_kernel(inner, heads, *refs):
    it = iter(refs)
    take = lambda n: [next(it) for _ in range(n)]
    att_own, gm, wa, qkv, lse_t, mixed, normed, x_ref, rows_in, order_qt, order_ot, lens = take(12)
    part_u, line_d, far_out, part_out, sums_in, sum_up = take(6)
    cells_out, grad_in, grad_q, grad_o, grad_u, grad_d, small_out = take(7)
    att, gmix, gk, gv, grads, part_q, part_o, part_own, line0, mask, lencol, own, got_out, acc, inbox = take(15)
    line_u, line_q, line_o = take(3)
    att_sems, red_s, ru, rq, ro = take(2), take(4), take(3), take(3), take(3)
    zd, zu, zq, zo = take(3), take(3), take(3), take(3)
    ys, yr, ls, sa, qa = take(5)
    n = Links(inner)
    greet(n.everyone)
    total, width = att.shape
    part = gmix.shape[1]


    def block(b, m):
        return pl.ds(pl.multiple_of((4 * b + m) * BLOCK, BLOCK), BLOCK)

    gather = BlockGather(n, lambda b: att_own.at[b], att, att_sems)
    get_att = [pltpu.make_async_copy(att_own.at[b], att.at[block(b, n.own)], ls.at[b]) for b in range(2)]
    for b in range(2):
        gather.start(b)
        get_att[b].start()

    def out_copy(b):
        return remote(far_out.at[b], got_out.at[b], ys.at[b], yr.at[b], n.ydev)

    for b in range(2):
        out_copy(b).start()
    cu, cq, co = CrossReduce(n, part_u, line_u, ru), CrossReduce(n, part_q, line_q, rq), CrossReduce(n, part_o, line_o, ro)
    lind, linu = LineReduce(n, line_d, grad_d, zd), LineReduce(n, line_u, grad_u, zu)
    linq, lino = LineReduce(n, line_q, grad_q, zq), LineReduce(n, line_o, grad_o, zo)
    cu.start()
    for d in (1, 2, 3):
        lind.start(d)
    for ld in (wa, qkv, mixed, order_ot, order_qt, gm):
        ld.start()
    rows_u = line_u.shape[1]
    mine = pl.ds(pl.multiple_of(n.x * 4 * rows_u, 16), 4 * rows_u)
    get_own = pltpu.make_async_copy(part_u.at[mine], part_own, ls.at[2])
    get_line = pltpu.make_async_copy(line_d.at[0], line0, ls.at[3])
    get_own.start()
    get_line.start()

    mask[...] = causal(True)
    key = lax.broadcasted_iota(jnp.int32, (4 * BLOCK, BLOCK), 0)
    lane = lax.broadcasted_iota(jnp.int32, (BLOCK, 2 * PAD_DIM), 1)
    wa_v, qkv_v = wa.get(), qkv.get()
    group = wa_v.shape[0] // 4
    gmix[...] = jnp.zeros_like(gmix)
    grads[...] = jnp.zeros_like(grads)

    def to_heads(b):
        def one(t):
            r = rows_at(4 * b + t, BLOCK)
            gmix[r] = dot_nt(att[r], wa_v[3 * group :]).astype(BF16)

        loop(4, one)

    def attend(b, blocks):
        base = 4 * b * BLOCK

        def head(h):
            half = h % 2
            here = lane // PAD_DIM == half
            for i in blocks:
                r = slice(base + i * BLOCK, base + (i + 1) * BLOCK)
                keys = slice(base, base + (i + 1) * BLOCK)
                end = (i + 1) * BLOCK
                key_here = lax.broadcasted_iota(jnp.int32, (end, 2 * PAD_DIM), 1) // PAD_DIM == half
                cols = head_cols(part, 0, h)
                q, k, v = (qkv_v[rr, head_cols(part, p, h)] for p, rr in ((0, r), (1, keys), (2, keys)))
                g = gmix[r, cols]
                zero = jnp.zeros_like(q)
                q, g = jnp.where(here, q, zero), jnp.where(here, g, zero)
                s = dot_nt(k, q) * SCALE2 + lencol[:end]
                diag = s[i * BLOCK :] + mask[...]
                s = jnp.concatenate([s[: i * BLOCK], diag], axis=0) if i else diag
                p = jnp.exp2(s - lse_t[pl.ds(h, 1), r])
                gp = dot_nt(v, g)
                inner_sum = jnp.sum(p * gp, axis=0, keepdims=True)
                ds = (p * (gp - inner_sum)).astype(BF16)
                gv[:end, cols] += dot_nn(p.astype(BF16), g)
                gk[:end, cols] += dot_nn(ds, q)
                gq = (dot_tn(ds, k) * SCALE).astype(BF16)
                grads[r, cols] = jnp.where(here, gq, grads[r, cols])

        loop(heads, head)

    def settle(b):
        def one(t):
            r, rr = rows_at(t, BLOCK), rows_at(4 * b + t, BLOCK)
            grads[rr, part : 2 * part] = (gk[r] * SCALE).astype(BF16)
            grads[rr, 2 * part :] = gv[r].astype(BF16)

        loop(4, one)

    red = BlockReduce(n, red_s)

    def project_back(b):
        w = wa_v.at[pl.ds(0, 3 * group)]

        def rows(m):
            return grads[block(b, m)]

        red.put(b, red.CROSS, dot_nn(rows(n.far_sib), w[...]))
        red.put(b, red.OVER, dot_nn(rows(n.far), w[...]))
        red.hold(b)
        red.over(b)
        red.put(b, red.NEAR, dot_nn(rows(n.sib), w[...]))
        own[b] = dot_nn(rows(n.own), w[...])

    gain = rows_in[0:1]
    gm_v = gm.get()

    def first_norm(b):
        red.near(b)
        red.wait(b)

        def finish(i):
            r = rows_at(i, STRIP)
            e = own[b, r] + red.extra(b, r)
            xhat, rstd = norm_parts(x_ref[b, r].astype(F32))
            grad_in[b, r] = (gm_v[b, r] + norm_back(e, gain, xhat, rstd)).astype(BF16)
            acc[0, 0:1, :width] += jnp.sum(e * xhat, axis=0, keepdims=True)
            acc[0, 1:2, :width] += jnp.sum(e, axis=0, keepdims=True)

        loop(BLOCK // STRIP, finish)

    put_out = [pltpu.make_async_copy(got_out.at[b], cells_out.at[b], ls.at[4 + b]) for b in range(2)]

    def output(b):
        out_copy(b).wait_recv()

        def finish(i):
            r = rows_at(i, 2 * STRIP)
            got_out[b, r] = (part_out[b, r] + got_out[b, r].astype(F32)).astype(BF16)

        loop(BLOCK // (2 * STRIP), finish)
        put_out[b].start()

    acc[0] = jnp.zeros_like(acc[0])
    acc[0, 2:3, :width] = sums_in[2:3]
    acc[0, 3:4, :width] = sums_in[0:1]
    acc[0, 4:5, :width] = sums_in[1:2]
    acc[0, 5:6, :width] = sums_in[3:4]
    acc[0, pl.ds(12 + n.n, 1)] = sum_up[...]

    def lengths_of(b):
        lencol[...] = jnp.where(key < lens[b], 0.0, -1e30)
        gk[...] = jnp.zeros_like(gk)
        gv[...] = jnp.zeros_like(gv)

    for cp in get_att:
        cp.wait()
    lengths_of(0)
    gather.near(0)
    gather.onward(0)
    gather.wait(0)
    to_heads(0)
    attend(0, (0, 3))
    gather.near(1)
    gather.onward(1)
    gather.wait(1)
    to_heads(1)
    mixed_v, ordo = mixed.get(), order_ot.get()
    stack_o = dot_tn(mixed_v[...], att[...]).astype(BF16)
    part_o[...] = dot_nn(ordo[...], stack_o).astype(BF16)
    co.start()
    gather.sent()
    normed.start()
    attend(0, (1, 2))
    settle(0)
    project_back(0)
    get_own.wait()
    for d in (1, 2, 3, 0):
        cu.finish(d, part_own, 0)
        if d:
            linu.start(d)
    get_line.wait()
    lind.finish(line0[...])
    lengths_of(1)
    attend(1, (0, 3))
    output(0)
    output(1)
    for d in (1, 2, 3, 0):
        co.finish(d)
        if d:
            lino.start(d)
    attend(1, (1, 2))
    settle(1)
    project_back(1)
    linu.finish()
    lino.finish()
    normed_v, oq = normed.get(), order_qt.get()
    def grad_proj(q):
        cols = rows_at(q, WIDE)
        qkv_v[cols, :width] = dot_tn(grads[:, cols], normed_v[...]).astype(BF16)

    loop(3 * part // WIDE, grad_proj)
    rows_q = line_q.shape[1]

    def reorder(x):
        at = pl.ds(pl.multiple_of(x * 4 * rows_q, 16), 4 * rows_q)
        part_q[at] = dot_nn(oq[at], qkv_v[: 3 * part, :width]).astype(BF16)

    reorder(1 - n.x)
    cq.start()
    reorder(n.x)

    def sum_rows(t):
        acc[0, pl.ds(8 + n.n, 1)] += jnp.sum(grads[rows_at(t, BLOCK)].astype(F32), axis=0, keepdims=True)

    loop(total // BLOCK, sum_rows)
    first_norm(0)
    first_norm(1)
    peers = [n.cdev, n.xdev, n.ydev, n.pair, n.along[1]]

    def small_copy(i):
        return remote(acc.at[i], inbox.at[i], sa.at[i], qa.at[i], peers[i])

    def small_step(i):
        if i > 0:
            small_copy(i - 1).wait_recv()
            acc[i] = acc[i - 1] + inbox[i - 1]
        if i < 5:
            small_copy(i).start()

    small_step(0)
    for d in (1, 2, 3, 0):
        cq.finish(d)
        if d:
            linq.start(d)
        small_step(4 if d == 0 else d)
    small_step(5)
    small_out[...] = acc[5]
    linq.finish()
    for b in range(2):
        out_copy(b).wait_send()
        put_out[b].wait()
    for i in range(5):
        small_copy(i).wait_send()
    for g in (red, cu, cq, co, lind, linu, linq, lino):
        g.sent()


ANY = pl.BlockSpec(memory_space=pl.ANY)
VM = pl.BlockSpec(memory_space=pltpu.VMEM)
SM = pl.BlockSpec(memory_space=pltpu.SMEM)
ASYNC = "async"


def call(kernel, ident, name, outs, ins, scratch, share=None):
    share = share or {}
    lazy_in = [i for i, (_, s) in enumerate(ins) if s is ASYNC]
    lazy_out = [i for i, (_, _, s) in enumerate(outs) if s is ASYNC]
    extra = [pltpu.VMEM(ins[i][0].shape, ins[i][0].dtype) for i in lazy_in if i not in share]
    extra += [pltpu.VMEM(outs[i][0], outs[i][1]) for i in lazy_out]
    extra += [dma((max(1, len(lazy_in)),)), dma((max(1, len(lazy_out)), PARTS))]

    def body(*refs):
        refs = list(refs)
        bufs = refs[len(refs) - len(extra) :]
        refs = refs[: len(refs) - len(extra)]
        in_sems, out_sems = bufs[-2:]
        bufs = iter(bufs)
        for b, i in enumerate(lazy_in):
            buf = refs[len(ins) + len(outs) + share[i]] if i in share else next(bufs)
            refs[i] = Load(refs[i], buf, in_sems.at[b])
        for b, i in enumerate(lazy_out):
            at = len(ins) + i
            refs[at] = Store(refs[at], next(bufs), out_sems.at[b])
        kernel(*refs)

    return pl.pallas_call(
        body,
        out_shape=[jax.ShapeDtypeStruct(s, d) for s, d, _ in outs],
        in_specs=[ANY if s is ASYNC else s for _, s in ins],
        out_specs=[ANY if s is ASYNC else s for _, _, s in outs],
        scratch_shapes=[*scratch, *extra],
        compiler_params=pltpu.CompilerParams(
            collective_id=ident, has_side_effects=True, vmem_limit_bytes=VMEM_LIMIT
        ),
        name=name,
    )(*[a for a, _ in ins])


def order_matrix(rows, heads, parts, wide):
    m = np.zeros((parts * wide, OUTER * rows), np.float32)
    each = HEAD_DIM // OUTER
    for x in range(2):
        for z in range(4):
            w = 2 * z + x
            for g in range(parts * heads):
                part, head = g % parts, g // parts
                for e in range(each):
                    m[part * wide + head * PAD_DIM + w * each + e, (x * 4 + z) * rows + g * each + e] = 1
    return m


def fit(a):
    return jnp.pad(a, ((0, -a.shape[0] % 16), (0, 0)))


def on_device(
    cells_in, lengths, w_qkv, w_out, w_up, w_down, ln1_gain, ln1_shift, bias_qv, bias_out,
    ln2_gain, ln2_shift, bias_up, bias_down, cotangent,
):
    wide = lax.axis_size("wide")
    inner = wide // OUTER
    shards = [w_qkv, w_out, w_up, w_down]
    if inner > 1:
        groups = [[o * inner + i for i in range(inner)] for o in range(OUTER)]
        shards = [
            lax.all_gather(s, "wide", axis=1, tiled=True, axis_index_groups=groups) for s in shards
        ]
    width = cells_in.shape[3]
    total = 8 * BLOCK
    heads = width // HEAD_DIM // 4
    part = -(-heads // 2) * 2 * PAD_DIM
    n = lax.axis_index("narrow")
    w_q, w_o, w_u, w_d = (fit(s.reshape(-1, width)) for s in shards)
    used = [s.size // width for s in shards]
    rows_q, rows_o, rows = w_q.shape[0], w_o.shape[0], w_u.shape[0]
    units = OUTER * rows
    order_q, order_o = order_matrix(rows_q, heads, 3, part), order_matrix(rows_o, heads, 1, part)

    def constant(a):
        return jnp.asarray(np.ascontiguousarray(a), BF16)

    rows_in = jnp.stack([ln1_gain, ln1_shift, bias_out, ln2_gain, ln2_shift, bias_down])
    b_qv = lax.dynamic_index_in_dim(bias_qv.reshape(2, 4, heads, HEAD_DIM), n, axis=1, keepdims=False)
    b_qv = jnp.pad(b_qv, ((0, 0), (0, 0), (0, PAD_DIM - HEAD_DIM))).reshape(2, heads * PAD_DIM)
    b_qv = jnp.pad(b_qv, ((0, 0), (0, part - heads * PAD_DIM)))
    bias_qkv = jnp.stack([b_qv[0], jnp.zeros_like(b_qv[0]), b_qv[1]]).reshape(1, -1)
    b_u = lax.dynamic_index_in_dim(bias_up.reshape(4, used[2], 4, 2), n, axis=0, keepdims=False).transpose(2, 1, 0)
    b_u = jnp.pad(b_u, ((0, 0), (0, 0), (0, rows - used[2]))).reshape(1, -1)
    lens = lengths[:, 0]
    cells, cot_own = cells_in[:, 0], cotangent[:, 0]

    own2 = (2, BLOCK, width)
    vmem = pltpu.VMEM
    g_u, g_d, cot, normed, qkv, mixed, lse, wa, middle, n2 = call(
        functools.partial(forward_kernel, inner, heads), 0, "forward",
        [((OUTER, rows, width), BF16, ANY), ((OUTER, rows, width), BF16, ANY), ((total, width), BF16, ANY),
         ((total, width), BF16, ASYNC), ((total, 3 * part), BF16, ASYNC), ((total, part), BF16, ASYNC),
         ((8, total), F32, VM), ((4 * part, width), BF16, ASYNC), (own2, F32, VM), (own2, BF16, VM)],
        [(w_q, VM), (w_o, VM), (w_u, VM), (w_d, VM), (cells, VM), (cot_own, VM), (rows_in, VM), (bias_qkv, VM),
         (constant(order_q), ASYNC), (constant(order_o), ASYNC), (lens, SM)],
        [vmem((OUTER, rows_q, width), BF16), vmem((OUTER, rows_o, width), BF16), vmem(own2, F32),
         vmem((BLOCK, BLOCK), F32), vmem((2, 8, 4 * BLOCK), F32), vmem((total, 2 * PAD_DIM), F32),
         *SlabGather.SEMS * 4, *BlockGather.SEMS * 2, *BlockReduce.scratch(width), dma((2,))],
    )
    part_u, line_d, grad_mid, att, far_out, part_out, sums, sum_up = call(
        functools.partial(hidden_kernel, inner), 1, "hidden_units",
        [((units, width), BF16, ASYNC), ((4, rows, width), BF16, ASYNC), (own2, F32, ASYNC), (own2, BF16, VM),
         (own2, BF16, VM), (own2, F32, VM), ((8, width), F32, VM), ((1, units), F32, VM)],
        [(n2, VM), (g_u.reshape(units, width), ASYNC), (g_d.reshape(units, width), ASYNC), (b_u, VM), (cot, ASYNC),
         (middle, ASYNC), (rows_in, VM)],
        [vmem((total, width), BF16), vmem((total, units), BF16), vmem((total, units), BF16), vmem(own2, F32),
         vmem((units, width), BF16),
         *BlockGather.SEMS, *BlockReduce.scratch(width), *BlockReduce.scratch(width), *CrossReduce.scratch(rows, width),
         dma((2,))],
    )
    small_shape = (16, units)
    cells_out, grad_in, grad_q, grad_o, grad_u, grad_d, small = call(
        functools.partial(backward_kernel, inner, heads), 2, "backward",
        [(own2, BF16, ANY), (own2, BF16, VM), ((used[0], width), F32, VM), ((used[1], width), F32, VM),
         ((used[2], width), F32, VM), ((used[3], width), F32, VM), (small_shape, F32, VM)],
        [(att, ANY), (grad_mid, ASYNC), (wa, ASYNC), (qkv, ASYNC), (lse, VM), (mixed, ASYNC), (normed, ASYNC),
         (cells, VM), (rows_in, VM), (constant(order_q.T), ASYNC), (constant(order_o.T), ASYNC), (lens, SM),
         (part_u, ANY), (line_d, ANY), (far_out, ANY), (part_out, VM), (sums, VM), (sum_up, VM)],
        [vmem((total, width), BF16), vmem((total, part), BF16), vmem((total // 2, part), F32), vmem((total // 2, part), F32),
         vmem((total, 3 * part), BF16), vmem((OUTER * rows_q, width), BF16), vmem((OUTER * rows_o, width), BF16),
         vmem((4 * rows, width), BF16), vmem((rows, width), BF16), vmem((BLOCK, BLOCK), F32),
         vmem((4 * BLOCK, BLOCK), F32), vmem(own2, F32),
         vmem(own2, BF16), vmem((6, *small_shape), F32), vmem((5, *small_shape), F32),
         vmem((4, rows, width), BF16), vmem((4, rows_q, width), BF16), vmem((4, rows_o, width), BF16),
         *BlockGather.SEMS, *BlockReduce.scratch(width), *CrossReduce.scratch(rows, width),
         *CrossReduce.scratch(rows_q, width), *CrossReduce.scratch(rows_o, width),
         *LineReduce.scratch(rows, width), *LineReduce.scratch(rows, width), *LineReduce.scratch(rows_q, width),
         *LineReduce.scratch(rows_o, width), dma((2,)), dma((2,)), dma((6,)), dma((5,)), dma((5,))],
        share={6: 0},
    )
    grads = [g.reshape(s.shape) for g, s in zip((grad_q, grad_o, grad_u, grad_d), shards)]
    if inner > 1:
        grads = [
            lax.psum_scatter(g, "wide", scatter_dimension=1, axis_index_groups=groups, tiled=True)
            for g in grads
        ]
    sum_qkv = small[8:12].reshape(4, 3, part)[:, :, : heads * PAD_DIM].reshape(4, 3, heads, PAD_DIM)[..., :HEAD_DIM]
    grad_b = jnp.concatenate([sum_qkv[:, 0].reshape(-1), sum_qkv[:, 2].reshape(-1)])
    grad_bu = small[12:16].reshape(4, 2, 4, rows)[..., : used[2]].transpose(0, 3, 2, 1).reshape(-1)
    flat = [small[i, :width] for i in range(6)]
    return (
        cells_out[:, None], grad_in[:, None], *grads, flat[0], flat[1], grad_b, flat[2], flat[3], flat[4], grad_bu, flat[5],
    )


def solution(mesh):
    cell = P(None, "wide", "narrow", None)
    shard = P("narrow", "wide")
    return jax.shard_map(
        on_device,
        mesh=mesh,
        in_specs=(cell, P(None, "wide"), *[shard] * 4, *[P()] * 8, cell),
        out_specs=(cell, cell, *[shard] * 4, *[P()] * 8),
        check_vma=False,
    )
```

```python
import functools

import jax
import jax.numpy as jnp
import numpy as np
from jax import lax
from jax.experimental import pallas as pl
from jax.experimental.pallas import tpu as pltpu
from jax.sharding import PartitionSpec as P

HEAD_DIM = 56
PAD_DIM = 64
OUTER = 8
NORM_EPS = 1e-05
SCALE = HEAD_DIM ** (-0.5)
SCALE2 = SCALE * 1.4426950408889634
MESH = pl.DeviceIdType.MESH
BF16 = jnp.bfloat16
F32 = jnp.float32
BLOCK = 256
STRIP = 32
VMEM_LIMIT = 63 * 2**20 + 2**19


class Links:
    def __init__(self, inner):
        w = lax.axis_index("wide")
        n = lax.axis_index("narrow")
        outer, wi = w // inner, w % inner
        z, x, y, c = outer // 2, outer % 2, n // 2, n % 2
        self.z, self.x, self.y, self.c, self.n = z, x, y, c, n

        def device(z, x, y, c):
            return ((2 * z + x) * inner + wi, 2 * y + c)

        self.along = [device((z + d) % 4, x, y, c) for d in (1, 2, 3)]
        self.xdev = device(z, 1 - x, y, c)
        self.ydev = device(z, x, 1 - y, c)
        self.cdev = device(z, x, y, 1 - c)
        self.pair = device(z + 1 - 2 * (z % 2), x, y, c)
        self.everyone = [*self.along, self.xdev, self.ydev, self.cdev]
        self.own, self.sib = n, 2 * y + 1 - c
        self.far, self.far_sib = 2 * (1 - y) + c, 2 * (1 - y) + 1 - c

    def back(self, d):
        return (self.z + 4 - d) % 4

    def ahead(self, d):
        return (self.z + d) % 4


def remote(src, dst, send, recv, dev):
    return pltpu.make_async_remote_copy(
        src_ref=src, dst_ref=dst, send_sem=send, recv_sem=recv, device_id=dev, device_id_type=MESH
    )


def greet(devices):
    barrier = pltpu.get_barrier_semaphore()
    for dev in devices:
        pl.semaphore_signal(barrier, inc=1, device_id=dev, device_id_type=MESH)
    pl.semaphore_wait(barrier, len(devices))


dma = pltpu.SemaphoreType.DMA


class SlabGather:
    SEMS = [dma((3,)), dma((3,)), dma((4,)), dma((4,)), dma((1,))]

    def __init__(self, n, own, out, sems):
        self.n, self.own, self.out = n, own, out
        self.zs, self.zr, self.xs, self.xr, self.ls = sems
        self.keep = pltpu.make_async_copy(own, out.at[n.x * 4 + n.z], self.ls.at[0])

    def zcopy(self, d):
        n = self.n
        return remote(self.own, self.out.at[n.x * 4 + n.z], self.zs.at[d - 1], self.zr.at[d - 1], n.along[d - 1])

    def zcame(self, d):
        v = self.out.at[self.n.x * 4 + self.n.back(d)]
        return remote(v, v, self.zs.at[d - 1], self.zr.at[d - 1], self.n.along[d - 1])

    def xcopy(self, d):
        n = self.n
        v = self.out.at[n.x * 4 + n.back(d)]
        return remote(self.own if d == 0 else v, v, self.xs.at[d], self.xr.at[d], n.xdev)

    def xcame(self, d):
        n = self.n
        v = self.out.at[(1 - n.x) * 4 + n.back(d)]
        return remote(v, v, self.xs.at[d], self.xr.at[d], n.xdev)

    def start(self):
        for d in (1, 2, 3):
            self.zcopy(d).start()
        self.xcopy(0).start()
        self.keep.start()

    def cross(self, d):
        self.zcame(d).wait_recv()
        self.xcopy(d).start()

    def wait(self):
        self.keep.wait()
        for d in range(4):
            self.xcame(d).wait_recv()

    def sent(self):
        for d in (1, 2, 3):
            self.zcopy(d).wait_send()
        for d in range(4):
            self.xcopy(d).wait_send()


class LineGather:
    SEMS = [dma((3,)), dma((3,)), dma((1,))]

    def __init__(self, n, own, out, sems):
        self.n, self.own, self.out = n, own, out
        self.zs, self.zr, self.ls = sems
        self.keep = pltpu.make_async_copy(own, out.at[n.z], self.ls.at[0])

    def copy(self, d):
        n = self.n
        return remote(self.own, self.out.at[n.z], self.zs.at[d - 1], self.zr.at[d - 1], n.along[d - 1])

    def start(self):
        for d in (1, 2, 3):
            self.copy(d).start()
        self.keep.start()

    def wait(self):
        self.keep.wait()
        for d in (1, 2, 3):
            v = self.out.at[self.n.back(d)]
            remote(v, v, self.zs.at[d - 1], self.zr.at[d - 1], self.n.along[d - 1]).wait_recv()

    def sent(self):
        for d in (1, 2, 3):
            self.copy(d).wait_send()


class CrossGather:
    SEMS = [dma((4,)), dma((4,)), dma((4,))]

    def __init__(self, n, line, out, sems):
        self.n, self.line, self.out = n, line, out
        self.s, self.q, self.ls = sems
        self.size = line.shape[1]

    def slab(self, x, j):
        return self.out.at[pl.ds(pl.multiple_of((x * 4 + j) * self.size, 16), self.size)]

    def copy(self, j):
        return remote(self.line.at[j], self.slab(self.n.x, j), self.s.at[j], self.q.at[j], self.n.xdev)

    def keep(self, j):
        return pltpu.make_async_copy(self.line.at[j], self.slab(self.n.x, j), self.ls.at[j])

    def start(self):
        for j in range(4):
            self.copy(j).start()
            self.keep(j).start()

    def wait(self):
        for j in range(4):
            self.keep(j).wait()
            v = self.slab(1 - self.n.x, j)
            remote(v, v, self.s.at[j], self.q.at[j], self.n.xdev).wait_recv()

    def sent(self):
        for j in range(4):
            self.copy(j).wait_send()


class CrossReduce:
    @staticmethod
    def scratch(rows, width):
        return [pltpu.VMEM((4, rows, width), BF16), dma((4,)), dma((4,))]

    def __init__(self, n, part, line, scratch):
        self.n, self.part, self.line = n, part, line
        self.rx, self.s, self.q = scratch
        self.rows = line.shape[1]

    def slab(self, x, d):
        rows = self.rows
        return pl.ds(pl.multiple_of((x * 4 + self.n.ahead(d)) * rows, 16), rows)

    def copy(self, d):
        src = self.part.at[self.slab(1 - self.n.x, d)]
        return remote(src, self.rx.at[d], self.s.at[d], self.q.at[d], self.n.xdev)

    def start(self, slots=(1, 2, 3, 0)):
        for d in slots:
            self.copy(d).start()

    def finish(self, d, part=None, x=None):
        part = self.part if part is None else part
        x = self.n.x if x is None else x
        self.copy(d).wait_recv()
        total = part[self.slab(x, d)].astype(F32) + self.rx[d].astype(F32)
        self.line[d] = total.astype(BF16)

    def sent(self):
        for d in range(4):
            self.copy(d).wait_send()


class LineReduce:
    @staticmethod
    def scratch(rows, width):
        return [pltpu.VMEM((3, rows, width), BF16), dma((3,)), dma((3,))]

    def __init__(self, n, line, out, scratch):
        self.n, self.line, self.out = n, line, out
        self.rz, self.s, self.q = scratch

    def copy(self, d):
        return remote(self.line.at[d], self.rz.at[d - 1], self.s.at[d - 1], self.q.at[d - 1], self.n.along[d - 1])

    def start(self, d):
        self.copy(d).start()

    def finish(self, line=None):
        for d in (1, 2, 3):
            self.copy(d).wait_recv()
        total = (self.line[0] if line is None else line).astype(F32)
        for d in range(3):
            total += self.rz[d].astype(F32)
        self.out[...] = total[: self.out.shape[0]]

    def sent(self):
        for d in (1, 2, 3):
            self.copy(d).wait_send()


class BlockGather:
    SEMS = [dma((2, 3)), dma((2, 3))]

    def __init__(self, n, src, dst, sems):
        self.n, self.src, self.dst = n, src, dst
        self.s, self.q = sems

    def rows(self, b, m):
        return self.dst.at[pl.ds(pl.multiple_of((4 * b + m) * BLOCK, BLOCK), BLOCK)]

    def copy(self, b, i):
        n = self.n
        if i == 2:
            v = self.rows(b, n.far)
            return remote(v, v, self.s.at[b, 2], self.q.at[b, 2], n.cdev)
        return remote(self.src(b), self.rows(b, n.own), self.s.at[b, i], self.q.at[b, i], (n.ydev, n.cdev)[i])

    def came(self, b, i):
        n = self.n
        v = self.rows(b, (n.far, n.sib, n.far_sib)[i])
        return remote(v, v, self.s.at[b, i], self.q.at[b, i], (n.ydev, n.cdev, n.cdev)[i])

    def start(self, b):
        self.copy(b, 0).start()
        self.copy(b, 1).start()

    def near(self, b):
        self.came(b, 1).wait_recv()

    def onward(self, b):
        self.came(b, 0).wait_recv()
        self.copy(b, 2).start()

    def wait(self, b):
        self.came(b, 2).wait_recv()

    def sent(self):
        for b in range(2):
            for i in range(3):
                self.copy(b, i).wait_send()


class BlockReduce:
    @staticmethod
    def scratch(width):
        return [pltpu.VMEM((2, 3, BLOCK, width), BF16), pltpu.VMEM((2, 3, BLOCK, width), BF16), dma((2, 3)), dma((2, 3))]

    NEAR, CROSS, OVER = 0, 1, 2

    def __init__(self, n, scratch):
        self.n = n
        self.out, self.got, self.s, self.q = scratch

    def copy(self, b, i):
        n = self.n
        dev = n.ydev if i == self.OVER else n.cdev
        return remote(self.out.at[b, i], self.got.at[b, i], self.s.at[b, i], self.q.at[b, i], dev)

    def put(self, b, i, value):
        self.out[b, i] = value.astype(BF16)
        if i != self.OVER:
            self.copy(b, i).start()

    def hold(self, b):
        self.copy(b, self.CROSS).wait_recv()

        def add(i):
            r = rows_at(i, 2 * STRIP)
            total = self.out[b, self.OVER, r].astype(F32) + self.got[b, self.CROSS, r].astype(F32)
            self.out[b, self.OVER, r] = total.astype(BF16)

        loop(BLOCK // (2 * STRIP), add)

    def over(self, b):
        self.copy(b, self.OVER).start()

    def near(self, b):
        self.copy(b, self.NEAR).wait_recv()

    def wait(self, b):
        self.copy(b, self.OVER).wait_recv()

    def extra(self, b, r):
        return self.got[b, self.NEAR, r].astype(F32) + self.got[b, self.OVER, r].astype(F32)

    def sent(self, over=True):
        for b in range(2):
            for i in range(3 if over else 2):
                self.copy(b, i).wait_send()


class Load:
    def __init__(self, src, buf, sem):
        self.src, self.buf = src, buf
        self.copy = pltpu.make_async_copy(src, buf, sem)
        self.waiting = False

    def start(self):
        self.copy.start()
        self.waiting = True

    def get(self):
        if self.waiting:
            self.copy.wait()
            self.waiting = False
        return self.buf


class Store:
    def __init__(self, dst, buf, sems):
        self.dst, self.buf, self.sems, self.copies = dst, buf, sems, []

    def put(self, start=None, size=None):
        src, dst = self.buf, self.dst
        if size is not None:
            src, dst = src.at[pl.ds(start, size)], dst.at[pl.ds(start, size)]
        copy = pltpu.make_async_copy(src, dst, self.sems.at[len(self.copies)])
        copy.start()
        self.copies.append(copy)

    def wait(self):
        for copy in self.copies:
            copy.wait()


class Steps:
    def __init__(self, steps):
        self.steps = list(steps)

    def __call__(self, count=1):
        for _ in range(count):
            if self.steps:
                self.steps.pop(0)()

    def rest(self):
        self(len(self.steps))


def dot(a, b, dims):
    return lax.dot_general(a, b, (dims, ((), ())), preferred_element_type=F32)


def dot_nn(a, b):
    return dot(a, b, ((1,), (0,)))


def dot_nt(a, b):
    return dot(a, b, ((1,), (1,)))


def dot_tn(a, b):
    return dot(a, b, ((0,), (0,)))


def rows_at(i, size):
    return pl.ds(pl.multiple_of(i * size, size), size)


def loop(count, body):
    def step(i, carry):
        body(i)
        return carry

    lax.fori_loop(0, count, step, 0)


def norm_parts(v):
    center = v - jnp.mean(v, axis=-1, keepdims=True)
    rstd = lax.rsqrt(jnp.mean(center * center, axis=-1, keepdims=True) + NORM_EPS)
    return center * rstd, rstd


def norm_back(e, gain, xhat, rstd):
    eg = e * gain
    return rstd * (
        eg - jnp.mean(eg, axis=-1, keepdims=True) - xhat * jnp.mean(eg * xhat, axis=-1, keepdims=True)
    )


def gelu(u):
    t = jnp.tanh(0.7978845608 * (u + 0.044715 * u * u * u))
    h = 0.5 * u * (1.0 + t)
    d = 0.5 * (1.0 + t) + 0.5 * u * (1.0 - t * t) * 0.7978845608 * (1.0 + 3 * 0.044715 * u * u)
    return h, d


PARTS = 4
WIDE = 384


def head_cols(part, p, h):
    return pl.ds(pl.multiple_of(p * part + h // 2 * 2 * PAD_DIM, 2 * PAD_DIM), 2 * PAD_DIM)


def causal(swap):
    a = lax.broadcasted_iota(jnp.int32, (BLOCK, BLOCK), 0)
    b = lax.broadcasted_iota(jnp.int32, (BLOCK, BLOCK), 1)
    return jnp.where((a <= b) if swap else (b <= a), 0.0, -1e30)


def forward_kernel(inner, heads, *refs):
    it = iter(refs)
    take = lambda n: [next(it) for _ in range(n)]
    shards, (x_ref, g_ref) = take(4), take(2)
    gain_in, shift_in, bias_out_in, gain2_in, shift2_in = take(5)
    bias_qkv, order_q, order_o, lens = take(4)
    out_u, out_d, cot, normed_st, qkv_st, mixed_st, lse_t, wa_st, middle, n2 = take(10)
    gq, go, own, mask, lenrow, lse = take(6)
    wq, wo, wu, wd = take(4)
    q_sems, o_sems, u_sems, d_sems = take(5), take(5), take(5), take(3)
    n1_sems, g_sems, red_s, ls = take(2), take(2), take(4), take(1)[0]
    n = Links(inner)
    normed, qkv, mixed, wa = (st.buf for st in (normed_st, qkv_st, mixed_st, wa_st))
    width = normed.shape[1]
    part = mixed.shape[1]
    greet(n.everyone)
    sq, so = SlabGather(n, wq, gq, q_sems), SlabGather(n, wo, go, o_sems)
    su, sd = SlabGather(n, wu, out_u, u_sems), LineGather(n, wd, out_d, d_sems)
    for own_slab, shard in zip((wq, wo, wu, wd), shards):
        rows, used = own_slab.shape[0], shard.shape[0]
        if rows > used:
            own_slab[rows - 16 :] = jnp.zeros((16, width), BF16)
        own_slab[:used] = shard[...]
        if own_slab is wq:
            sq.start()
    order_q.start()
    order_o.start()
    gain, shift, bias_out, gain2, shift2 = (
        ref[...].reshape(1, width) for ref in (gain_in, shift_in, bias_out_in, gain2_in, shift2_in)
    )

    def own_rows(b):
        return pl.ds(pl.multiple_of((4 * b + n.own) * BLOCK, BLOCK), BLOCK)

    ng = BlockGather(n, lambda b: normed.at[own_rows(b)], normed, n1_sems)
    gg = BlockGather(n, lambda b: g_ref.at[b, 0], cot, g_sems)
    for b in range(2):

        def norm(i, b=b):
            xhat, _ = norm_parts(x_ref[b, 0, rows_at(i, 2 * STRIP)].astype(F32))
            at = pl.multiple_of((4 * b + n.own) * BLOCK + i * 2 * STRIP, 2 * STRIP)
            normed[pl.ds(at, 2 * STRIP)] = (xhat * gain + shift).astype(BF16)

        loop(BLOCK // (2 * STRIP), norm)
        ng.start(b)
    for d in (1, 2, 3):
        sq.cross(d)
    so.start()
    su.start()
    sd.start()
    keep_g = [pltpu.make_async_copy(g_ref.at[b, 0], cot.at[own_rows(b)], ls.at[b]) for b in range(2)]
    for b in range(2):
        gg.start(b)
        keep_g[b].start()
    mask[...] = causal(False)
    key = lax.broadcasted_iota(jnp.int32, (8, 4 * BLOCK), 1)
    for b in range(2):
        lenrow[b] = jnp.where(key < lens[b], 0.0, -1e30)
    lse[...] = jnp.zeros_like(lse)
    mixed[...] = jnp.zeros_like(mixed)
    ng.onward(0)
    order_v = order_q.get()
    sq.wait()
    group = wa.shape[0] // 4
    slabs = jnp.concatenate([gq[s] for s in range(8)], axis=0)
    for p in range(3):
        wa[p * group : (p + 1) * group] = dot_nn(order_v[p * group : (p + 1) * group], slabs).astype(BF16)

    steps = Steps(
        [functools.partial(so.cross, d) for d in (1, 2, 3)]
        + [functools.partial(su.cross, d) for d in (1, 2, 3)]
    )
    lane = lax.broadcasted_iota(jnp.int32, (BLOCK, 2 * PAD_DIM), 1)

    def project(b):
        def one(t):
            r = rows_at(4 * b + t, BLOCK)
            a = normed[r]
            for p in range(3):
                cols = slice(p * part, (p + 1) * part)
                qkv[r, cols] = (dot_nt(a, wa[cols]) + bias_qkv[:, cols]).astype(BF16)

        loop(4, one)

    def attend(b, blocks):
        base = 4 * b * BLOCK

        def head(h):
            half = h % 2
            here = lane // PAD_DIM == half
            for i in blocks:
                r = slice(base + i * BLOCK, base + (i + 1) * BLOCK)
                keys = slice(base, base + (i + 1) * BLOCK)
                end = (i + 1) * BLOCK
                q = qkv[r, head_cols(part, 0, h)]
                k, v = qkv[keys, head_cols(part, 1, h)], qkv[keys, head_cols(part, 2, h)]
                s = dot_nt(jnp.where(here, q, jnp.zeros_like(q)), k) * SCALE2 + lenrow[b, 0:1, :end]
                diag = s[:, i * BLOCK :] + mask[...]
                s = jnp.concatenate([s[:, : i * BLOCK], diag], axis=1) if i else diag
                m = jnp.max(s, axis=-1, keepdims=True)
                e = jnp.exp2(s - m)
                t = jnp.sum(e, axis=-1, keepdims=True)
                p = (e * (1.0 / t)).astype(BF16)
                o = dot_nn(p, v).astype(BF16)
                cols = head_cols(part, 0, h)
                mixed[r, cols] = jnp.where(here, o, mixed[r, cols])
                lse[r] = jnp.where(lane == h, m + jnp.log2(t), lse[r])

        loop(heads, head)

    red = BlockReduce(n, red_s)

    def out_project(b):
        w = wa.at[pl.ds(3 * group, group)]

        def rows(m):
            return mixed[pl.ds(pl.multiple_of((4 * b + m) * BLOCK, BLOCK), BLOCK)]

        red.put(b, red.CROSS, dot_nn(rows(n.far_sib), w[...]))
        red.put(b, red.OVER, dot_nn(rows(n.far), w[...]))
        red.hold(b)
        red.over(b)
        red.put(b, red.NEAR, dot_nn(rows(n.sib), w[...]))
        own[b] = dot_nn(rows(n.own), w[...])

    def second_norm(b):
        red.near(b)
        red.wait(b)

        def finish(i):
            r = rows_at(i, STRIP)
            mid = x_ref[b, 0, r].astype(F32) + own[b, r] + red.extra(b, r) + bias_out
            middle[b, r] = mid
            xhat, _ = norm_parts(mid)
            n2[b, r] = (xhat * gain2 + shift2).astype(BF16)

        loop(BLOCK // STRIP, finish)

    ng.near(0)
    ng.wait(0)
    project(0)
    steps(3)
    attend(0, (0, 3))
    ng.onward(1)
    attend(0, (1, 2))
    steps()
    so.wait()
    ordo = order_o.get()
    slabs_o = jnp.concatenate([go[s] for s in range(8)], axis=0)
    wa[3 * group :] = dot_nn(ordo[...], slabs_o).astype(BF16)
    wa_st.put()
    out_project(0)
    ng.near(1)
    ng.wait(1)
    normed_st.put()
    project(1)
    qkv_st.put()
    gg.onward(0)
    steps(3)
    attend(1, (0, 3))
    gg.onward(1)
    attend(1, (1, 2))
    mixed_st.put()
    lse_t[...] = jnp.transpose(lse[...])[0:8]
    out_project(1)
    steps.rest()
    second_norm(0)
    second_norm(1)
    su.wait()
    sd.wait()
    for b in range(2):
        gg.near(b)
        gg.wait(b)
        keep_g[b].wait()
    for g in (sq, so, su, sd, ng, gg, red):
        g.sent()
    for st in (normed_st, qkv_st, mixed_st, wa_st):
        st.wait()


def hidden_kernel(inner, *refs):
    it = iter(refs)
    take = lambda n: [next(it) for _ in range(n)]
    n2_own, wu, line_w, bias_up, cot, middle, bias_down_in, gain_in = take(8)
    part_st, lined_st, gm_st, att, far_out, part_out, sums, sum_up = take(8)
    n2, hidden, grad_up, own, part_d, wd = take(6)
    n2_sems, red_s, out_s, rd, wd_sems, ls = take(2), take(4), take(4), take(3), take(3), take(1)[0]
    n = Links(inner)
    greet([n.xdev, n.ydev, n.cdev])
    total, width = n2.shape
    units = hidden.shape[1]
    gather = BlockGather(n, lambda b: n2_own.at[b], n2, n2_sems)
    weights = CrossGather(n, line_w, wd, wd_sems)
    for b in range(2):
        gather.start(b)
    wu.start()
    weights.start()
    for ld in (cot, middle):
        ld.start()

    def block(b, m):
        return pl.ds(pl.multiple_of((4 * b + m) * BLOCK, BLOCK), BLOCK)

    for b in range(2):
        cp = pltpu.make_async_copy(n2_own.at[b], n2.at[block(b, n.own)], ls.at[b])
        cp.start()
        cp.wait()
    red, out = BlockReduce(n, red_s), BlockReduce(n, out_s)
    sum_up[...] = jnp.zeros_like(sum_up)
    sums[...] = jnp.zeros_like(sums)
    wu_v = wu.get()

    def up(r):
        h, d = gelu(dot_nt(n2[r], wu_v[...]) + bias_up[...])
        hidden[r] = h.astype(BF16)
        grad_up[r] = d.astype(BF16)

    def down(r):
        g = (dot_nt(cot_v[r], wd[...]) * grad_up[r].astype(F32)).astype(BF16)
        grad_up[r] = g
        sum_up[...] += jnp.sum(g.astype(F32), axis=0, keepdims=True)

    def grad_in_of(r):
        return dot_nn(grad_up[r], wu_v[...])

    def output_of(r):
        return dot_nn(hidden[r], wd[...])

    loop(2, lambda b: up(block(b, n.own)))
    for b in range(2):
        gather.near(b)
    loop(2, lambda b: up(block(b, n.sib)))
    for b in range(2):
        gather.onward(b)
        up(block(b, n.far))
        gather.wait(b)
        up(block(b, n.far_sib))
    cot_v = cot.get()
    sum_d = CrossReduce(n, part_d, lined_st.buf, rd)

    def grad_down(q):
        cols = rows_at(q, WIDE)
        part_d[cols] = dot_tn(hidden[:, cols], cot_v[...]).astype(BF16)

    loop(units // WIDE, grad_down)
    sum_d.start()
    weights.wait()
    for b in range(2):
        down(block(b, n.far_sib))
        red.put(b, red.CROSS, grad_in_of(block(b, n.far_sib)))
        down(block(b, n.far))
        red.put(b, red.OVER, grad_in_of(block(b, n.far)))
        red.hold(b)
        red.over(b)
    for b in range(2):
        down(block(b, n.sib))
        red.put(b, red.NEAR, grad_in_of(block(b, n.sib)))
    bias_down, gain = bias_down_in[...].reshape(1, width), gain_in[...].reshape(1, width)
    middle_v = middle.get()

    def mine(b):
        r = block(b, n.own)
        down(r)
        own[b] = grad_in_of(r)
        part_out[b] = middle_v[b] + output_of(r) + bias_down

    loop(2, mine)
    for b in range(2):
        out.put(b, out.CROSS, output_of(block(b, n.far_sib)))
        out.put(b, out.OVER, output_of(block(b, n.far)))
        out.put(b, out.NEAR, output_of(block(b, n.sib)))
        out.hold(b)
        far_out[b] = out.out[b, out.OVER]
    grad_mid = gm_st.buf
    part_u = part_st.buf

    def grad_units(q):
        cols = rows_at(q, WIDE)
        part_u[cols] = dot_tn(grad_up[:, cols], n2[...]).astype(BF16)

    def norm_back_of(b):
        red.near(b)
        red.wait(b)
        out.near(b)

        def finish(i):
            r = rows_at(i, STRIP)
            at = pl.ds(pl.multiple_of((4 * b + n.own) * BLOCK + i * STRIP, STRIP), STRIP)
            e = own[b, r] + red.extra(b, r)
            xhat, rstd = norm_parts(middle_v[b, r])
            top = cot_v[at].astype(F32)
            g = top + norm_back(e, gain, xhat, rstd)
            grad_mid[b, r] = g
            low = g.astype(BF16)
            att[b, r] = low
            part_out[b, r] += out.got[b, out.NEAR, r].astype(F32)
            sums[0:1] += jnp.sum(e * xhat, axis=0, keepdims=True)
            sums[1:2] += jnp.sum(e, axis=0, keepdims=True)
            sums[2:3] += jnp.sum(low.astype(F32), axis=0, keepdims=True)
            sums[3:4] += jnp.sum(top, axis=0, keepdims=True)

        loop(BLOCK // STRIP, finish)

    loop(units // WIDE, grad_units)
    part_st.put()
    norm_back_of(0)
    norm_back_of(1)
    gm_st.put()
    for d in (1, 2, 3, 0):
        sum_d.finish(d)
    lined_st.put()
    gather.sent()
    weights.sent()
    red.sent()
    out.sent(False)
    sum_d.sent()
    for st in (part_st, lined_st, gm_st):
        st.wait()


def backward_kernel(inner, heads, *refs):
    it = iter(refs)
    take = lambda n: [next(it) for _ in range(n)]
    att_own, gm, wa, qkv, lse_t, mixed, normed, x_ref, gain_in, order_qt, order_ot, lens = take(12)
    part_u, line_d, far_out, part_out, sums_in, sum_up = take(6)
    cells_out, grad_in, grad_q, grad_o, grad_u, grad_d, small_out = take(7)
    att, gmix, gk, gv, grads, part_q, part_o, part_own, line0, mask, lencol, own, got_out, acc, inbox = take(15)
    line_u, line_q, line_o = take(3)
    att_sems, red_s, ru, rq, ro = take(2), take(4), take(3), take(3), take(3)
    zd, zu, zq, zo = take(3), take(3), take(3), take(3)
    ys, yr, ls, sa, qa = take(5)
    n = Links(inner)
    greet(n.everyone)
    total, width = att.shape
    part = gmix.shape[1]


    def block(b, m):
        return pl.ds(pl.multiple_of((4 * b + m) * BLOCK, BLOCK), BLOCK)

    gather = BlockGather(n, lambda b: att_own.at[b], att, att_sems)
    get_att = [pltpu.make_async_copy(att_own.at[b], att.at[block(b, n.own)], ls.at[b]) for b in range(2)]
    for b in range(2):
        gather.start(b)
        get_att[b].start()

    def out_copy(b):
        return remote(far_out.at[b], got_out.at[b], ys.at[b], yr.at[b], n.ydev)

    for b in range(2):
        out_copy(b).start()
    cu, cq, co = CrossReduce(n, part_u, line_u, ru), CrossReduce(n, part_q, line_q, rq), CrossReduce(n, part_o, line_o, ro)
    lind, linu = LineReduce(n, line_d, grad_d, zd), LineReduce(n, line_u, grad_u, zu)
    linq, lino = LineReduce(n, line_q, grad_q, zq), LineReduce(n, line_o, grad_o, zo)
    cu.start()
    for d in (1, 2, 3):
        lind.start(d)
    for ld in (wa, qkv, mixed, order_ot, order_qt, gm):
        ld.start()
    rows_u = line_u.shape[1]
    mine = pl.ds(pl.multiple_of(n.x * 4 * rows_u, 16), 4 * rows_u)
    get_own = pltpu.make_async_copy(part_u.at[mine], part_own, ls.at[2])
    get_line = pltpu.make_async_copy(line_d.at[0], line0, ls.at[3])
    get_own.start()
    get_line.start()

    mask[...] = causal(True)
    key = lax.broadcasted_iota(jnp.int32, (4 * BLOCK, BLOCK), 0)
    lane = lax.broadcasted_iota(jnp.int32, (BLOCK, 2 * PAD_DIM), 1)
    wa_v, qkv_v = wa.get(), qkv.get()
    group = wa_v.shape[0] // 4
    gmix[...] = jnp.zeros_like(gmix)
    grads[...] = jnp.zeros_like(grads)

    def to_heads(b):
        def one(t):
            r = rows_at(4 * b + t, BLOCK)
            gmix[r] = dot_nt(att[r], wa_v[3 * group :]).astype(BF16)

        loop(4, one)

    def attend(b, blocks):
        base = 4 * b * BLOCK

        def head(h):
            half = h % 2
            here = lane // PAD_DIM == half
            for i in blocks:
                r = slice(base + i * BLOCK, base + (i + 1) * BLOCK)
                keys = slice(base, base + (i + 1) * BLOCK)
                end = (i + 1) * BLOCK
                key_here = lax.broadcasted_iota(jnp.int32, (end, 2 * PAD_DIM), 1) // PAD_DIM == half
                cols = head_cols(part, 0, h)
                q, k, v = (qkv_v[rr, head_cols(part, p, h)] for p, rr in ((0, r), (1, keys), (2, keys)))
                g = gmix[r, cols]
                zero = jnp.zeros_like(q)
                q, g = jnp.where(here, q, zero), jnp.where(here, g, zero)
                s = dot_nt(k, q) * SCALE2 + lencol[:end]
                diag = s[i * BLOCK :] + mask[...]
                s = jnp.concatenate([s[: i * BLOCK], diag], axis=0) if i else diag
                p = jnp.exp2(s - lse_t[pl.ds(h, 1), r])
                gp = dot_nt(v, g)
                inner_sum = jnp.sum(p * gp, axis=0, keepdims=True)
                ds = (p * (gp - inner_sum)).astype(BF16)
                gv[:end, cols] += dot_nn(p.astype(BF16), g)
                gk[:end, cols] += dot_nn(ds, q)
                gq = (dot_tn(ds, k) * SCALE).astype(BF16)
                grads[r, cols] = jnp.where(here, gq, grads[r, cols])

        loop(heads, head)

    def settle(b):
        def one(t):
            r, rr = rows_at(t, BLOCK), rows_at(4 * b + t, BLOCK)
            grads[rr, part : 2 * part] = (gk[r] * SCALE).astype(BF16)
            grads[rr, 2 * part :] = gv[r].astype(BF16)

        loop(4, one)

    red = BlockReduce(n, red_s)

    def project_back(b):
        w = wa_v.at[pl.ds(0, 3 * group)]

        def rows(m):
            return grads[block(b, m)]

        red.put(b, red.CROSS, dot_nn(rows(n.far_sib), w[...]))
        red.put(b, red.OVER, dot_nn(rows(n.far), w[...]))
        red.hold(b)
        red.over(b)
        red.put(b, red.NEAR, dot_nn(rows(n.sib), w[...]))
        own[b] = dot_nn(rows(n.own), w[...])

    gain = gain_in[...].reshape(1, width)
    gm_v = gm.get()

    def first_norm(b):
        red.near(b)
        red.wait(b)

        def finish(i):
            r = rows_at(i, STRIP)
            e = own[b, r] + red.extra(b, r)
            xhat, rstd = norm_parts(x_ref[b, 0, r].astype(F32))
            grad_in[b, 0, r] = (gm_v[b, r] + norm_back(e, gain, xhat, rstd)).astype(BF16)
            acc[0, 0:1, :width] += jnp.sum(e * xhat, axis=0, keepdims=True)
            acc[0, 1:2, :width] += jnp.sum(e, axis=0, keepdims=True)

        loop(BLOCK // STRIP, finish)

    put_out = [pltpu.make_async_copy(got_out.at[b], cells_out.at[b, 0], ls.at[4 + b]) for b in range(2)]

    def output(b):
        out_copy(b).wait_recv()

        def finish(i):
            r = rows_at(i, 2 * STRIP)
            got_out[b, r] = (part_out[b, r] + got_out[b, r].astype(F32)).astype(BF16)

        loop(BLOCK // (2 * STRIP), finish)
        put_out[b].start()

    acc[0] = jnp.zeros_like(acc[0])
    acc[0, 2:3, :width] = sums_in[2:3]
    acc[0, 3:4, :width] = sums_in[0:1]
    acc[0, 4:5, :width] = sums_in[1:2]
    acc[0, 5:6, :width] = sums_in[3:4]
    acc[0, pl.ds(12 + n.n, 1)] = sum_up[...]

    def lengths_of(b):
        lencol[...] = jnp.where(key < lens[b], 0.0, -1e30)
        gk[...] = jnp.zeros_like(gk)
        gv[...] = jnp.zeros_like(gv)

    for cp in get_att:
        cp.wait()
    lengths_of(0)
    gather.near(0)
    gather.onward(0)
    gather.wait(0)
    to_heads(0)
    attend(0, (0, 3))
    get_own.wait()
    for d in (1, 2, 3, 0):
        cu.finish(d, part_own, 0)
        if d:
            linu.start(d)
    get_line.wait()
    lind.finish(line0[...])
    gather.near(1)
    gather.onward(1)
    gather.wait(1)
    to_heads(1)
    mixed_v, ordo = mixed.get(), order_ot.get()
    stack_o = dot_tn(mixed_v[...], att[...]).astype(BF16)
    part_o[...] = dot_nn(ordo[...], stack_o).astype(BF16)
    co.start()
    gather.sent()
    normed.start()
    attend(0, (1, 2))
    settle(0)
    project_back(0)
    for d in (1, 2, 3, 0):
        co.finish(d)
        if d:
            lino.start(d)
    lengths_of(1)
    attend(1, (0, 3))
    output(0)
    output(1)
    attend(1, (1, 2))
    settle(1)
    project_back(1)
    normed_v, oq = normed.get(), order_qt.get()
    def grad_proj(q):
        cols = rows_at(q, WIDE)
        qkv_v[cols, :width] = dot_tn(grads[:, cols], normed_v[...]).astype(BF16)

    loop(3 * part // WIDE, grad_proj)
    rows_q = line_q.shape[1]

    def reorder(x):
        at = pl.ds(pl.multiple_of(x * 4 * rows_q, 16), 4 * rows_q)
        part_q[at] = dot_nn(oq[at], qkv_v[: 3 * part, :width]).astype(BF16)

    reorder(1 - n.x)
    cq.start()
    reorder(n.x)

    def sum_rows(t):
        acc[0, pl.ds(8 + n.n, 1)] += jnp.sum(grads[rows_at(t, BLOCK)].astype(F32), axis=0, keepdims=True)

    loop(total // BLOCK, sum_rows)
    first_norm(0)
    linu.finish()
    lino.finish()
    first_norm(1)
    peers = [n.cdev, n.xdev, n.ydev, n.pair, n.along[1]]

    def small_copy(i):
        return remote(acc.at[i], inbox.at[i], sa.at[i], qa.at[i], peers[i])

    def small_step(i):
        if i > 0:
            small_copy(i - 1).wait_recv()
            acc[i] = acc[i - 1] + inbox[i - 1]
        if i < 5:
            small_copy(i).start()

    small_step(0)
    for d in (1, 2, 3, 0):
        cq.finish(d)
        if d:
            linq.start(d)
        small_step(4 if d == 0 else d)
    small_step(5)
    small_out[...] = acc[5]
    linq.finish()
    for b in range(2):
        out_copy(b).wait_send()
        put_out[b].wait()
    for i in range(5):
        small_copy(i).wait_send()
    for g in (red, cu, cq, co, lind, linu, linq, lino):
        g.sent()


ANY = pl.BlockSpec(memory_space=pl.ANY)
VM = pl.BlockSpec(memory_space=pltpu.VMEM)
SM = pl.BlockSpec(memory_space=pltpu.SMEM)
ASYNC = "async"


def call(kernel, ident, name, outs, ins, scratch, share=None):
    share = share or {}
    lazy_in = [i for i, (_, s) in enumerate(ins) if s is ASYNC]
    lazy_out = [i for i, (_, _, s) in enumerate(outs) if s is ASYNC]
    extra = [pltpu.VMEM(ins[i][0].shape, ins[i][0].dtype) for i in lazy_in if i not in share]
    extra += [pltpu.VMEM(outs[i][0], outs[i][1]) for i in lazy_out]
    extra += [dma((max(1, len(lazy_in)),)), dma((max(1, len(lazy_out)), PARTS))]

    def body(*refs):
        refs = list(refs)
        bufs = refs[len(refs) - len(extra) :]
        refs = refs[: len(refs) - len(extra)]
        in_sems, out_sems = bufs[-2:]
        bufs = iter(bufs)
        for b, i in enumerate(lazy_in):
            buf = refs[len(ins) + len(outs) + share[i]] if i in share else next(bufs)
            refs[i] = Load(refs[i], buf, in_sems.at[b])
        for b, i in enumerate(lazy_out):
            at = len(ins) + i
            refs[at] = Store(refs[at], next(bufs), out_sems.at[b])
        kernel(*refs)

    return pl.pallas_call(
        body,
        out_shape=[jax.ShapeDtypeStruct(s, d) for s, d, _ in outs],
        in_specs=[ANY if s is ASYNC else s for _, s in ins],
        out_specs=[ANY if s is ASYNC else s for _, _, s in outs],
        scratch_shapes=[*scratch, *extra],
        compiler_params=pltpu.CompilerParams(
            collective_id=ident, has_side_effects=True, vmem_limit_bytes=VMEM_LIMIT
        ),
        name=name,
    )(*[a for a, _ in ins])


def order_matrix(rows, heads, parts, wide):
    m = np.zeros((parts * wide, OUTER * rows), np.float32)
    each = HEAD_DIM // OUTER
    for x in range(2):
        for z in range(4):
            w = 2 * z + x
            for g in range(parts * heads):
                part, head = g % parts, g // parts
                for e in range(each):
                    m[part * wide + head * PAD_DIM + w * each + e, (x * 4 + z) * rows + g * each + e] = 1
    return m


def on_device(
    cells_in, lengths, w_qkv, w_out, w_up, w_down, ln1_gain, ln1_shift, bias_qv, bias_out,
    ln2_gain, ln2_shift, bias_up, bias_down, cotangent,
):
    wide = lax.axis_size("wide")
    inner = wide // OUTER
    shards = [w_qkv, w_out, w_up, w_down]
    if inner > 1:
        groups = [[o * inner + i for i in range(inner)] for o in range(OUTER)]
        shards = [
            lax.all_gather(s, "wide", axis=1, tiled=True, axis_index_groups=groups) for s in shards
        ]
    width = cells_in.shape[3]
    total = 8 * BLOCK
    heads = width // HEAD_DIM // 4
    part = -(-heads // 2) * 2 * PAD_DIM
    n = lax.axis_index("narrow")
    weights = [s.reshape(-1, width) for s in shards]
    used = [s.size // width for s in shards]
    rows_q, rows_o, rows = (-(-u // 16) * 16 for u in used[:3])
    units = OUTER * rows
    order_q, order_o = order_matrix(rows_q, heads, 3, part), order_matrix(rows_o, heads, 1, part)

    def constant(a):
        return jnp.asarray(np.ascontiguousarray(a), BF16)

    b_qv = lax.dynamic_index_in_dim(bias_qv.reshape(2, 4, heads, HEAD_DIM), n, axis=1, keepdims=False)
    b_qv = jnp.pad(b_qv, ((0, 0), (0, 0), (0, PAD_DIM - HEAD_DIM))).reshape(2, heads * PAD_DIM)
    b_qv = jnp.pad(b_qv, ((0, 0), (0, part - heads * PAD_DIM)))
    bias_qkv = jnp.stack([b_qv[0], jnp.zeros_like(b_qv[0]), b_qv[1]]).reshape(1, -1)
    b_u = lax.dynamic_slice_in_dim(bias_up, n * used[2] * OUTER, used[2] * OUTER).reshape(used[2], 4, 2).transpose(2, 1, 0)
    b_u = jnp.pad(b_u, ((0, 0), (0, 0), (0, rows - used[2]))).reshape(1, -1)
    lens = lengths[:, 0]

    own2 = (2, BLOCK, width)
    vmem = pltpu.VMEM
    g_u, g_d, cot, normed, qkv, mixed, lse, wa, middle, n2 = call(
        functools.partial(forward_kernel, inner, heads), 0, "forward",
        [((OUTER, rows, width), BF16, ANY), ((4, rows, width), BF16, ANY), ((total, width), BF16, ANY),
         ((total, width), BF16, ASYNC), ((total, 3 * part), BF16, ASYNC), ((total, part), BF16, ASYNC),
         ((8, total), F32, VM), ((4 * part, width), BF16, ASYNC), (own2, F32, VM), (own2, BF16, VM)],
        [*[(w, VM) for w in weights], (cells_in, VM), (cotangent, VM),
         *[(v, VM) for v in (ln1_gain, ln1_shift, bias_out, ln2_gain, ln2_shift)], (bias_qkv, VM),
         (constant(order_q), ASYNC), (constant(order_o), ASYNC), (lens, SM)],
        [vmem((OUTER, rows_q, width), BF16), vmem((OUTER, rows_o, width), BF16), vmem(own2, F32),
         vmem((BLOCK, BLOCK), F32), vmem((2, 8, 4 * BLOCK), F32), vmem((total, 2 * PAD_DIM), F32),
         *[vmem((r, width), BF16) for r in (rows_q, rows_o, rows, rows)],
         *SlabGather.SEMS * 3, *LineGather.SEMS, *BlockGather.SEMS * 2, *BlockReduce.scratch(width), dma((2,))],
    )
    part_u, line_d, grad_mid, att, far_out, part_out, sums, sum_up = call(
        functools.partial(hidden_kernel, inner), 1, "hidden_units",
        [((units, width), BF16, ASYNC), ((4, rows, width), BF16, ASYNC), (own2, F32, ASYNC), (own2, BF16, VM),
         (own2, BF16, VM), (own2, F32, VM), ((8, width), F32, VM), ((1, units), F32, VM)],
        [(n2, VM), (g_u.reshape(units, width), ASYNC), (g_d, ANY), (b_u, VM), (cot, ASYNC),
         (middle, ASYNC), (bias_down, VM), (ln2_gain, VM)],
        [vmem((total, width), BF16), vmem((total, units), BF16), vmem((total, units), BF16), vmem(own2, F32),
         vmem((units, width), BF16), vmem((units, width), BF16),
         *BlockGather.SEMS, *BlockReduce.scratch(width), *BlockReduce.scratch(width), *CrossReduce.scratch(rows, width),
         *CrossGather.SEMS, dma((2,))],
    )
    small_shape = (16, units)
    cells_out, grad_in, grad_q, grad_o, grad_u, grad_d, small = call(
        functools.partial(backward_kernel, inner, heads), 2, "backward",
        [(cells_in.shape, BF16, ANY), (cells_in.shape, BF16, VM), ((used[0], width), F32, VM), ((used[1], width), F32, VM),
         ((used[2], width), F32, VM), ((used[3], width), F32, VM), (small_shape, F32, VM)],
        [(att, ANY), (grad_mid, ASYNC), (wa, ASYNC), (qkv, ASYNC), (lse, VM), (mixed, ASYNC), (normed, ASYNC),
         (cells_in, VM), (ln1_gain, VM), (constant(order_q.T), ASYNC), (constant(order_o.T), ASYNC), (lens, SM),
         (part_u, ANY), (line_d, ANY), (far_out, ANY), (part_out, VM), (sums, VM), (sum_up, VM)],
        [vmem((total, width), BF16), vmem((total, part), BF16), vmem((total // 2, part), F32), vmem((total // 2, part), F32),
         vmem((total, 3 * part), BF16), vmem((OUTER * rows_q, width), BF16), vmem((OUTER * rows_o, width), BF16),
         vmem((4 * rows, width), BF16), vmem((rows, width), BF16), vmem((BLOCK, BLOCK), F32),
         vmem((4 * BLOCK, BLOCK), F32), vmem(own2, F32),
         vmem(own2, BF16), vmem((6, *small_shape), F32), vmem((5, *small_shape), F32),
         vmem((4, rows, width), BF16), vmem((4, rows_q, width), BF16), vmem((4, rows_o, width), BF16),
         *BlockGather.SEMS, *BlockReduce.scratch(width), *CrossReduce.scratch(rows, width),
         *CrossReduce.scratch(rows_q, width), *CrossReduce.scratch(rows_o, width),
         *LineReduce.scratch(rows, width), *LineReduce.scratch(rows, width), *LineReduce.scratch(rows_q, width),
         *LineReduce.scratch(rows_o, width), dma((2,)), dma((2,)), dma((6,)), dma((5,)), dma((5,))],
        share={6: 0},
    )
    grads = [g.reshape(s.shape) for g, s in zip((grad_q, grad_o, grad_u, grad_d), shards)]
    if inner > 1:
        grads = [
            lax.psum_scatter(g, "wide", scatter_dimension=1, axis_index_groups=groups, tiled=True)
            for g in grads
        ]
    sum_qkv = small[8:12].reshape(4, 3, part)[:, :, : heads * PAD_DIM].reshape(4, 3, heads, PAD_DIM)[..., :HEAD_DIM]
    grad_b = jnp.concatenate([sum_qkv[:, 0].reshape(-1), sum_qkv[:, 2].reshape(-1)])
    grad_bu = small[12:16].reshape(4, 2, 4, rows)[..., : used[2]].transpose(0, 3, 2, 1).reshape(-1)
    flat = [small[i, :width] for i in range(6)]
    return (
        cells_out, grad_in, *grads, flat[0], flat[1], grad_b, flat[2], flat[3], flat[4], grad_bu, flat[5],
    )


def solution(mesh):
    cell = P(None, "wide", "narrow", None)
    shard = P("narrow", "wide")
    return jax.shard_map(
        on_device,
        mesh=mesh,
        in_specs=(cell, P(None, "wide"), *[shard] * 4, *[P()] * 8, cell),
        out_specs=(cell, cell, *[shard] * 4, *[P()] * 8),
        check_vma=False,
    )
```

```python
import functools

import jax
import jax.numpy as jnp
import numpy as np
from jax import lax
from jax.experimental import pallas as pl
from jax.experimental.pallas import tpu as pltpu
from jax.sharding import PartitionSpec as P

HEAD_DIM = 56
PAD_DIM = 64
OUTER = 8
NORM_EPS = 1e-05
SCALE = HEAD_DIM ** (-0.5)
SCALE2 = SCALE * 1.4426950408889634
MESH = pl.DeviceIdType.MESH
BF16 = jnp.bfloat16
F32 = jnp.float32
BLOCK = 256
STRIP = 32
VMEM_LIMIT = 63 * 2**20 + 2**19


class Links:
    def __init__(self, inner):
        w = lax.axis_index("wide")
        n = lax.axis_index("narrow")
        outer, wi = w // inner, w % inner
        z, x, y, c = outer // 2, outer % 2, n // 2, n % 2
        self.z, self.x, self.y, self.c, self.n = z, x, y, c, n

        def device(z, x, y, c):
            return ((2 * z + x) * inner + wi, 2 * y + c)

        self.along = [device((z + d) % 4, x, y, c) for d in (1, 2, 3)]
        self.xdev = device(z, 1 - x, y, c)
        self.ydev = device(z, x, 1 - y, c)
        self.cdev = device(z, x, y, 1 - c)
        self.middle = (z == 1) | (z == 2)
        self.end = device(jnp.where(z >= 2, 3, 0), x, y, c)
        self.end_slot = jnp.where(z >= 2, 2, 0)
        self.cross = device(z, x, 1 - y, 1 - c)
        self.everyone = [*self.along, self.xdev, self.ydev, self.cdev]
        self.own, self.sib = n, 2 * y + 1 - c
        self.far, self.far_sib = 2 * (1 - y) + c, 2 * (1 - y) + 1 - c

    def back(self, d):
        return (self.z + 4 - d) % 4

    def ahead(self, d):
        return (self.z + d) % 4


def remote(src, dst, send, recv, dev):
    return pltpu.make_async_remote_copy(
        src_ref=src, dst_ref=dst, send_sem=send, recv_sem=recv, device_id=dev, device_id_type=MESH
    )


def greet(devices):
    barrier = pltpu.get_barrier_semaphore()
    for dev in devices:
        pl.semaphore_signal(barrier, inc=1, device_id=dev, device_id_type=MESH)
    pl.semaphore_wait(barrier, len(devices))


dma = pltpu.SemaphoreType.DMA


class Line:
    ORDER = (2, 1, 3)

    def zcopy(self, d):
        n = self.n
        return remote(self.own, self.place(n.z), self.zs.at[d - 1], self.zr.at[d - 1], n.along[d - 1])

    def direct(self, d, step):
        if d == 2:
            step()
        else:
            pl.when(self.n.z != (3 if d == 1 else 0))(step)

    def zstart(self):
        for d in self.ORDER:
            self.direct(d, self.zcopy(d).start)

    def zcame(self, d):
        v = self.place(self.n.back(d))
        return remote(v, v, self.zs.at[d - 1], self.zr.at[d - 1], self.n.along[d - 1])

    def zrelay(self):
        n = self.n
        v = self.place(n.back(2))
        return remote(v, v, self.zs.at[3], self.zr.at[n.end_slot], n.end)

    def zwait(self, d):
        self.zcame(d).wait_recv()
        if d == 2:
            pl.when(self.n.middle)(lambda: self.zrelay().start())

    def zsent(self):
        for d in self.ORDER:
            self.direct(d, self.zcopy(d).wait_send)
        pl.when(self.n.middle)(lambda: self.zrelay().wait_send())


class SlabGather(Line):
    SEMS = [dma((4,)), dma((3,)), dma((4,)), dma((4,)), dma((1,))]

    def __init__(self, n, own, out, sems):
        self.n, self.own, self.out = n, own, out
        self.zs, self.zr, self.xs, self.xr, self.ls = sems
        self.keep = pltpu.make_async_copy(own, out.at[n.x * 4 + n.z], self.ls.at[0])

    def place(self, z):
        return self.out.at[self.n.x * 4 + z]

    def xcopy(self, d):
        n = self.n
        v = self.out.at[n.x * 4 + n.back(d)]
        return remote(self.own if d == 0 else v, v, self.xs.at[d], self.xr.at[d], n.xdev)

    def xcame(self, d):
        n = self.n
        v = self.out.at[(1 - n.x) * 4 + n.back(d)]
        return remote(v, v, self.xs.at[d], self.xr.at[d], n.xdev)

    def start(self):
        self.zstart()
        self.keep.start()

    def begin(self):
        self.xcopy(0).start()

    def cross(self, d):
        self.zwait(d)
        self.xcopy(d).start()

    def wait(self):
        self.keep.wait()
        for d in range(4):
            self.xcame(d).wait_recv()

    def sent(self):
        self.zsent()
        for d in range(4):
            self.xcopy(d).wait_send()


class LineGather(Line):
    SEMS = [dma((4,)), dma((3,)), dma((1,))]

    def __init__(self, n, own, out, sems):
        self.n, self.own, self.out = n, own, out
        self.zs, self.zr, self.ls = sems
        self.keep = pltpu.make_async_copy(own, out.at[n.z], self.ls.at[0])

    def place(self, z):
        return self.out.at[z]

    def start(self):
        self.zstart()
        self.keep.start()

    def wait(self):
        self.keep.wait()
        for d in (1, 3):
            self.zwait(d)

    def sent(self):
        self.zsent()


class CrossGather:
    SEMS = [dma((4,)), dma((4,)), dma((4,))]

    def __init__(self, n, line, out, sems):
        self.n, self.line, self.out = n, line, out
        self.s, self.q, self.ls = sems
        self.size = line.shape[1]

    def slab(self, x, j):
        return self.out.at[pl.ds(pl.multiple_of((x * 4 + j) * self.size, 16), self.size)]

    def copy(self, j):
        return remote(self.line.at[j], self.slab(self.n.x, j), self.s.at[j], self.q.at[j], self.n.xdev)

    def keep(self, j):
        return pltpu.make_async_copy(self.line.at[j], self.slab(self.n.x, j), self.ls.at[j])

    def start(self):
        for j in range(4):
            self.copy(j).start()
            self.keep(j).start()

    def wait(self):
        for j in range(4):
            self.keep(j).wait()
            v = self.slab(1 - self.n.x, j)
            remote(v, v, self.s.at[j], self.q.at[j], self.n.xdev).wait_recv()

    def sent(self):
        for j in range(4):
            self.copy(j).wait_send()


class CrossReduce:
    @staticmethod
    def scratch(rows, width):
        return [pltpu.VMEM((4, rows, width), BF16), dma((4,)), dma((4,))]

    def __init__(self, n, part, line, scratch):
        self.n, self.part, self.line = n, part, line
        self.rx, self.s, self.q = scratch
        self.rows = line.shape[1]

    def slab(self, x, d):
        rows = self.rows
        return pl.ds(pl.multiple_of((x * 4 + self.n.ahead(d)) * rows, 16), rows)

    def copy(self, d):
        src = self.part.at[self.slab(1 - self.n.x, d)]
        return remote(src, self.rx.at[d], self.s.at[d], self.q.at[d], self.n.xdev)

    def start(self, slots=(1, 2, 3, 0)):
        for d in slots:
            self.copy(d).start()

    def finish(self, d, part=None, x=None):
        part = self.part if part is None else part
        x = self.n.x if x is None else x
        self.copy(d).wait_recv()
        total = part[self.slab(x, d)].astype(F32) + self.rx[d].astype(F32)
        self.line[d] = total.astype(BF16)

    def sent(self):
        for d in range(4):
            self.copy(d).wait_send()


class LineReduce:
    @staticmethod
    def scratch(rows, width):
        return [pltpu.VMEM((3, rows, width), BF16), dma((3,)), dma((3,))]

    def __init__(self, n, line, out, scratch):
        self.n, self.line, self.out = n, line, out
        self.rz, self.s, self.q = scratch

    def copy(self, d):
        return remote(self.line.at[d], self.rz.at[d - 1], self.s.at[d - 1], self.q.at[d - 1], self.n.along[d - 1])

    def start(self, d):
        self.copy(d).start()

    def finish(self, line=None):
        for d in (1, 2, 3):
            self.copy(d).wait_recv()
        total = (self.line[0] if line is None else line).astype(F32)
        for d in range(3):
            total += self.rz[d].astype(F32)
        self.out[...] = total[: self.out.shape[0]]

    def sent(self):
        for d in (1, 2, 3):
            self.copy(d).wait_send()


class BlockGather:
    SEMS = [dma((2, 3)), dma((2, 3))]

    def __init__(self, n, src, dst, sems):
        self.n, self.src, self.dst = n, src, dst
        self.s, self.q = sems

    def rows(self, b, m):
        return self.dst.at[pl.ds(pl.multiple_of((4 * b + m) * BLOCK, BLOCK), BLOCK)]

    def copy(self, b, i):
        n = self.n
        if i == 2:
            v = self.rows(b, n.far)
            return remote(v, v, self.s.at[b, 2], self.q.at[b, 2], n.cdev)
        return remote(self.src(b), self.rows(b, n.own), self.s.at[b, i], self.q.at[b, i], (n.ydev, n.cdev)[i])

    def came(self, b, i):
        n = self.n
        v = self.rows(b, (n.far, n.sib, n.far_sib)[i])
        return remote(v, v, self.s.at[b, i], self.q.at[b, i], (n.ydev, n.cdev, n.cdev)[i])

    def start(self, b):
        self.copy(b, 0).start()
        self.copy(b, 1).start()

    def near(self, b):
        self.came(b, 1).wait_recv()

    def onward(self, b):
        self.came(b, 0).wait_recv()
        self.copy(b, 2).start()

    def wait(self, b):
        self.came(b, 2).wait_recv()

    def sent(self):
        for b in range(2):
            for i in range(3):
                self.copy(b, i).wait_send()


class BlockReduce:
    @staticmethod
    def scratch(width):
        return [pltpu.VMEM((2, 3, BLOCK, width), BF16), pltpu.VMEM((2, 3, BLOCK, width), BF16), dma((2, 3)), dma((2, 3))]

    NEAR, CROSS, OVER = 0, 1, 2

    def __init__(self, n, scratch):
        self.n = n
        self.out, self.got, self.s, self.q = scratch

    def copy(self, b, i):
        n = self.n
        dev = n.ydev if i == self.OVER else n.cdev
        return remote(self.out.at[b, i], self.got.at[b, i], self.s.at[b, i], self.q.at[b, i], dev)

    def put(self, b, i, value):
        self.out[b, i] = value.astype(BF16)
        if i != self.OVER:
            self.copy(b, i).start()

    def hold(self, b):
        self.copy(b, self.CROSS).wait_recv()

        def add(i):
            r = rows_at(i, 2 * STRIP)
            total = self.out[b, self.OVER, r].astype(F32) + self.got[b, self.CROSS, r].astype(F32)
            self.out[b, self.OVER, r] = total.astype(BF16)

        loop(BLOCK // (2 * STRIP), add)

    def over(self, b):
        self.copy(b, self.OVER).start()

    def near(self, b):
        self.copy(b, self.NEAR).wait_recv()

    def wait(self, b):
        self.copy(b, self.OVER).wait_recv()

    def extra(self, b, r):
        return self.got[b, self.NEAR, r].astype(F32) + self.got[b, self.OVER, r].astype(F32)

    def sent(self, over=True):
        for b in range(2):
            for i in range(3 if over else 2):
                self.copy(b, i).wait_send()


class Load:
    def __init__(self, src, buf, sem):
        self.src, self.buf = src, buf
        self.copy = pltpu.make_async_copy(src, buf, sem)
        self.waiting = False

    def start(self):
        self.copy.start()
        self.waiting = True

    def get(self):
        if self.waiting:
            self.copy.wait()
            self.waiting = False
        return self.buf


class Store:
    def __init__(self, dst, buf, sems):
        self.dst, self.buf, self.sems, self.copies = dst, buf, sems, []

    def put(self, start=None, size=None):
        src, dst = self.buf, self.dst
        if size is not None:
            src, dst = src.at[pl.ds(start, size)], dst.at[pl.ds(start, size)]
        copy = pltpu.make_async_copy(src, dst, self.sems.at[len(self.copies)])
        copy.start()
        self.copies.append(copy)

    def wait(self):
        for copy in self.copies:
            copy.wait()


class Steps:
    def __init__(self, steps):
        self.steps = list(steps)

    def __call__(self, count=1):
        for _ in range(count):
            if self.steps:
                self.steps.pop(0)()

    def rest(self):
        self(len(self.steps))


def dot(a, b, dims):
    return lax.dot_general(a, b, (dims, ((), ())), preferred_element_type=F32)


def dot_nn(a, b):
    return dot(a, b, ((1,), (0,)))


def dot_nt(a, b):
    return dot(a, b, ((1,), (1,)))


def dot_tn(a, b):
    return dot(a, b, ((0,), (0,)))


def rows_at(i, size):
    return pl.ds(pl.multiple_of(i * size, size), size)


def loop(count, body):
    def step(i, carry):
        body(i)
        return carry

    lax.fori_loop(0, count, step, 0)


def norm_parts(v):
    center = v - jnp.mean(v, axis=-1, keepdims=True)
    rstd = lax.rsqrt(jnp.mean(center * center, axis=-1, keepdims=True) + NORM_EPS)
    return center * rstd, rstd


def norm_back(e, gain, xhat, rstd):
    eg = e * gain
    return rstd * (
        eg - jnp.mean(eg, axis=-1, keepdims=True) - xhat * jnp.mean(eg * xhat, axis=-1, keepdims=True)
    )


def gelu(u):
    t = jnp.tanh(0.7978845608 * (u + 0.044715 * u * u * u))
    h = 0.5 * u * (1.0 + t)
    d = 0.5 * (1.0 + t) + 0.5 * u * (1.0 - t * t) * 0.7978845608 * (1.0 + 3 * 0.044715 * u * u)
    return h, d


PARTS = 4
WIDE = 384


def head_cols(part, p, h):
    return pl.ds(pl.multiple_of(p * part + h // 2 * 2 * PAD_DIM, 2 * PAD_DIM), 2 * PAD_DIM)


def causal(swap):
    a = lax.broadcasted_iota(jnp.int32, (BLOCK, BLOCK), 0)
    b = lax.broadcasted_iota(jnp.int32, (BLOCK, BLOCK), 1)
    return jnp.where((a <= b) if swap else (b <= a), 0.0, -1e30)


def forward_kernel(inner, heads, *refs):
    it = iter(refs)
    take = lambda n: [next(it) for _ in range(n)]
    shards, (x_ref, g_ref) = take(4), take(2)
    gain_in, shift_in, bias_out_in, gain2_in, shift2_in = take(5)
    bias_qkv, order_q, order_o, lens = take(4)
    out_u, out_d, cot, normed_st, qkv_st, mixed_st, lse_t, wa_st, middle, n2 = take(10)
    gq, go, own, mask, lenrow, lse = take(6)
    wq, wo, wu, wd = take(4)
    q_sems, o_sems, u_sems, d_sems = take(5), take(5), take(5), take(3)
    n1_sems, g_sems, red_s, ls = take(2), take(2), take(4), take(1)[0]
    n = Links(inner)
    normed, qkv, mixed, wa = (st.buf for st in (normed_st, qkv_st, mixed_st, wa_st))
    width = normed.shape[1]
    part = mixed.shape[1]
    greet(n.everyone)
    sq, so = SlabGather(n, wq, gq, q_sems), SlabGather(n, wo, go, o_sems)
    su, sd = SlabGather(n, wu, out_u, u_sems), LineGather(n, wd, out_d, d_sems)
    for own_slab, shard in zip((wq, wo, wu, wd), shards):
        rows, used = own_slab.shape[0], shard.shape[0]
        if rows > used:
            own_slab[rows - 16 :] = jnp.zeros((16, width), BF16)
        own_slab[:used] = shard[...]
        if own_slab is wq:
            sq.start()
            sq.begin()
    order_q.start()
    order_o.start()
    gain, shift, bias_out, gain2, shift2 = (
        ref[...].reshape(1, width) for ref in (gain_in, shift_in, bias_out_in, gain2_in, shift2_in)
    )

    def own_rows(b):
        return pl.ds(pl.multiple_of((4 * b + n.own) * BLOCK, BLOCK), BLOCK)

    ng = BlockGather(n, lambda b: normed.at[own_rows(b)], normed, n1_sems)
    gg = BlockGather(n, lambda b: g_ref.at[b, 0], cot, g_sems)
    for b in range(2):

        def norm(i, b=b):
            xhat, _ = norm_parts(x_ref[b, 0, rows_at(i, 2 * STRIP)].astype(F32))
            at = pl.multiple_of((4 * b + n.own) * BLOCK + i * 2 * STRIP, 2 * STRIP)
            normed[pl.ds(at, 2 * STRIP)] = (xhat * gain + shift).astype(BF16)

        loop(BLOCK // (2 * STRIP), norm)
        ng.start(b)
    for g in (so, su, sd):
        g.start()
    for d in Line.ORDER:
        sq.cross(d)
    so.begin()
    su.begin()
    keep_g = [pltpu.make_async_copy(g_ref.at[b, 0], cot.at[own_rows(b)], ls.at[b]) for b in range(2)]
    for b in range(2):
        gg.start(b)
        keep_g[b].start()
    mask[...] = causal(False)
    key = lax.broadcasted_iota(jnp.int32, (8, 4 * BLOCK), 1)
    for b in range(2):
        lenrow[b] = jnp.where(key < lens[b], 0.0, -1e30)
    lse[...] = jnp.zeros_like(lse)
    mixed[...] = jnp.zeros_like(mixed)
    ng.onward(0)
    order_v = order_q.get()
    sq.wait()
    group = wa.shape[0] // 4
    slabs = jnp.concatenate([gq[s] for s in range(8)], axis=0)
    for p in range(3):
        wa[p * group : (p + 1) * group] = dot_nn(order_v[p * group : (p + 1) * group], slabs).astype(BF16)

    steps = Steps(
        [functools.partial(so.cross, d) for d in Line.ORDER]
        + [functools.partial(su.cross, d) for d in Line.ORDER]
        + [functools.partial(sd.zwait, 2)]
    )
    lane = lax.broadcasted_iota(jnp.int32, (BLOCK, 2 * PAD_DIM), 1)

    def project(b):
        def one(t):
            r = rows_at(4 * b + t, BLOCK)
            a = normed[r]
            for p in range(3):
                cols = slice(p * part, (p + 1) * part)
                qkv[r, cols] = (dot_nt(a, wa[cols]) + bias_qkv[:, cols]).astype(BF16)

        loop(4, one)

    def attend(b, blocks):
        base = 4 * b * BLOCK

        def head(h):
            half = h % 2
            here = lane // PAD_DIM == half
            for i in blocks:
                r = slice(base + i * BLOCK, base + (i + 1) * BLOCK)
                keys = slice(base, base + (i + 1) * BLOCK)
                end = (i + 1) * BLOCK
                q = qkv[r, head_cols(part, 0, h)]
                k, v = qkv[keys, head_cols(part, 1, h)], qkv[keys, head_cols(part, 2, h)]
                s = dot_nt(jnp.where(here, q, jnp.zeros_like(q)), k) * SCALE2 + lenrow[b, 0:1, :end]
                diag = s[:, i * BLOCK :] + mask[...]
                s = jnp.concatenate([s[:, : i * BLOCK], diag], axis=1) if i else diag
                m = jnp.max(s, axis=-1, keepdims=True)
                e = jnp.exp2(s - m)
                t = jnp.sum(e, axis=-1, keepdims=True)
                p = (e * (1.0 / t)).astype(BF16)
                o = dot_nn(p, v).astype(BF16)
                cols = head_cols(part, 0, h)
                mixed[r, cols] = jnp.where(here, o, mixed[r, cols])
                lse[r] = jnp.where(lane == h, m + jnp.log2(t), lse[r])

        loop(heads, head)

    red = BlockReduce(n, red_s)

    def out_project(b):
        w = wa.at[pl.ds(3 * group, group)]

        def rows(m):
            return mixed[pl.ds(pl.multiple_of((4 * b + m) * BLOCK, BLOCK), BLOCK)]

        red.put(b, red.CROSS, dot_nn(rows(n.far_sib), w[...]))
        red.put(b, red.OVER, dot_nn(rows(n.far), w[...]))
        red.hold(b)
        red.over(b)
        red.put(b, red.NEAR, dot_nn(rows(n.sib), w[...]))
        own[b] = dot_nn(rows(n.own), w[...])

    def second_norm(b):
        red.near(b)
        red.wait(b)

        def finish(i):
            r = rows_at(i, STRIP)
            mid = x_ref[b, 0, r].astype(F32) + own[b, r] + red.extra(b, r) + bias_out
            middle[b, r] = mid
            xhat, _ = norm_parts(mid)
            n2[b, r] = (xhat * gain2 + shift2).astype(BF16)

        loop(BLOCK // STRIP, finish)

    ng.near(0)
    ng.wait(0)
    project(0)
    steps(3)
    attend(0, (0, 3))
    ng.onward(1)
    attend(0, (1, 2))
    so.wait()
    ordo = order_o.get()
    slabs_o = jnp.concatenate([go[s] for s in range(8)], axis=0)
    wa[3 * group :] = dot_nn(ordo[...], slabs_o).astype(BF16)
    wa_st.put()
    out_project(0)
    ng.near(1)
    ng.wait(1)
    normed_st.put()
    project(1)
    qkv_st.put()
    steps()
    attend(1, (0, 3))
    steps.rest()
    gg.onward(0)
    attend(1, (1, 2))
    gg.onward(1)
    mixed_st.put()
    lse_t[...] = jnp.transpose(lse[...])[0:8]
    out_project(1)
    steps.rest()
    second_norm(0)
    second_norm(1)
    su.wait()
    sd.wait()
    for b in range(2):
        gg.near(b)
        gg.wait(b)
        keep_g[b].wait()
    for g in (sq, so, su, sd, ng, gg, red):
        g.sent()
    for st in (normed_st, qkv_st, mixed_st, wa_st):
        st.wait()


def hidden_kernel(inner, *refs):
    it = iter(refs)
    take = lambda n: [next(it) for _ in range(n)]
    n2_own, wu, line_w, bias_up, cot, middle, bias_down_in, gain_in = take(8)
    part_st, lined_st, gm_st, att, far_out, part_out, sums, sum_up = take(8)
    n2, hidden, grad_up, own, wd, part_d = take(6)
    n2_sems, red_s, out_s, wd_sems, rd, ls = take(2), take(4), take(4), take(3), take(3), take(1)[0]
    n = Links(inner)
    greet([n.xdev, n.ydev, n.cdev])
    total, width = n2.shape
    units = hidden.shape[1]
    gather = BlockGather(n, lambda b: n2_own.at[b], n2, n2_sems)
    weights = CrossGather(n, line_w, wd, wd_sems)
    for b in range(2):
        gather.start(b)
    wu.start()
    weights.start()
    for ld in (cot, middle):
        ld.start()

    def block(b, m):
        return pl.ds(pl.multiple_of((4 * b + m) * BLOCK, BLOCK), BLOCK)

    for b in range(2):
        cp = pltpu.make_async_copy(n2_own.at[b], n2.at[block(b, n.own)], ls.at[b])
        cp.start()
        cp.wait()
    red, out = BlockReduce(n, red_s), BlockReduce(n, out_s)
    sum_up[...] = jnp.zeros_like(sum_up)
    sums[...] = jnp.zeros_like(sums)
    wu_v = wu.get()

    def up(r):
        h, d = gelu(dot_nt(n2[r], wu_v[...]) + bias_up[...])
        hidden[r] = h.astype(BF16)
        grad_up[r] = d.astype(BF16)

    def down(r):
        g = (dot_nt(cot_v[r], wd[...]) * grad_up[r].astype(F32)).astype(BF16)
        grad_up[r] = g
        sum_up[...] += jnp.sum(g.astype(F32), axis=0, keepdims=True)

    def grad_in_of(r):
        return dot_nn(grad_up[r], wu_v[...])

    def output_of(r):
        return dot_nn(hidden[r], wd[...])

    loop(2, lambda b: up(block(b, n.own)))
    for b in range(2):
        gather.near(b)
    loop(2, lambda b: up(block(b, n.sib)))
    cot_v = cot.get()
    sum_d = CrossReduce(n, part_d, lined_st.buf, rd)

    def grad_down(b):
        tokens = slice(4 * b * BLOCK, 4 * (b + 1) * BLOCK)

        def one(q):
            cols = rows_at(q, WIDE)
            total = dot_tn(hidden[tokens, cols], cot_v[tokens])
            part_d[cols] = (total if b == 0 else total + part_d[cols].astype(F32)).astype(BF16)

        loop(units // WIDE, one)

    for b in range(2):
        gather.onward(b)
        up(block(b, n.far))
        gather.wait(b)
        up(block(b, n.far_sib))
        if b == 0:
            grad_down(0)
    weights.wait()
    for b in range(2):
        down(block(b, n.far_sib))
        red.put(b, red.CROSS, grad_in_of(block(b, n.far_sib)))
        down(block(b, n.far))
        red.put(b, red.OVER, grad_in_of(block(b, n.far)))
        red.hold(b)
        red.over(b)
    grad_down(1)
    sum_d.start()
    for b in range(2):
        down(block(b, n.sib))
        red.put(b, red.NEAR, grad_in_of(block(b, n.sib)))
    bias_down, gain = bias_down_in[...].reshape(1, width), gain_in[...].reshape(1, width)
    middle_v = middle.get()

    def mine(b):
        r = block(b, n.own)
        down(r)
        own[b] = grad_in_of(r)
        part_out[b] = middle_v[b] + output_of(r) + bias_down

    loop(2, mine)
    for b in range(2):
        out.put(b, out.CROSS, output_of(block(b, n.far_sib)))
        out.put(b, out.OVER, output_of(block(b, n.far)))
        out.put(b, out.NEAR, output_of(block(b, n.sib)))
        out.hold(b)
        far_out[b] = out.out[b, out.OVER]
    grad_mid = gm_st.buf
    part_u = part_st.buf

    def grad_units(q):
        cols = rows_at(q, WIDE)
        part_u[cols] = dot_tn(grad_up[:, cols], n2[...]).astype(BF16)

    def norm_back_of(b):
        red.near(b)
        red.wait(b)
        out.near(b)

        def finish(i):
            r = rows_at(i, STRIP)
            at = pl.ds(pl.multiple_of((4 * b + n.own) * BLOCK + i * STRIP, STRIP), STRIP)
            e = own[b, r] + red.extra(b, r)
            xhat, rstd = norm_parts(middle_v[b, r])
            top = cot_v[at].astype(F32)
            g = top + norm_back(e, gain, xhat, rstd)
            grad_mid[b, r] = g
            low = g.astype(BF16)
            att[b, r] = low
            part_out[b, r] += out.got[b, out.NEAR, r].astype(F32)
            sums[0:1] += jnp.sum(e * xhat, axis=0, keepdims=True)
            sums[1:2] += jnp.sum(e, axis=0, keepdims=True)
            sums[2:3] += jnp.sum(low.astype(F32), axis=0, keepdims=True)
            sums[3:4] += jnp.sum(top, axis=0, keepdims=True)

        loop(BLOCK // STRIP, finish)

    loop(units // WIDE, grad_units)
    part_st.put()
    norm_back_of(0)
    norm_back_of(1)
    gm_st.put()
    for d in (1, 2, 3, 0):
        sum_d.finish(d)
    lined_st.put()
    gather.sent()
    weights.sent()
    red.sent()
    out.sent(False)
    sum_d.sent()
    for st in (part_st, lined_st, gm_st):
        st.wait()


def backward_kernel(inner, heads, *refs):
    it = iter(refs)
    take = lambda n: [next(it) for _ in range(n)]
    att_own, gm, wa, qkv, lse_t, mixed, normed, x_ref, gain_in, order_a, order_b, order_ot, lens = take(13)
    part_u, line_d, far_out, part_out, sums_in, sum_up = take(6)
    cells_out, grad_in, grad_qa, grad_qb, grad_o, grad_u, grad_d, small_out = take(8)
    att, gmix, gk, gv, grads, part_qa, part_qb, part_o, part_own, mask, lencol, own, got_out, acc, inbox = take(15)
    line0, line_u, line_qa, line_qb, line_o = take(5)
    att_sems, red_s, ru, rqa, rqb, ro = take(2), take(4), take(3), take(3), take(3), take(3)
    zd, zu, zqa, zqb, zo = take(3), take(3), take(3), take(3), take(3)
    ys, yr, ls, sa, qa = take(5)
    n = Links(inner)
    greet([*n.everyone, n.cross])
    total, width = att.shape
    part = gmix.shape[1]


    def block(b, m):
        return pl.ds(pl.multiple_of((4 * b + m) * BLOCK, BLOCK), BLOCK)

    gather = BlockGather(n, lambda b: att_own.at[b], att, att_sems)
    get_att = [pltpu.make_async_copy(att_own.at[b], att.at[block(b, n.own)], ls.at[b]) for b in range(2)]
    for b in range(2):
        gather.start(b)
        get_att[b].start()

    def out_copy(b):
        return remote(far_out.at[b], got_out.at[b], ys.at[b], yr.at[b], n.ydev)

    for b in range(2):
        out_copy(b).start()
    cu, co = CrossReduce(n, part_u, line_u, ru), CrossReduce(n, part_o, line_o, ro)
    cqa, cqb = CrossReduce(n, part_qa, line_qa, rqa), CrossReduce(n, part_qb, line_qb, rqb)
    lind, linu = LineReduce(n, line_d, grad_d, zd), LineReduce(n, line_u, grad_u, zu)
    lino = LineReduce(n, line_o, grad_o, zo)
    linqa, linqb = LineReduce(n, line_qa, grad_qa, zqa), LineReduce(n, line_qb, grad_qb, zqb)
    cu.start()
    for d in (1, 2, 3):
        lind.start(d)
    for ld in (wa, qkv, mixed, order_ot, gm, order_a):
        ld.start()
    rows_u = line_u.shape[1]
    mine = pl.ds(pl.multiple_of(n.x * 4 * rows_u, 16), 4 * rows_u)
    get_line = pltpu.make_async_copy(line_d.at[0], line0, ls.at[2])
    get_u = pltpu.make_async_copy(part_u.at[mine], part_own, ls.at[3])
    get_u.start()
    get_line.start()

    def pass_on(cross, along, slots):
        for d in slots:
            cross.finish(d, part_own, 0)
            if d:
                along.start(d)


    mask[...] = causal(True)
    key = lax.broadcasted_iota(jnp.int32, (4 * BLOCK, BLOCK // 2), 0)
    lane = lax.broadcasted_iota(jnp.int32, (BLOCK, 2 * PAD_DIM), 1)
    wa_v, qkv_v = wa.get(), qkv.get()
    group = wa_v.shape[0] // 4
    gmix[...] = jnp.zeros_like(gmix)
    grads[...] = jnp.zeros_like(grads)

    def to_heads(b):
        def one(t):
            r = rows_at(4 * b + t, BLOCK)
            gmix[r] = dot_nt(att[r], wa_v[3 * group :]).astype(BF16)

        loop(4, one)

    def attend(b, blocks, first=0, count=heads):
        base = 4 * b * BLOCK

        def head(i):
            h = first + i
            half = h % 2
            here = lane // PAD_DIM == half
            for i in blocks:
                r = slice(base + i * BLOCK, base + (i + 1) * BLOCK)
                keys = slice(base, base + (i + 1) * BLOCK)
                end = (i + 1) * BLOCK
                key_here = lax.broadcasted_iota(jnp.int32, (end, 2 * PAD_DIM), 1) // PAD_DIM == half
                cols = head_cols(part, 0, h)
                q, k, v = (qkv_v[rr, head_cols(part, p, h)] for p, rr in ((0, r), (1, keys), (2, keys)))
                g = gmix[r, cols]
                zero = jnp.zeros_like(q)
                q, g = jnp.where(here, q, zero), jnp.where(here, g, zero)
                column = lencol[:end]
                s = dot_nt(k, q) * SCALE2 + jnp.concatenate([column, column], axis=1)
                diag = s[i * BLOCK :] + mask[...]
                s = jnp.concatenate([s[: i * BLOCK], diag], axis=0) if i else diag
                p = jnp.exp2(s - lse_t[pl.ds(h, 1), r])
                gp = dot_nt(v, g)
                inner_sum = jnp.sum(p * gp, axis=0, keepdims=True)
                ds = (p * (gp - inner_sum)).astype(BF16)
                gv[:end, cols] += dot_nn(p.astype(BF16), g)
                gk[:end, cols] += dot_nn(ds, q)
                gq = (dot_tn(ds, k) * SCALE).astype(BF16)
                grads[r, cols] = jnp.where(here, gq, grads[r, cols])

        loop(count, head)

    def settle(b, first=0, last=part):
        def one(t):
            r, rr = rows_at(t, BLOCK), rows_at(4 * b + t, BLOCK)
            grads[rr, part + first : part + last] = (gk[r, first:last] * SCALE).astype(BF16)
            grads[rr, 2 * part + first : 2 * part + last] = gv[r, first:last].astype(BF16)

        loop(4, one)

    red = BlockReduce(n, red_s)

    def project_back(b):
        w = wa_v.at[pl.ds(0, 3 * group)]

        def rows(m):
            return grads[block(b, m)]

        red.put(b, red.CROSS, dot_nn(rows(n.far_sib), w[...]))
        red.put(b, red.OVER, dot_nn(rows(n.far), w[...]))
        red.hold(b)
        red.over(b)
        red.put(b, red.NEAR, dot_nn(rows(n.sib), w[...]))
        own[b] = dot_nn(rows(n.own), w[...])

    gain = gain_in[...].reshape(1, width)
    gm_v = gm.get()

    def first_norm(b):
        red.near(b)
        red.wait(b)

        def finish(i):
            r = rows_at(i, STRIP)
            e = own[b, r] + red.extra(b, r)
            xhat, rstd = norm_parts(x_ref[b, 0, r].astype(F32))
            grad_in[b, 0, r] = (gm_v[b, r] + norm_back(e, gain, xhat, rstd)).astype(BF16)
            acc[0, 0:1, :width] += jnp.sum(e * xhat, axis=0, keepdims=True)
            acc[0, 1:2, :width] += jnp.sum(e, axis=0, keepdims=True)

        loop(BLOCK // STRIP, finish)

    put_out = [pltpu.make_async_copy(got_out.at[b], cells_out.at[b, 0], ls.at[4 + b]) for b in range(2)]

    def output(b):
        out_copy(b).wait_recv()

        def finish(i):
            r = rows_at(i, 2 * STRIP)
            got_out[b, r] = (part_out[b, r] + got_out[b, r].astype(F32)).astype(BF16)

        loop(BLOCK // (2 * STRIP), finish)
        put_out[b].start()

    acc[0] = jnp.zeros_like(acc[0])
    acc[0, 2:3, :width] = sums_in[2:3]
    acc[0, 3:4, :width] = sums_in[0:1]
    acc[0, 4:5, :width] = sums_in[1:2]
    acc[0, 5:6, :width] = sums_in[3:4]
    acc[0, pl.ds(12 + n.n, 1)] = sum_up[...]

    def lengths_of(b):
        lencol[...] = jnp.where(key < lens[b], 0.0, -1e30)
        gk[...] = jnp.zeros_like(gk)
        gv[...] = jnp.zeros_like(gv)

    for cp in get_att:
        cp.wait()
    lengths_of(0)
    gather.near(0)
    gather.onward(0)
    gather.wait(0)
    to_heads(0)
    attend(0, (0, 3))
    get_u.wait()
    pass_on(cu, linu, (1, 2, 3))
    gather.near(1)
    gather.onward(1)
    gather.wait(1)
    to_heads(1)
    mixed_v, ordo = mixed.get(), order_ot.get()
    stack_o = dot_tn(mixed_v[...], att[...]).astype(BF16)
    part_o[...] = dot_nn(ordo[...], stack_o).astype(BF16)
    co.start()
    gather.sent()
    normed.start()
    attend(0, (1, 2))
    settle(0)
    pass_on(cu, linu, (0,))
    project_back(0)
    lengths_of(1)
    pair = 2 * PAD_DIM
    attend(1, (0, 3), 0, 2)
    for d in (1, 2, 3, 0):
        co.finish(d)
        if d:
            lino.start(d)
    attend(1, (1, 2), 0, 2)
    settle(1, 0, pair)
    normed_v, oa = normed.get(), order_a.get()
    stack_a = part_own
    for p in range(3):
        stack_a[p * pair : (p + 1) * pair] = dot_tn(grads[:, p * part : p * part + pair], normed_v[...]).astype(BF16)

    def reorder(order, stack, dst, x):
        size = dst.shape[0] // 2
        at = pl.ds(pl.multiple_of(x * size, 16), size)
        dst[at] = dot_nn(order[at], stack()).astype(BF16)

    def from_a():
        return stack_a[: 3 * pair]

    reorder(oa, from_a, part_qa, 1 - n.x)
    cqa.start()
    reorder(oa, from_a, part_qa, n.x)
    attend(1, (0, 3), 2, heads - 2)
    output(0)
    output(1)
    for d in (1, 2, 3, 0):
        cqa.finish(d)
        if d:
            linqa.start(d)
    attend(1, (1, 2), 2, heads - 2)
    order_b.start()
    settle(1, pair, part)
    project_back(1)
    rest = part - pair

    for p in range(3):
        m = dot_tn(grads[:, p * part + pair : (p + 1) * part], normed_v[...])
        qkv_v[p * rest : (p + 1) * rest, :width] = m.astype(BF16)

    def from_b():
        return qkv_v[: 3 * rest, :width]

    ob = order_b.get()
    reorder(ob, from_b, part_qb, 1 - n.x)
    cqb.start()
    reorder(ob, from_b, part_qb, n.x)

    def sum_rows(t):
        acc[0, pl.ds(8 + n.n, 1)] += jnp.sum(grads[rows_at(t, BLOCK)].astype(F32), axis=0, keepdims=True)

    loop(total // BLOCK, sum_rows)
    first_norm(0)
    get_line.wait()
    lind.finish(line0[...])
    for g in (linu, lino):
        g.finish()
    cqb.finish(1)
    linqb.start(1)
    first_norm(1)

    def small_copy(i):
        if i < 3:
            return remote(acc.at[0], inbox.at[n.n], sa.at[i], qa.at[i], (n.cdev, n.ydev, n.cross)[i])
        if i == 3:
            return remote(acc.at[1], inbox.at[4], sa.at[3], qa.at[3], n.xdev)
        return remote(acc.at[2], inbox.at[5 + n.z], sa.at[i], qa.at[i], n.along[i - 4])

    def small_came(i):
        if i < 3:
            v = inbox.at[(n.sib, n.far, n.far_sib)[i]]
        else:
            v = inbox.at[4] if i == 3 else inbox.at[5 + n.back(i - 3)]
        dev = [n.cdev, n.ydev, n.cross, n.xdev, *n.along][i]
        return remote(v, v, sa.at[i], qa.at[i], dev)

    inbox[n.n] = acc[0]
    for i in (2, 1, 0):
        small_copy(i).start()
    cqb.finish(2)
    linqb.start(2)
    for i in range(3):
        small_came(i).wait_recv()
    acc[1] = (inbox[0] + inbox[1]) + (inbox[2] + inbox[3])
    small_copy(3).start()
    cqb.finish(3)
    linqb.start(3)
    small_came(3).wait_recv()
    acc[2] = acc[1] + inbox[4]
    inbox[5 + n.z] = acc[2]
    for i in (4, 5, 6):
        small_copy(i).start()
    linqa.finish()
    cqb.finish(0)
    for i in (4, 5, 6):
        small_came(i).wait_recv()
    small_out[...] = (inbox[5] + inbox[6]) + (inbox[7] + inbox[8])
    linqb.finish()
    for b in range(2):
        out_copy(b).wait_send()
        put_out[b].wait()
    for i in range(7):
        small_copy(i).wait_send()
    for g in (red, cu, cqa, cqb, co, lind, linu, linqa, linqb, lino):
        g.sent()


ANY = pl.BlockSpec(memory_space=pl.ANY)
VM = pl.BlockSpec(memory_space=pltpu.VMEM)
SM = pl.BlockSpec(memory_space=pltpu.SMEM)
ASYNC = "async"


def call(kernel, ident, name, outs, ins, scratch, share=None):
    share = share or {}
    lazy_in = [i for i, (_, s) in enumerate(ins) if s is ASYNC]
    lazy_out = [i for i, (_, _, s) in enumerate(outs) if s is ASYNC]
    extra = [pltpu.VMEM(ins[i][0].shape, ins[i][0].dtype) for i in lazy_in if i not in share]
    extra += [pltpu.VMEM(outs[i][0], outs[i][1]) for i in lazy_out]
    extra += [dma((max(1, len(lazy_in)),)), dma((max(1, len(lazy_out)), PARTS))]

    def body(*refs):
        refs = list(refs)
        bufs = refs[len(refs) - len(extra) :]
        refs = refs[: len(refs) - len(extra)]
        in_sems, out_sems = bufs[-2:]
        bufs = iter(bufs)
        for b, i in enumerate(lazy_in):
            if i not in share:
                buf = next(bufs)
            elif isinstance(share[i], int):
                buf = refs[len(ins) + len(outs) + share[i]]
            else:
                other, first = share[i]
                buf = refs[other].buf.at[pl.ds(first, ins[i][0].shape[0]), pl.ds(0, ins[i][0].shape[1])]
            refs[i] = Load(refs[i], buf, in_sems.at[b])
        for b, i in enumerate(lazy_out):
            at = len(ins) + i
            refs[at] = Store(refs[at], next(bufs), out_sems.at[b])
        kernel(*refs)

    return pl.pallas_call(
        body,
        out_shape=[jax.ShapeDtypeStruct(s, d) for s, d, _ in outs],
        in_specs=[ANY if s is ASYNC else s for _, s in ins],
        out_specs=[ANY if s is ASYNC else s for _, _, s in outs],
        scratch_shapes=[*scratch, *extra],
        compiler_params=pltpu.CompilerParams(
            collective_id=ident, has_side_effects=True, vmem_limit_bytes=VMEM_LIMIT
        ),
        name=name,
    )(*[a for a, _ in ins])


def order_matrix(rows, heads, parts, wide):
    m = np.zeros((parts * wide, OUTER * rows), np.float32)
    each = HEAD_DIM // OUTER
    for x in range(2):
        for z in range(4):
            w = 2 * z + x
            for g in range(parts * heads):
                part, head = g % parts, g // parts
                for e in range(each):
                    m[part * wide + head * PAD_DIM + w * each + e, (x * 4 + z) * rows + g * each + e] = 1
    return m


def on_device(
    cells_in, lengths, w_qkv, w_out, w_up, w_down, ln1_gain, ln1_shift, bias_qv, bias_out,
    ln2_gain, ln2_shift, bias_up, bias_down, cotangent,
):
    wide = lax.axis_size("wide")
    inner = wide // OUTER
    shards = [w_qkv, w_out, w_up, w_down]
    if inner > 1:
        groups = [[o * inner + i for i in range(inner)] for o in range(OUTER)]
        shards = [
            lax.all_gather(s, "wide", axis=1, tiled=True, axis_index_groups=groups) for s in shards
        ]
    width = cells_in.shape[3]
    total = 8 * BLOCK
    heads = width // HEAD_DIM // 4
    part = -(-heads // 2) * 2 * PAD_DIM
    n = lax.axis_index("narrow")
    weights = [s.reshape(-1, width) for s in shards]
    used = [s.size // width for s in shards]
    rows_q, rows_o, rows = (-(-u // 16) * 16 for u in used[:3])
    units = OUTER * rows
    order_q, order_o = order_matrix(rows_q, heads, 3, part), order_matrix(rows_o, heads, 1, part)
    each = HEAD_DIM // OUTER * 3
    used_a, used_b = 2 * each, (heads - 2) * each
    rows_a, rows_b = (-(-u // 16) * 16 for u in (used_a, used_b))
    order_a = order_matrix(rows_a, 2, 3, 2 * PAD_DIM)
    order_b = order_matrix(rows_b, heads - 2, 3, part - 2 * PAD_DIM)

    def constant(a):
        return jnp.asarray(np.ascontiguousarray(a), BF16)

    b_qv = lax.dynamic_index_in_dim(bias_qv.reshape(2, 4, heads, HEAD_DIM), n, axis=1, keepdims=False)
    b_qv = jnp.pad(b_qv, ((0, 0), (0, 0), (0, PAD_DIM - HEAD_DIM))).reshape(2, heads * PAD_DIM)
    b_qv = jnp.pad(b_qv, ((0, 0), (0, part - heads * PAD_DIM)))
    bias_qkv = jnp.stack([b_qv[0], jnp.zeros_like(b_qv[0]), b_qv[1]]).reshape(1, -1)
    b_u = lax.dynamic_slice_in_dim(bias_up, n * used[2] * OUTER, used[2] * OUTER).reshape(used[2], 4, 2).transpose(2, 1, 0)
    b_u = jnp.pad(b_u, ((0, 0), (0, 0), (0, rows - used[2]))).reshape(1, -1)
    lens = lengths[:, 0]

    own2 = (2, BLOCK, width)
    vmem = pltpu.VMEM
    g_u, g_d, cot, normed, qkv, mixed, lse, wa, middle, n2 = call(
        functools.partial(forward_kernel, inner, heads), 0, "forward",
        [((OUTER, rows, width), BF16, ANY), ((4, rows, width), BF16, ANY), ((total, width), BF16, ANY),
         ((total, width), BF16, ASYNC), ((total, 3 * part), BF16, ASYNC), ((total, part), BF16, ASYNC),
         ((8, total), F32, VM), ((4 * part, width), BF16, ASYNC), (own2, F32, VM), (own2, BF16, VM)],
        [*[(w, VM) for w in weights], (cells_in, VM), (cotangent, VM),
         *[(v, VM) for v in (ln1_gain, ln1_shift, bias_out, ln2_gain, ln2_shift)], (bias_qkv, VM),
         (constant(order_q), ASYNC), (constant(order_o), ASYNC), (lens, SM)],
        [vmem((OUTER, rows_q, width), BF16), vmem((OUTER, rows_o, width), BF16), vmem(own2, F32),
         vmem((BLOCK, BLOCK), F32), vmem((2, 8, 4 * BLOCK), F32), vmem((total, 2 * PAD_DIM), F32),
         *[vmem((r, width), BF16) for r in (rows_q, rows_o, rows, rows)],
         *SlabGather.SEMS * 3, *LineGather.SEMS, *BlockGather.SEMS * 2, *BlockReduce.scratch(width), dma((2,))],
    )
    part_u, line_d, grad_mid, att, far_out, part_out, sums, sum_up = call(
        functools.partial(hidden_kernel, inner), 1, "hidden_units",
        [((units, width), BF16, ASYNC), ((4, rows, width), BF16, ASYNC), (own2, F32, ASYNC), (own2, BF16, VM),
         (own2, BF16, VM), (own2, F32, VM), ((8, width), F32, VM), ((1, units), F32, VM)],
        [(n2, VM), (g_u.reshape(units, width), ASYNC), (g_d, ANY), (b_u, VM), (cot, ASYNC),
         (middle, ASYNC), (bias_down, VM), (ln2_gain, VM)],
        [vmem((total, width), BF16), vmem((total, units), BF16), vmem((total, units), BF16), vmem(own2, F32),
         vmem((units, width), BF16), vmem((units, width), BF16),
         *BlockGather.SEMS, *BlockReduce.scratch(width), *BlockReduce.scratch(width), *CrossGather.SEMS,
         *CrossReduce.scratch(rows, width), dma((2,))],
    )
    small_shape = (16, units)
    cells_out, grad_in, grad_qa, grad_qb, grad_o, grad_u, grad_d, small = call(
        functools.partial(backward_kernel, inner, heads), 2, "backward",
        [(cells_in.shape, BF16, ANY), (cells_in.shape, BF16, VM), ((used_a, width), F32, VM), ((used_b, width), F32, VM),
         ((used[1], width), F32, VM), ((used[2], width), F32, VM), ((used[3], width), F32, VM), (small_shape, F32, VM)],
        [(att, ANY), (grad_mid, ASYNC), (wa, ASYNC), (qkv, ASYNC), (lse, VM), (mixed, ASYNC), (normed, ASYNC),
         (cells_in, VM), (ln1_gain, VM), (constant(order_a.T), ASYNC), (constant(order_b.T), ASYNC),
         (constant(order_o.T), ASYNC), (lens, SM),
         (part_u, ANY), (line_d, ANY), (far_out, ANY), (part_out, VM), (sums, VM), (sum_up, VM)],
        [vmem((total, width), BF16), vmem((total, part), BF16), vmem((total // 2, part), F32), vmem((total // 2, part), F32),
         vmem((total, 3 * part), BF16), vmem((OUTER * rows_a, width), BF16), vmem((OUTER * rows_b, width), BF16),
         vmem((OUTER * rows_o, width), BF16), vmem((4 * rows, width), BF16), vmem((BLOCK, BLOCK), F32),
         vmem((4 * BLOCK, BLOCK // 2), F32), vmem(own2, F32),
         vmem(own2, BF16), vmem((3, *small_shape), F32), vmem((9, *small_shape), F32),
         vmem((rows, width), BF16), *[vmem((4, r, width), BF16) for r in (rows, rows_a, rows_b, rows_o)],
         *BlockGather.SEMS, *BlockReduce.scratch(width), *CrossReduce.scratch(rows, width),
         *CrossReduce.scratch(rows_a, width), *CrossReduce.scratch(rows_b, width), *CrossReduce.scratch(rows_o, width),
         *LineReduce.scratch(rows, width), *LineReduce.scratch(rows, width), *LineReduce.scratch(rows_a, width),
         *LineReduce.scratch(rows_b, width), *LineReduce.scratch(rows_o, width),
         dma((2,)), dma((2,)), dma((6,)), dma((7,)), dma((7,))],
        share={6: 0, 10: (3, 3 * part)},
    )
    grad_q = jnp.concatenate([grad_qa, grad_qb], axis=0)
    grads = [g.reshape(s.shape) for g, s in zip((grad_q, grad_o, grad_u, grad_d), shards)]
    if inner > 1:
        grads = [
            lax.psum_scatter(g, "wide", scatter_dimension=1, axis_index_groups=groups, tiled=True)
            for g in grads
        ]
    sum_qkv = small[8:12].reshape(4, 3, part)[:, :, : heads * PAD_DIM].reshape(4, 3, heads, PAD_DIM)[..., :HEAD_DIM]
    grad_b = jnp.concatenate([sum_qkv[:, 0].reshape(-1), sum_qkv[:, 2].reshape(-1)])
    grad_bu = small[12:16].reshape(4, 2, 4, rows)[..., : used[2]].transpose(0, 3, 2, 1).reshape(-1)
    flat = [small[i, :width] for i in range(6)]
    return (
        cells_out, grad_in, *grads, flat[0], flat[1], grad_b, flat[2], flat[3], flat[4], grad_bu, flat[5],
    )


def solution(mesh):
    cell = P(None, "wide", "narrow", None)
    shard = P("narrow", "wide")
    return jax.shard_map(
        on_device,
        mesh=mesh,
        in_specs=(cell, P(None, "wide"), *[shard] * 4, *[P()] * 8, cell),
        out_specs=(cell, cell, *[shard] * 4, *[P()] * 8),
        check_vma=False,
    )
```

```python
import functools

import jax
import jax.numpy as jnp
import numpy as np
from jax import lax
from jax.experimental import pallas as pl
from jax.experimental.pallas import tpu as pltpu
from jax.sharding import PartitionSpec as P

HEAD_DIM = 56
PAD_DIM = 64
OUTER = 8
NORM_EPS = 1e-05
SCALE = HEAD_DIM ** (-0.5)
SCALE2 = SCALE * 1.4426950408889634
MESH = pl.DeviceIdType.MESH
BF16 = jnp.bfloat16
F32 = jnp.float32
BLOCK = 256
STRIP = 32
VMEM_LIMIT = 63 * 2**20 + 2**19


class Links:
    def __init__(self, inner):
        w = lax.axis_index("wide")
        n = lax.axis_index("narrow")
        outer, wi = w // inner, w % inner
        z, x, y, c = outer // 2, outer % 2, n // 2, n % 2
        self.z, self.x, self.y, self.c, self.n = z, x, y, c, n

        def device(z, x, y, c):
            return ((2 * z + x) * inner + wi, 2 * y + c)

        self.along = [device((z + d) % 4, x, y, c) for d in (1, 2, 3)]
        self.xdev = device(z, 1 - x, y, c)
        self.ydev = device(z, x, 1 - y, c)
        self.cdev = device(z, x, y, 1 - c)
        self.middle = (z == 1) | (z == 2)
        self.end = device(jnp.where(z >= 2, 3, 0), x, y, c)
        self.end_slot = jnp.where(z >= 2, 2, 0)
        self.cross = device(z, x, 1 - y, 1 - c)
        self.everyone = [*self.along, self.xdev, self.ydev, self.cdev]
        self.own, self.sib = n, 2 * y + 1 - c
        self.far, self.far_sib = 2 * (1 - y) + c, 2 * (1 - y) + 1 - c

    def back(self, d):
        return (self.z + 4 - d) % 4

    def ahead(self, d):
        return (self.z + d) % 4


def remote(src, dst, send, recv, dev):
    return pltpu.make_async_remote_copy(
        src_ref=src, dst_ref=dst, send_sem=send, recv_sem=recv, device_id=dev, device_id_type=MESH
    )


def greet(devices):
    barrier = pltpu.get_barrier_semaphore()
    for dev in devices:
        pl.semaphore_signal(barrier, inc=1, device_id=dev, device_id_type=MESH)
    pl.semaphore_wait(barrier, len(devices))


dma = pltpu.SemaphoreType.DMA


class Line:
    ORDER = (2, 1, 3)

    def zcopy(self, d):
        n = self.n
        return remote(self.own, self.place(n.z), self.zs.at[d - 1], self.zr.at[d - 1], n.along[d - 1])

    def direct(self, d, step):
        if d == 2:
            step()
        else:
            pl.when(self.n.z != (3 if d == 1 else 0))(step)

    def zstart(self):
        for d in self.ORDER:
            self.direct(d, self.zcopy(d).start)

    def zcame(self, d):
        v = self.place(self.n.back(d))
        return remote(v, v, self.zs.at[d - 1], self.zr.at[d - 1], self.n.along[d - 1])

    def zrelay(self):
        n = self.n
        v = self.place(n.back(2))
        return remote(v, v, self.zs.at[3], self.zr.at[n.end_slot], n.end)

    def zwait(self, d):
        self.zcame(d).wait_recv()
        if d == 2:
            pl.when(self.n.middle)(lambda: self.zrelay().start())

    def zsent(self):
        for d in self.ORDER:
            self.direct(d, self.zcopy(d).wait_send)
        pl.when(self.n.middle)(lambda: self.zrelay().wait_send())


class SlabGather(Line):
    SEMS = [dma((4,)), dma((3,)), dma((4,)), dma((4,)), dma((1,))]

    def __init__(self, n, own, out, sems):
        self.n, self.own, self.out = n, own, out
        self.zs, self.zr, self.xs, self.xr, self.ls = sems
        self.keep = pltpu.make_async_copy(own, out.at[n.x * 4 + n.z], self.ls.at[0])

    def place(self, z):
        return self.out.at[self.n.x * 4 + z]

    def xcopy(self, d):
        n = self.n
        v = self.out.at[n.x * 4 + n.back(d)]
        return remote(self.own if d == 0 else v, v, self.xs.at[d], self.xr.at[d], n.xdev)

    def xcame(self, d):
        n = self.n
        v = self.out.at[(1 - n.x) * 4 + n.back(d)]
        return remote(v, v, self.xs.at[d], self.xr.at[d], n.xdev)

    def start(self):
        self.zstart()
        self.keep.start()

    def begin(self):
        self.xcopy(0).start()

    def cross(self, d):
        self.zwait(d)
        self.xcopy(d).start()

    def wait(self):
        self.keep.wait()
        for d in range(4):
            self.xcame(d).wait_recv()

    def sent(self):
        self.zsent()
        for d in range(4):
            self.xcopy(d).wait_send()


class LineGather(Line):
    SEMS = [dma((4,)), dma((3,)), dma((1,))]

    def __init__(self, n, own, out, sems):
        self.n, self.own, self.out = n, own, out
        self.zs, self.zr, self.ls = sems
        self.keep = pltpu.make_async_copy(own, out.at[n.z], self.ls.at[0])

    def place(self, z):
        return self.out.at[z]

    def start(self):
        self.zstart()
        self.keep.start()

    def wait(self):
        self.keep.wait()
        for d in (1, 3):
            self.zwait(d)

    def sent(self):
        self.zsent()


class CrossGather:
    SEMS = [dma((4,)), dma((4,)), dma((4,))]

    def __init__(self, n, line, out, sems):
        self.n, self.line, self.out = n, line, out
        self.s, self.q, self.ls = sems
        self.size = line.shape[1]

    def slab(self, x, j):
        return self.out.at[pl.ds(pl.multiple_of((x * 4 + j) * self.size, 16), self.size)]

    def copy(self, j):
        return remote(self.line.at[j], self.slab(self.n.x, j), self.s.at[j], self.q.at[j], self.n.xdev)

    def keep(self, j):
        return pltpu.make_async_copy(self.line.at[j], self.slab(self.n.x, j), self.ls.at[j])

    def start(self):
        for j in range(4):
            self.copy(j).start()
            self.keep(j).start()

    def wait(self):
        for j in range(4):
            self.keep(j).wait()
            v = self.slab(1 - self.n.x, j)
            remote(v, v, self.s.at[j], self.q.at[j], self.n.xdev).wait_recv()

    def sent(self):
        for j in range(4):
            self.copy(j).wait_send()


class CrossReduce:
    @staticmethod
    def scratch(rows, width):
        return [pltpu.VMEM((4, rows, width), BF16), dma((4,)), dma((4,))]

    def __init__(self, n, part, line, scratch):
        self.n, self.part, self.line = n, part, line
        self.rx, self.s, self.q = scratch
        self.rows = line.shape[1]

    def slab(self, x, d):
        rows = self.rows
        return pl.ds(pl.multiple_of((x * 4 + self.n.ahead(d)) * rows, 16), rows)

    def copy(self, d):
        src = self.part.at[self.slab(1 - self.n.x, d)]
        return remote(src, self.rx.at[d], self.s.at[d], self.q.at[d], self.n.xdev)

    def start(self, slots=(1, 2, 3, 0)):
        for d in slots:
            self.copy(d).start()

    def finish(self, d, part=None, x=None):
        part = self.part if part is None else part
        x = self.n.x if x is None else x
        self.copy(d).wait_recv()
        total = part[self.slab(x, d)].astype(F32) + self.rx[d].astype(F32)
        self.line[d] = total.astype(BF16)

    def sent(self):
        for d in range(4):
            self.copy(d).wait_send()


class LineReduce:
    @staticmethod
    def scratch(rows, width):
        return [pltpu.VMEM((3, rows, width), BF16), dma((3,)), dma((3,))]

    def __init__(self, n, line, out, scratch):
        self.n, self.line, self.out = n, line, out
        self.rz, self.s, self.q = scratch

    def copy(self, d):
        return remote(self.line.at[d], self.rz.at[d - 1], self.s.at[d - 1], self.q.at[d - 1], self.n.along[d - 1])

    def start(self, d):
        self.copy(d).start()

    def finish(self, line=None):
        for d in (1, 2, 3):
            self.copy(d).wait_recv()
        total = (self.line[0] if line is None else line).astype(F32)
        for d in range(3):
            total += self.rz[d].astype(F32)
        self.out[...] = total[: self.out.shape[0]]

    def sent(self):
        for d in (1, 2, 3):
            self.copy(d).wait_send()


class BlockGather:
    SEMS = [dma((2, 3)), dma((2, 3))]

    def __init__(self, n, src, dst, sems):
        self.n, self.src, self.dst = n, src, dst
        self.s, self.q = sems

    def rows(self, b, m):
        return self.dst.at[pl.ds(pl.multiple_of((4 * b + m) * BLOCK, BLOCK), BLOCK)]

    def copy(self, b, i):
        n = self.n
        if i == 2:
            v = self.rows(b, n.far)
            return remote(v, v, self.s.at[b, 2], self.q.at[b, 2], n.cdev)
        return remote(self.src(b), self.rows(b, n.own), self.s.at[b, i], self.q.at[b, i], (n.ydev, n.cdev)[i])

    def came(self, b, i):
        n = self.n
        v = self.rows(b, (n.far, n.sib, n.far_sib)[i])
        return remote(v, v, self.s.at[b, i], self.q.at[b, i], (n.ydev, n.cdev, n.cdev)[i])

    def start(self, b):
        self.copy(b, 0).start()
        self.copy(b, 1).start()

    def near(self, b):
        self.came(b, 1).wait_recv()

    def onward(self, b):
        self.came(b, 0).wait_recv()
        self.copy(b, 2).start()

    def wait(self, b):
        self.came(b, 2).wait_recv()

    def sent(self):
        for b in range(2):
            for i in range(3):
                self.copy(b, i).wait_send()


class BlockReduce:
    @staticmethod
    def scratch(width):
        return [pltpu.VMEM((2, 3, BLOCK, width), BF16), pltpu.VMEM((2, 3, BLOCK, width), BF16), dma((2, 3)), dma((2, 3))]

    NEAR, CROSS, OVER = 0, 1, 2

    def __init__(self, n, scratch):
        self.n = n
        self.out, self.got, self.s, self.q = scratch

    def copy(self, b, i):
        n = self.n
        dev = n.ydev if i == self.OVER else n.cdev
        return remote(self.out.at[b, i], self.got.at[b, i], self.s.at[b, i], self.q.at[b, i], dev)

    def put(self, b, i, value):
        self.out[b, i] = value.astype(BF16)
        if i != self.OVER:
            self.copy(b, i).start()

    def hold(self, b):
        self.copy(b, self.CROSS).wait_recv()

        def add(i):
            r = rows_at(i, 2 * STRIP)
            total = self.out[b, self.OVER, r].astype(F32) + self.got[b, self.CROSS, r].astype(F32)
            self.out[b, self.OVER, r] = total.astype(BF16)

        loop(BLOCK // (2 * STRIP), add)

    def over(self, b):
        self.copy(b, self.OVER).start()

    def near(self, b):
        self.copy(b, self.NEAR).wait_recv()

    def wait(self, b):
        self.copy(b, self.OVER).wait_recv()

    def extra(self, b, r):
        return self.got[b, self.NEAR, r].astype(F32) + self.got[b, self.OVER, r].astype(F32)

    def sent(self, over=True):
        for b in range(2):
            for i in range(3 if over else 2):
                self.copy(b, i).wait_send()


class Load:
    def __init__(self, src, buf, sem):
        self.src, self.buf = src, buf
        self.copy = pltpu.make_async_copy(src, buf, sem)
        self.waiting = False

    def start(self):
        self.copy.start()
        self.waiting = True

    def get(self):
        if self.waiting:
            self.copy.wait()
            self.waiting = False
        return self.buf


class Store:
    def __init__(self, dst, buf, sems):
        self.dst, self.buf, self.sems, self.copies = dst, buf, sems, []

    def put(self, start=None, size=None):
        src, dst = self.buf, self.dst
        if size is not None:
            src, dst = src.at[pl.ds(start, size)], dst.at[pl.ds(start, size)]
        copy = pltpu.make_async_copy(src, dst, self.sems.at[len(self.copies)])
        copy.start()
        self.copies.append(copy)

    def wait(self):
        for copy in self.copies:
            copy.wait()


class Steps:
    def __init__(self, steps):
        self.steps = list(steps)

    def __call__(self, count=1):
        for _ in range(count):
            if self.steps:
                self.steps.pop(0)()

    def rest(self):
        self(len(self.steps))


def dot(a, b, dims):
    return lax.dot_general(a, b, (dims, ((), ())), preferred_element_type=F32)


def dot_nn(a, b):
    return dot(a, b, ((1,), (0,)))


def dot_nt(a, b):
    return dot(a, b, ((1,), (1,)))


def dot_tn(a, b):
    return dot(a, b, ((0,), (0,)))


def rows_at(i, size):
    return pl.ds(pl.multiple_of(i * size, size), size)


def loop(count, body):
    def step(i, carry):
        body(i)
        return carry

    lax.fori_loop(0, count, step, 0)


def norm_parts(v):
    center = v - jnp.mean(v, axis=-1, keepdims=True)
    rstd = lax.rsqrt(jnp.mean(center * center, axis=-1, keepdims=True) + NORM_EPS)
    return center * rstd, rstd


def norm_back(e, gain, xhat, rstd):
    eg = e * gain
    return rstd * (
        eg - jnp.mean(eg, axis=-1, keepdims=True) - xhat * jnp.mean(eg * xhat, axis=-1, keepdims=True)
    )


def gelu(u):
    t = jnp.tanh(0.7978845608 * (u + 0.044715 * u * u * u))
    h = 0.5 * u * (1.0 + t)
    d = 0.5 * (1.0 + t) + 0.5 * u * (1.0 - t * t) * 0.7978845608 * (1.0 + 3 * 0.044715 * u * u)
    return h, d


PARTS = 4
WIDE = 384


def head_cols(part, p, h):
    return pl.ds(pl.multiple_of(p * part + h // 2 * 2 * PAD_DIM, 2 * PAD_DIM), 2 * PAD_DIM)


def causal(swap):
    a = lax.broadcasted_iota(jnp.int32, (BLOCK, BLOCK), 0)
    b = lax.broadcasted_iota(jnp.int32, (BLOCK, BLOCK), 1)
    return jnp.where((a <= b) if swap else (b <= a), 0.0, -1e30)


def forward_kernel(inner, heads, *refs):
    it = iter(refs)
    take = lambda n: [next(it) for _ in range(n)]
    shards, (x_ref, g_ref) = take(5), take(2)
    gain_in, shift_in, bias_out_in, gain2_in, shift2_in = take(5)
    bias_qkv, order_a, order_b, order_o, lens = take(5)
    out_u, out_d, cot, normed_st, qkv_st, mixed_st, lse_t, wa_st, middle, n2 = take(10)
    gqa, gqb, go, own, mask, lenrow, lse = take(7)
    wqa, wqb, wo, wu, wd = take(5)
    qa_sems, qb_sems, o_sems, u_sems, d_sems = take(5), take(5), take(5), take(5), take(3)
    n1_sems, g_sems, red_s, ls = take(2), take(2), take(4), take(1)[0]
    n = Links(inner)
    normed, qkv, mixed, wa = (st.buf for st in (normed_st, qkv_st, mixed_st, wa_st))
    width = normed.shape[1]
    part = mixed.shape[1]
    greet(n.everyone)
    sqa, sqb = SlabGather(n, wqa, gqa, qa_sems), SlabGather(n, wqb, gqb, qb_sems)
    so = SlabGather(n, wo, go, o_sems)
    su, sd = SlabGather(n, wu, out_u, u_sems), LineGather(n, wd, out_d, d_sems)
    for own_slab, shard in zip((wqa, wqb, wo, wu, wd), shards):
        rows, used = own_slab.shape[0], shard.shape[0]
        if rows > used:
            own_slab[rows - 16 :] = jnp.zeros((16, width), BF16)
        own_slab[:used] = shard[...]
        if own_slab is wqa:
            sqa.start()
            sqa.begin()
        if own_slab is wqb:
            sqb.start()
    for ld in (order_a, order_b, order_o):
        ld.start()
    gain, shift, bias_out, gain2, shift2 = (
        ref[...].reshape(1, width) for ref in (gain_in, shift_in, bias_out_in, gain2_in, shift2_in)
    )

    def own_rows(b):
        return pl.ds(pl.multiple_of((4 * b + n.own) * BLOCK, BLOCK), BLOCK)

    ng = BlockGather(n, lambda b: normed.at[own_rows(b)], normed, n1_sems)
    gg = BlockGather(n, lambda b: g_ref.at[b, 0], cot, g_sems)
    for b in range(2):

        def norm(i, b=b):
            xhat, _ = norm_parts(x_ref[b, 0, rows_at(i, 2 * STRIP)].astype(F32))
            at = pl.multiple_of((4 * b + n.own) * BLOCK + i * 2 * STRIP, 2 * STRIP)
            normed[pl.ds(at, 2 * STRIP)] = (xhat * gain + shift).astype(BF16)

        loop(BLOCK // (2 * STRIP), norm)
        ng.start(b)
    for d in Line.ORDER:
        sqa.cross(d)
    sqb.begin()
    keep_g = [pltpu.make_async_copy(g_ref.at[b, 0], cot.at[own_rows(b)], ls.at[b]) for b in range(2)]
    for b in range(2):
        gg.start(b)
        keep_g[b].start()
    mask[...] = causal(False)
    key = lax.broadcasted_iota(jnp.int32, (8, 4 * BLOCK), 1)
    for b in range(2):
        lenrow[b] = jnp.where(key < lens[b], 0.0, -1e30)
    lse[...] = jnp.zeros_like(lse)
    mixed[...] = jnp.zeros_like(mixed)
    group = wa.shape[0] // 4
    pair = 2 * PAD_DIM

    def arrange(order, gathered, first, size):
        slabs = jnp.concatenate([gathered[s] for s in range(8)], axis=0)
        for p in range(3):
            at = p * group + first
            wa[at : at + size] = dot_nn(order[p * size : (p + 1) * size], slabs).astype(BF16)

    steps = Steps(
        [functools.partial(so.cross, d) for d in Line.ORDER]
        + [functools.partial(su.cross, 2), sd.start, functools.partial(su.cross, 1)]
        + [functools.partial(su.cross, 3), functools.partial(sd.zwait, 2)]
    )
    lane = lax.broadcasted_iota(jnp.int32, (BLOCK, 2 * PAD_DIM), 1)

    def project(b, first=0, last=part):
        def one(t):
            r = rows_at(4 * b + t, BLOCK)
            a = normed[r]
            for p in range(3):
                cols = slice(p * part + first, p * part + last)
                qkv[r, cols] = (dot_nt(a, wa[cols]) + bias_qkv[:, cols]).astype(BF16)

        loop(4, one)

    def attend(b, blocks, first=0, count=heads):
        base = 4 * b * BLOCK

        def head(i):
            h = first + i
            half = h % 2
            here = lane // PAD_DIM == half
            for i in blocks:
                r = slice(base + i * BLOCK, base + (i + 1) * BLOCK)
                keys = slice(base, base + (i + 1) * BLOCK)
                end = (i + 1) * BLOCK
                q = qkv[r, head_cols(part, 0, h)]
                k, v = qkv[keys, head_cols(part, 1, h)], qkv[keys, head_cols(part, 2, h)]
                s = dot_nt(jnp.where(here, q, jnp.zeros_like(q)), k) * SCALE2 + lenrow[b, 0:1, :end]
                diag = s[:, i * BLOCK :] + mask[...]
                s = jnp.concatenate([s[:, : i * BLOCK], diag], axis=1) if i else diag
                m = jnp.max(s, axis=-1, keepdims=True)
                e = jnp.exp2(s - m)
                t = jnp.sum(e, axis=-1, keepdims=True)
                p = (e * (1.0 / t)).astype(BF16)
                o = dot_nn(p, v).astype(BF16)
                cols = head_cols(part, 0, h)
                mixed[r, cols] = jnp.where(here, o, mixed[r, cols])
                lse[r] = jnp.where(lane == h, m + jnp.log2(t), lse[r])

        loop(count, head)

    red = BlockReduce(n, red_s)

    def out_project(b):
        w = wa.at[pl.ds(3 * group, group)]

        def rows(m):
            return mixed[pl.ds(pl.multiple_of((4 * b + m) * BLOCK, BLOCK), BLOCK)]

        red.put(b, red.CROSS, dot_nn(rows(n.far_sib), w[...]))
        red.put(b, red.OVER, dot_nn(rows(n.far), w[...]))
        red.hold(b)
        red.over(b)
        red.put(b, red.NEAR, dot_nn(rows(n.sib), w[...]))
        own[b] = dot_nn(rows(n.own), w[...])

    def second_norm(b):
        red.near(b)
        red.wait(b)

        def finish(i):
            r = rows_at(i, STRIP)
            mid = x_ref[b, 0, r].astype(F32) + own[b, r] + red.extra(b, r) + bias_out
            middle[b, r] = mid
            xhat, _ = norm_parts(mid)
            n2[b, r] = (xhat * gain2 + shift2).astype(BF16)

        loop(BLOCK // STRIP, finish)

    oa = order_a.get()
    sqa.wait()
    arrange(oa, gqa, 0, pair)
    ng.onward(0)
    sqb.cross(2)
    so.start()
    su.start()
    for d in Line.ORDER[1:]:
        sqb.cross(d)
    so.begin()
    su.begin()
    ng.near(0)
    ng.wait(0)
    project(0, 0, pair)
    attend(0, (0, 3), 0, 2)
    ng.onward(1)
    attend(0, (1, 2), 0, 2)
    ob = order_b.get()
    sqb.wait()
    arrange(ob, gqb, pair, group - pair)
    project(0, pair, part)
    steps(3)
    attend(0, (0, 3), 2, heads - 2)
    steps(2)
    attend(0, (1, 2), 2, heads - 2)
    so.wait()
    ordo = order_o.get()
    slabs_o = jnp.concatenate([go[s] for s in range(8)], axis=0)
    wa[3 * group :] = dot_nn(ordo[...], slabs_o).astype(BF16)
    wa_st.put()
    out_project(0)
    ng.near(1)
    ng.wait(1)
    normed_st.put()
    project(1)
    qkv_st.put()
    steps()
    attend(1, (0, 3))
    steps.rest()
    gg.onward(0)
    attend(1, (1, 2))
    gg.onward(1)
    mixed_st.put()
    lse_t[...] = jnp.transpose(lse[...])[0:8]
    out_project(1)
    steps.rest()
    second_norm(0)
    second_norm(1)
    su.wait()
    sd.wait()
    for b in range(2):
        gg.near(b)
        gg.wait(b)
        keep_g[b].wait()
    for g in (sqa, sqb, so, su, sd, ng, gg, red):
        g.sent()
    for st in (normed_st, qkv_st, mixed_st, wa_st):
        st.wait()


def hidden_kernel(inner, *refs):
    it = iter(refs)
    take = lambda n: [next(it) for _ in range(n)]
    n2_own, wu, line_w, bias_up, cot, middle, bias_down_in, gain_in = take(8)
    part_st, lined_st, gm_st, att, far_out, part_out, sums, sum_up = take(8)
    n2, hidden, grad_up, own, wd, part_d = take(6)
    n2_sems, red_s, out_s, wd_sems, rd, ls = take(2), take(4), take(4), take(3), take(3), take(1)[0]
    n = Links(inner)
    greet([n.xdev, n.ydev, n.cdev])
    total, width = n2.shape
    units = hidden.shape[1]
    gather = BlockGather(n, lambda b: n2_own.at[b], n2, n2_sems)
    weights = CrossGather(n, line_w, wd, wd_sems)
    for b in range(2):
        gather.start(b)
    wu.start()
    weights.start()
    for ld in (cot, middle):
        ld.start()

    def block(b, m):
        return pl.ds(pl.multiple_of((4 * b + m) * BLOCK, BLOCK), BLOCK)

    for b in range(2):
        cp = pltpu.make_async_copy(n2_own.at[b], n2.at[block(b, n.own)], ls.at[b])
        cp.start()
        cp.wait()
    red, out = BlockReduce(n, red_s), BlockReduce(n, out_s)
    sum_up[...] = jnp.zeros_like(sum_up)
    sums[...] = jnp.zeros_like(sums)
    wu_v = wu.get()

    def up(r):
        h, d = gelu(dot_nt(n2[r], wu_v[...]) + bias_up[...])
        hidden[r] = h.astype(BF16)
        grad_up[r] = d.astype(BF16)

    def down(r):
        g = (dot_nt(cot_v[r], wd[...]) * grad_up[r].astype(F32)).astype(BF16)
        grad_up[r] = g
        sum_up[...] += jnp.sum(g.astype(F32), axis=0, keepdims=True)

    def grad_in_of(r):
        return dot_nn(grad_up[r], wu_v[...])

    def output_of(r):
        return dot_nn(hidden[r], wd[...])

    loop(2, lambda b: up(block(b, n.own)))
    for b in range(2):
        gather.near(b)
    loop(2, lambda b: up(block(b, n.sib)))
    cot_v = cot.get()
    sum_d = CrossReduce(n, part_d, lined_st.buf, rd)

    def grad_down(b):
        tokens = slice(4 * b * BLOCK, 4 * (b + 1) * BLOCK)

        def one(q):
            cols = rows_at(q, WIDE)
            total = dot_tn(hidden[tokens, cols], cot_v[tokens])
            part_d[cols] = (total if b == 0 else total + part_d[cols].astype(F32)).astype(BF16)

        loop(units // WIDE, one)

    for b in range(2):
        gather.onward(b)
        up(block(b, n.far))
        gather.wait(b)
        up(block(b, n.far_sib))
        if b == 0:
            grad_down(0)
    weights.wait()
    for b in range(2):
        down(block(b, n.far_sib))
        red.put(b, red.CROSS, grad_in_of(block(b, n.far_sib)))
        down(block(b, n.far))
        red.put(b, red.OVER, grad_in_of(block(b, n.far)))
        red.hold(b)
        red.over(b)
    grad_down(1)
    sum_d.start()
    for b in range(2):
        down(block(b, n.sib))
        red.put(b, red.NEAR, grad_in_of(block(b, n.sib)))
    bias_down, gain = bias_down_in[...].reshape(1, width), gain_in[...].reshape(1, width)
    middle_v = middle.get()

    def mine(b):
        r = block(b, n.own)
        down(r)
        own[b] = grad_in_of(r)
        part_out[b] = middle_v[b] + output_of(r) + bias_down

    loop(2, mine)
    for b in range(2):
        out.put(b, out.CROSS, output_of(block(b, n.far_sib)))
        out.put(b, out.OVER, output_of(block(b, n.far)))
        out.put(b, out.NEAR, output_of(block(b, n.sib)))
        out.hold(b)
        far_out[b] = out.out[b, out.OVER]
    grad_mid = gm_st.buf
    part_u = part_st.buf

    def grad_units(q):
        cols = rows_at(q, WIDE)
        part_u[cols] = dot_tn(grad_up[:, cols], n2[...]).astype(BF16)

    def norm_back_of(b):
        red.near(b)
        red.wait(b)
        out.near(b)

        def finish(i):
            r = rows_at(i, STRIP)
            at = pl.ds(pl.multiple_of((4 * b + n.own) * BLOCK + i * STRIP, STRIP), STRIP)
            e = own[b, r] + red.extra(b, r)
            xhat, rstd = norm_parts(middle_v[b, r])
            top = cot_v[at].astype(F32)
            g = top + norm_back(e, gain, xhat, rstd)
            grad_mid[b, r] = g
            low = g.astype(BF16)
            att[b, r] = low
            part_out[b, r] += out.got[b, out.NEAR, r].astype(F32)
            sums[0:1] += jnp.sum(e * xhat, axis=0, keepdims=True)
            sums[1:2] += jnp.sum(e, axis=0, keepdims=True)
            sums[2:3] += jnp.sum(low.astype(F32), axis=0, keepdims=True)
            sums[3:4] += jnp.sum(top, axis=0, keepdims=True)

        loop(BLOCK // STRIP, finish)

    loop(units // WIDE, grad_units)
    part_st.put()
    norm_back_of(0)
    norm_back_of(1)
    gm_st.put()
    for d in (1, 2, 3, 0):
        sum_d.finish(d)
    lined_st.put()
    gather.sent()
    weights.sent()
    red.sent()
    out.sent(False)
    sum_d.sent()
    for st in (part_st, lined_st, gm_st):
        st.wait()


def backward_kernel(inner, heads, *refs):
    it = iter(refs)
    take = lambda n: [next(it) for _ in range(n)]
    att_own, gm, wa, qkv, lse_t, mixed, normed, x_ref, gain_in, order_a, order_b, order_ot, lens = take(13)
    part_u, line_d, far_out, part_out, sums_in, sum_up = take(6)
    cells_out, grad_in, grad_qa, grad_qb, grad_o, grad_u, grad_d, small_out = take(8)
    att, gmix, gk, gv, grads, part_qa, part_qb, part_o, part_own, mask, lencol, own, got_out, acc, inbox = take(15)
    line0, line_u, line_qa, line_qb, line_o = take(5)
    att_sems, red_s, ru, rqa, rqb, ro = take(2), take(4), take(3), take(3), take(3), take(3)
    zd, zu, zqa, zqb, zo = take(3), take(3), take(3), take(3), take(3)
    ys, yr, ls, sa, qa = take(5)
    n = Links(inner)
    greet([*n.everyone, n.cross])
    total, width = att.shape
    part = gmix.shape[1]


    def block(b, m):
        return pl.ds(pl.multiple_of((4 * b + m) * BLOCK, BLOCK), BLOCK)

    gather = BlockGather(n, lambda b: att_own.at[b], att, att_sems)
    get_att = [pltpu.make_async_copy(att_own.at[b], att.at[block(b, n.own)], ls.at[b]) for b in range(2)]
    for b in range(2):
        gather.start(b)
        get_att[b].start()

    def out_copy(b):
        return remote(far_out.at[b], got_out.at[b], ys.at[b], yr.at[b], n.ydev)

    for b in range(2):
        out_copy(b).start()
    cu, co = CrossReduce(n, part_u, line_u, ru), CrossReduce(n, part_o, line_o, ro)
    cqa, cqb = CrossReduce(n, part_qa, line_qa, rqa), CrossReduce(n, part_qb, line_qb, rqb)
    lind, linu = LineReduce(n, line_d, grad_d, zd), LineReduce(n, line_u, grad_u, zu)
    lino = LineReduce(n, line_o, grad_o, zo)
    linqa, linqb = LineReduce(n, line_qa, grad_qa, zqa), LineReduce(n, line_qb, grad_qb, zqb)
    cu.start()
    for d in (1, 2, 3):
        lind.start(d)
    for ld in (wa, qkv, mixed, order_ot, gm, order_a):
        ld.start()
    rows_u = line_u.shape[1]
    mine = pl.ds(pl.multiple_of(n.x * 4 * rows_u, 16), 4 * rows_u)
    get_line = pltpu.make_async_copy(line_d.at[0], line0, ls.at[2])
    get_u = pltpu.make_async_copy(part_u.at[mine], part_own, ls.at[3])
    get_u.start()
    get_line.start()

    def pass_on(cross, along, slots):
        for d in slots:
            cross.finish(d, part_own, 0)
            if d:
                along.start(d)


    mask[...] = causal(True)
    key = lax.broadcasted_iota(jnp.int32, (4 * BLOCK, BLOCK // 2), 0)
    lane = lax.broadcasted_iota(jnp.int32, (BLOCK, 2 * PAD_DIM), 1)
    wa_v, qkv_v = wa.get(), qkv.get()
    group = wa_v.shape[0] // 4
    gmix[...] = jnp.zeros_like(gmix)
    grads[...] = jnp.zeros_like(grads)

    def to_heads(b):
        def one(t):
            r = rows_at(4 * b + t, BLOCK)
            gmix[r] = dot_nt(att[r], wa_v[3 * group :]).astype(BF16)

        loop(4, one)

    def attend(b, blocks, first=0, count=heads):
        base = 4 * b * BLOCK

        def head(i):
            h = first + i
            half = h % 2
            here = lane // PAD_DIM == half
            for i in blocks:
                r = slice(base + i * BLOCK, base + (i + 1) * BLOCK)
                keys = slice(base, base + (i + 1) * BLOCK)
                end = (i + 1) * BLOCK
                key_here = lax.broadcasted_iota(jnp.int32, (end, 2 * PAD_DIM), 1) // PAD_DIM == half
                cols = head_cols(part, 0, h)
                q, k, v = (qkv_v[rr, head_cols(part, p, h)] for p, rr in ((0, r), (1, keys), (2, keys)))
                g = gmix[r, cols]
                zero = jnp.zeros_like(q)
                q, g = jnp.where(here, q, zero), jnp.where(here, g, zero)
                column = lencol[:end]
                s = dot_nt(k, q) * SCALE2 + jnp.concatenate([column, column], axis=1)
                diag = s[i * BLOCK :] + mask[...]
                s = jnp.concatenate([s[: i * BLOCK], diag], axis=0) if i else diag
                p = jnp.exp2(s - lse_t[pl.ds(h, 1), r])
                gp = dot_nt(v, g)
                inner_sum = jnp.sum(p * gp, axis=0, keepdims=True)
                ds = (p * (gp - inner_sum)).astype(BF16)
                gv[:end, cols] += dot_nn(p.astype(BF16), g)
                gk[:end, cols] += dot_nn(ds, q)
                gq = (dot_tn(ds, k) * SCALE).astype(BF16)
                grads[r, cols] = jnp.where(here, gq, grads[r, cols])

        loop(count, head)

    def settle(b, first=0, last=part):
        def one(t):
            r, rr = rows_at(t, BLOCK), rows_at(4 * b + t, BLOCK)
            grads[rr, part + first : part + last] = (gk[r, first:last] * SCALE).astype(BF16)
            grads[rr, 2 * part + first : 2 * part + last] = gv[r, first:last].astype(BF16)

        loop(4, one)

    red = BlockReduce(n, red_s)

    def project_back(b):
        w = wa_v.at[pl.ds(0, 3 * group)]

        def rows(m):
            return grads[block(b, m)]

        red.put(b, red.CROSS, dot_nn(rows(n.far_sib), w[...]))
        red.put(b, red.OVER, dot_nn(rows(n.far), w[...]))
        red.hold(b)
        red.over(b)
        red.put(b, red.NEAR, dot_nn(rows(n.sib), w[...]))
        own[b] = dot_nn(rows(n.own), w[...])

    gain = gain_in[...].reshape(1, width)
    gm_v = gm.get()

    def first_norm(b):
        red.near(b)
        red.wait(b)

        def finish(i):
            r = rows_at(i, STRIP)
            e = own[b, r] + red.extra(b, r)
            xhat, rstd = norm_parts(x_ref[b, 0, r].astype(F32))
            grad_in[b, 0, r] = (gm_v[b, r] + norm_back(e, gain, xhat, rstd)).astype(BF16)
            acc[0, 0:1, :width] += jnp.sum(e * xhat, axis=0, keepdims=True)
            acc[0, 1:2, :width] += jnp.sum(e, axis=0, keepdims=True)

        loop(BLOCK // STRIP, finish)

    put_out = [pltpu.make_async_copy(got_out.at[b], cells_out.at[b, 0], ls.at[4 + b]) for b in range(2)]

    def output(b):
        out_copy(b).wait_recv()

        def finish(i):
            r = rows_at(i, 2 * STRIP)
            got_out[b, r] = (part_out[b, r] + got_out[b, r].astype(F32)).astype(BF16)

        loop(BLOCK // (2 * STRIP), finish)
        put_out[b].start()

    acc[0] = jnp.zeros_like(acc[0])
    acc[0, 2:3, :width] = sums_in[2:3]
    acc[0, 3:4, :width] = sums_in[0:1]
    acc[0, 4:5, :width] = sums_in[1:2]
    acc[0, 5:6, :width] = sums_in[3:4]
    acc[0, pl.ds(12 + n.n, 1)] = sum_up[...]

    def lengths_of(b):
        lencol[...] = jnp.where(key < lens[b], 0.0, -1e30)
        gk[...] = jnp.zeros_like(gk)
        gv[...] = jnp.zeros_like(gv)

    for cp in get_att:
        cp.wait()
    lengths_of(0)
    gather.near(0)
    gather.onward(0)
    gather.wait(0)
    to_heads(0)
    attend(0, (0, 3))
    get_u.wait()
    pass_on(cu, linu, (1, 2, 3))
    gather.near(1)
    gather.onward(1)
    gather.wait(1)
    to_heads(1)
    mixed_v, ordo = mixed.get(), order_ot.get()
    stack_o = dot_tn(mixed_v[...], att[...]).astype(BF16)
    part_o[...] = dot_nn(ordo[...], stack_o).astype(BF16)
    co.start()
    gather.sent()
    normed.start()
    attend(0, (1, 2))
    settle(0)
    pass_on(cu, linu, (0,))
    project_back(0)
    lengths_of(1)
    pair = 2 * PAD_DIM
    attend(1, (0, 3), 0, 2)
    for d in (1, 2, 3, 0):
        co.finish(d)
        if d:
            lino.start(d)
    attend(1, (1, 2), 0, 2)
    settle(1, 0, pair)
    normed_v, oa = normed.get(), order_a.get()
    stack_a = part_own
    for p in range(3):
        stack_a[p * pair : (p + 1) * pair] = dot_tn(grads[:, p * part : p * part + pair], normed_v[...]).astype(BF16)

    def reorder(order, stack, dst, x):
        size = dst.shape[0] // 2
        at = pl.ds(pl.multiple_of(x * size, 16), size)
        dst[at] = dot_nn(order[at], stack()).astype(BF16)

    def from_a():
        return stack_a[: 3 * pair]

    reorder(oa, from_a, part_qa, 1 - n.x)
    cqa.start()
    reorder(oa, from_a, part_qa, n.x)
    attend(1, (0, 3), 2, heads - 2)
    output(0)
    output(1)
    for d in (1, 2, 3, 0):
        cqa.finish(d)
        if d:
            linqa.start(d)
    attend(1, (1, 2), 2, heads - 2)
    order_b.start()
    settle(1, pair, part)
    project_back(1)
    rest = part - pair

    for p in range(3):
        m = dot_tn(grads[:, p * part + pair : (p + 1) * part], normed_v[...])
        qkv_v[p * rest : (p + 1) * rest, :width] = m.astype(BF16)

    def from_b():
        return qkv_v[: 3 * rest, :width]

    ob = order_b.get()
    reorder(ob, from_b, part_qb, 1 - n.x)
    cqb.start()
    reorder(ob, from_b, part_qb, n.x)

    def sum_rows(t):
        acc[0, pl.ds(8 + n.n, 1)] += jnp.sum(grads[rows_at(t, BLOCK)].astype(F32), axis=0, keepdims=True)

    loop(total // BLOCK, sum_rows)
    first_norm(0)
    get_line.wait()
    lind.finish(line0[...])
    for g in (linu, lino):
        g.finish()
    cqb.finish(1)
    linqb.start(1)
    first_norm(1)

    def small_copy(i):
        if i < 3:
            return remote(acc.at[0], inbox.at[n.n], sa.at[i], qa.at[i], (n.cdev, n.ydev, n.cross)[i])
        if i == 3:
            return remote(acc.at[1], inbox.at[4], sa.at[3], qa.at[3], n.xdev)
        return remote(acc.at[2], inbox.at[5 + n.z], sa.at[i], qa.at[i], n.along[i - 4])

    def small_came(i):
        if i < 3:
            v = inbox.at[(n.sib, n.far, n.far_sib)[i]]
        else:
            v = inbox.at[4] if i == 3 else inbox.at[5 + n.back(i - 3)]
        dev = [n.cdev, n.ydev, n.cross, n.xdev, *n.along][i]
        return remote(v, v, sa.at[i], qa.at[i], dev)

    inbox[n.n] = acc[0]
    for i in (2, 1, 0):
        small_copy(i).start()
    cqb.finish(2)
    linqb.start(2)
    for i in range(3):
        small_came(i).wait_recv()
    acc[1] = (inbox[0] + inbox[1]) + (inbox[2] + inbox[3])
    small_copy(3).start()
    cqb.finish(3)
    linqb.start(3)
    small_came(3).wait_recv()
    acc[2] = acc[1] + inbox[4]
    inbox[5 + n.z] = acc[2]
    for i in (4, 5, 6):
        small_copy(i).start()
    linqa.finish()
    cqb.finish(0)
    for i in (4, 5, 6):
        small_came(i).wait_recv()
    small_out[...] = (inbox[5] + inbox[6]) + (inbox[7] + inbox[8])
    linqb.finish()
    for b in range(2):
        out_copy(b).wait_send()
        put_out[b].wait()
    for i in range(7):
        small_copy(i).wait_send()
    for g in (red, cu, cqa, cqb, co, lind, linu, linqa, linqb, lino):
        g.sent()


ANY = pl.BlockSpec(memory_space=pl.ANY)
VM = pl.BlockSpec(memory_space=pltpu.VMEM)
SM = pl.BlockSpec(memory_space=pltpu.SMEM)
ASYNC = "async"


def call(kernel, ident, name, outs, ins, scratch, share=None):
    share = share or {}
    lazy_in = [i for i, (_, s) in enumerate(ins) if s is ASYNC]
    lazy_out = [i for i, (_, _, s) in enumerate(outs) if s is ASYNC]
    extra = [pltpu.VMEM(ins[i][0].shape, ins[i][0].dtype) for i in lazy_in if i not in share]
    extra += [pltpu.VMEM(outs[i][0], outs[i][1]) for i in lazy_out]
    extra += [dma((max(1, len(lazy_in)),)), dma((max(1, len(lazy_out)), PARTS))]

    def body(*refs):
        refs = list(refs)
        bufs = refs[len(refs) - len(extra) :]
        refs = refs[: len(refs) - len(extra)]
        in_sems, out_sems = bufs[-2:]
        bufs = iter(bufs)
        for b, i in enumerate(lazy_in):
            if i not in share:
                buf = next(bufs)
            elif isinstance(share[i], int):
                buf = refs[len(ins) + len(outs) + share[i]]
            else:
                other, first = share[i]
                buf = refs[other].buf.at[pl.ds(first, ins[i][0].shape[0]), pl.ds(0, ins[i][0].shape[1])]
            refs[i] = Load(refs[i], buf, in_sems.at[b])
        for b, i in enumerate(lazy_out):
            at = len(ins) + i
            refs[at] = Store(refs[at], next(bufs), out_sems.at[b])
        kernel(*refs)

    return pl.pallas_call(
        body,
        out_shape=[jax.ShapeDtypeStruct(s, d) for s, d, _ in outs],
        in_specs=[ANY if s is ASYNC else s for _, s in ins],
        out_specs=[ANY if s is ASYNC else s for _, _, s in outs],
        scratch_shapes=[*scratch, *extra],
        compiler_params=pltpu.CompilerParams(
            collective_id=ident, has_side_effects=True, vmem_limit_bytes=VMEM_LIMIT
        ),
        name=name,
    )(*[a for a, _ in ins])


def order_matrix(rows, heads, parts, wide):
    m = np.zeros((parts * wide, OUTER * rows), np.float32)
    each = HEAD_DIM // OUTER
    for x in range(2):
        for z in range(4):
            w = 2 * z + x
            for g in range(parts * heads):
                part, head = g % parts, g // parts
                for e in range(each):
                    m[part * wide + head * PAD_DIM + w * each + e, (x * 4 + z) * rows + g * each + e] = 1
    return m


def on_device(
    cells_in, lengths, w_qkv, w_out, w_up, w_down, ln1_gain, ln1_shift, bias_qv, bias_out,
    ln2_gain, ln2_shift, bias_up, bias_down, cotangent,
):
    wide = lax.axis_size("wide")
    inner = wide // OUTER
    shards = [w_qkv, w_out, w_up, w_down]
    if inner > 1:
        groups = [[o * inner + i for i in range(inner)] for o in range(OUTER)]
        shards = [
            lax.all_gather(s, "wide", axis=1, tiled=True, axis_index_groups=groups) for s in shards
        ]
    width = cells_in.shape[3]
    total = 8 * BLOCK
    heads = width // HEAD_DIM // 4
    part = -(-heads // 2) * 2 * PAD_DIM
    n = lax.axis_index("narrow")
    weights = [s.reshape(-1, width) for s in (shards[0][:6], shards[0][6:], *shards[1:])]
    used = [s.size // width for s in shards]
    rows_o, rows = (-(-u // 16) * 16 for u in used[1:3])
    units = OUTER * rows
    order_o = order_matrix(rows_o, heads, 1, part)
    each = HEAD_DIM // OUTER * 3
    used_a, used_b = 2 * each, (heads - 2) * each
    rows_a, rows_b = (-(-u // 16) * 16 for u in (used_a, used_b))
    order_a = order_matrix(rows_a, 2, 3, 2 * PAD_DIM)
    order_b = order_matrix(rows_b, heads - 2, 3, part - 2 * PAD_DIM)

    def constant(a):
        return jnp.asarray(np.ascontiguousarray(a), BF16)

    b_qv = lax.dynamic_index_in_dim(bias_qv.reshape(2, 4, heads, HEAD_DIM), n, axis=1, keepdims=False)
    b_qv = jnp.pad(b_qv, ((0, 0), (0, 0), (0, PAD_DIM - HEAD_DIM))).reshape(2, heads * PAD_DIM)
    b_qv = jnp.pad(b_qv, ((0, 0), (0, part - heads * PAD_DIM)))
    bias_qkv = jnp.stack([b_qv[0], jnp.zeros_like(b_qv[0]), b_qv[1]]).reshape(1, -1)
    b_u = lax.dynamic_slice_in_dim(bias_up, n * used[2] * OUTER, used[2] * OUTER).reshape(used[2], 4, 2).transpose(2, 1, 0)
    b_u = jnp.pad(b_u, ((0, 0), (0, 0), (0, rows - used[2]))).reshape(1, -1)
    lens = lengths[:, 0]

    own2 = (2, BLOCK, width)
    vmem = pltpu.VMEM
    g_u, g_d, cot, normed, qkv, mixed, lse, wa, middle, n2 = call(
        functools.partial(forward_kernel, inner, heads), 0, "forward",
        [((OUTER, rows, width), BF16, ANY), ((4, rows, width), BF16, ANY), ((total, width), BF16, ANY),
         ((total, width), BF16, ASYNC), ((total, 3 * part), BF16, ASYNC), ((total, part), BF16, ASYNC),
         ((8, total), F32, VM), ((4 * part, width), BF16, ASYNC), (own2, F32, VM), (own2, BF16, VM)],
        [*[(w, VM) for w in weights], (cells_in, VM), (cotangent, VM),
         *[(v, VM) for v in (ln1_gain, ln1_shift, bias_out, ln2_gain, ln2_shift)], (bias_qkv, VM),
         (constant(order_a), ASYNC), (constant(order_b), ASYNC), (constant(order_o), ASYNC), (lens, SM)],
        [*[vmem((OUTER, r, width), BF16) for r in (rows_a, rows_b, rows_o)], vmem(own2, F32),
         vmem((BLOCK, BLOCK), F32), vmem((2, 8, 4 * BLOCK), F32), vmem((total, 2 * PAD_DIM), F32),
         *[vmem((r, width), BF16) for r in (rows_a, rows_b, rows_o, rows, rows)],
         *SlabGather.SEMS * 4, *LineGather.SEMS, *BlockGather.SEMS * 2, *BlockReduce.scratch(width), dma((2,))],
    )
    part_u, line_d, grad_mid, att, far_out, part_out, sums, sum_up = call(
        functools.partial(hidden_kernel, inner), 1, "hidden_units",
        [((units, width), BF16, ASYNC), ((4, rows, width), BF16, ASYNC), (own2, F32, ASYNC), (own2, BF16, VM),
         (own2, BF16, VM), (own2, F32, VM), ((8, width), F32, VM), ((1, units), F32, VM)],
        [(n2, VM), (g_u.reshape(units, width), ASYNC), (g_d, ANY), (b_u, VM), (cot, ASYNC),
         (middle, ASYNC), (bias_down, VM), (ln2_gain, VM)],
        [vmem((total, width), BF16), vmem((total, units), BF16), vmem((total, units), BF16), vmem(own2, F32),
         vmem((units, width), BF16), vmem((units, width), BF16),
         *BlockGather.SEMS, *BlockReduce.scratch(width), *BlockReduce.scratch(width), *CrossGather.SEMS,
         *CrossReduce.scratch(rows, width), dma((2,))],
    )
    small_shape = (16, units)
    cells_out, grad_in, grad_qa, grad_qb, grad_o, grad_u, grad_d, small = call(
        functools.partial(backward_kernel, inner, heads), 2, "backward",
        [(cells_in.shape, BF16, ANY), (cells_in.shape, BF16, VM), ((used_a, width), F32, VM), ((used_b, width), F32, VM),
         ((used[1], width), F32, VM), ((used[2], width), F32, VM), ((used[3], width), F32, VM), (small_shape, F32, VM)],
        [(att, ANY), (grad_mid, ASYNC), (wa, ASYNC), (qkv, ASYNC), (lse, VM), (mixed, ASYNC), (normed, ASYNC),
         (cells_in, VM), (ln1_gain, VM), (constant(order_a.T), ASYNC), (constant(order_b.T), ASYNC),
         (constant(order_o.T), ASYNC), (lens, SM),
         (part_u, ANY), (line_d, ANY), (far_out, ANY), (part_out, VM), (sums, VM), (sum_up, VM)],
        [vmem((total, width), BF16), vmem((total, part), BF16), vmem((total // 2, part), F32), vmem((total // 2, part), F32),
         vmem((total, 3 * part), BF16), vmem((OUTER * rows_a, width), BF16), vmem((OUTER * rows_b, width), BF16),
         vmem((OUTER * rows_o, width), BF16), vmem((4 * rows, width), BF16), vmem((BLOCK, BLOCK), F32),
         vmem((4 * BLOCK, BLOCK // 2), F32), vmem(own2, F32),
         vmem(own2, BF16), vmem((3, *small_shape), F32), vmem((9, *small_shape), F32),
         vmem((rows, width), BF16), *[vmem((4, r, width), BF16) for r in (rows, rows_a, rows_b, rows_o)],
         *BlockGather.SEMS, *BlockReduce.scratch(width), *CrossReduce.scratch(rows, width),
         *CrossReduce.scratch(rows_a, width), *CrossReduce.scratch(rows_b, width), *CrossReduce.scratch(rows_o, width),
         *LineReduce.scratch(rows, width), *LineReduce.scratch(rows, width), *LineReduce.scratch(rows_a, width),
         *LineReduce.scratch(rows_b, width), *LineReduce.scratch(rows_o, width),
         dma((2,)), dma((2,)), dma((6,)), dma((7,)), dma((7,))],
        share={6: 0, 10: (3, 3 * part)},
    )
    grad_q = jnp.concatenate([grad_qa, grad_qb], axis=0)
    grads = [g.reshape(s.shape) for g, s in zip((grad_q, grad_o, grad_u, grad_d), shards)]
    if inner > 1:
        grads = [
            lax.psum_scatter(g, "wide", scatter_dimension=1, axis_index_groups=groups, tiled=True)
            for g in grads
        ]
    sum_qkv = small[8:12].reshape(4, 3, part)[:, :, : heads * PAD_DIM].reshape(4, 3, heads, PAD_DIM)[..., :HEAD_DIM]
    grad_b = jnp.concatenate([sum_qkv[:, 0].reshape(-1), sum_qkv[:, 2].reshape(-1)])
    grad_bu = small[12:16].reshape(4, 2, 4, rows)[..., : used[2]].transpose(0, 3, 2, 1).reshape(-1)
    flat = [small[i, :width] for i in range(6)]
    return (
        cells_out, grad_in, *grads, flat[0], flat[1], grad_b, flat[2], flat[3], flat[4], grad_bu, flat[5],
    )


def solution(mesh):
    cell = P(None, "wide", "narrow", None)
    shard = P("narrow", "wide")
    return jax.shard_map(
        on_device,
        mesh=mesh,
        in_specs=(cell, P(None, "wide"), *[shard] * 4, *[P()] * 8, cell),
        out_specs=(cell, cell, *[shard] * 4, *[P()] * 8),
        check_vma=False,
    )
```
